32 devices in a mesh: dp: 4 (over z), row: 4 (over y, x), col: 2 (over core).
Axes of the slice: x: 2, y: 2, z: 4, core: 2. Of those that a mesh axis runs over, the one named last changes fastest.
Arguments:
- inputs: bfloat16 [4096, 2048], P('dp'), may hold values from -6 to 6
- segments: int32 [4, 1024], P('dp'), may hold values from 0 to 5, never falling along the last dimension, each value on 1 to 768 neighbouring positions
- mixer_gain: float32 [2048], replicated, may hold values from 0.5 to 1.5
- w_query: bfloat16 [2048, 2048], P('col', 'row'), may hold values from -0.125 to 0.125
- w_key: bfloat16 [2048, 2048], P('col', 'row'), may hold values from -0.125 to 0.125
- w_value: bfloat16 [2048, 2048], P('col', 'row'), may hold values from -0.125 to 0.125
- w_beta: bfloat16 [2048, 16], P('col', 'row'), may hold values from -0.125 to 0.125
- conv_query: float32 [2048, 4], P(('row', 'col')), may hold values from -3 to 3
- conv_key: float32 [2048, 4], P(('row', 'col')), may hold values from -3 to 3
- conv_value: float32 [2048, 4], P(('row', 'col')), may hold values from -3 to 3
- head_gain: float32 [128], replicated, may hold values from 0.5 to 1.5
- w_out: bfloat16 [2048, 2048], P('row', 'col'), may hold values from -0.125 to 0.125
- feed_gain: float32 [2048], replicated, may hold values from 0.5 to 1.5
- w_gate: bfloat16 [2048, 5632], P('col', 'row'), may hold values from -0.125 to 0.125
- w_up: bfloat16 [2048, 5632], P('col', 'row'), may hold values from -0.125 to 0.125
- w_down: bfloat16 [5632, 2048], P('row', 'col'), may hold values from -0.078125 to 0.078125
- cotangent: bfloat16 [4096, 2048], P('dp'), may hold values from -6 to 6
Outputs:
- output: bfloat16 [4096, 2048], P('dp')
- input_grad: bfloat16 [4096, 2048], P('dp')
- mixer_gain_grad: float32 [2048], P('dp')
- query_grad: float32 [2048, 2048], P(('col', 'dp'), 'row')
- key_grad: float32 [2048, 2048], P(('col', 'dp'), 'row')
- value_grad: float32 [2048, 2048], P(('col', 'dp'), 'row')
- beta_grad: float32 [2048, 16], P(('col', 'dp'), 'row')
- conv_query_grad: float32 [2048, 4], P(('row', 'col', 'dp'))
- conv_key_grad: float32 [2048, 4], P(('row', 'col', 'dp'))
- conv_value_grad: float32 [2048, 4], P(('row', 'col', 'dp'))
- head_gain_grad: float32 [128], replicated
- out_grad: float32 [2048, 2048], P(('row', 'dp'), 'col')
- feed_gain_grad: float32 [2048], P('dp')
- gate_grad: float32 [2048, 5632], P(('col', 'dp'), 'row')
- up_grad: float32 [2048, 5632], P(('col', 'dp'), 'row')
- down_grad: float32 [5632, 2048], P(('row', 'dp'), 'col')
The draws below stay inside these ranges and needn't reach their ends.
Inputs may be any that keep to these rules, and one draw needn't show every extreme that they name: `segments`: along each sequence the numbers never fall and begin at 0; a document has at most 768 tokens, and one of each sequence has exactly that many.
All inputs are finite; a program needn't handle non-finite values.
Results may differ from the reference program's by a relative error of at most 0.017.
Values may be sent and summed in bfloat16 or wider, within the bound.
No kernel may reach another device: no remote copies, remote signals or barrier semaphores. Data moves between devices by JAX's collectives and lax.ppermute only.
A program may use at most 192 MiB of HBM per device.

```python
import math
import jax
import jax.numpy as jnp
import numpy as np
from jax import lax

D = 2048
H = 16
HEAD_DIM = 128
FF = 5632
CONV = 4
SPAN = 64
LEN = 1024
SEQS = 1
HD = 2048
NSEQ = 4
TOKENS = 4096
N_DP = 4


def level_of(stream_key, shape, pieces, smallest, high):
    loudness = 1.0
    for axis_at, parts in pieces:
        heights = jax.random.uniform(jax.random.fold_in(jax.random.fold_in(stream_key, 6), axis_at), (parts,), jnp.float32, smallest / len(pieces), high / len(pieces))
        loudness = loudness * jnp.repeat(jnp.exp(heights), shape[axis_at] // parts).reshape((-1,) + (1,) * (len(shape) - 1 - axis_at))
    return loudness


def profile(amount, total, bound, lean):
    loads = [(1 << 20) // math.isqrt(standing ** lean) + 1 for standing in range(2, amount + 1)]
    rest, given = total - bound - (amount - 1), [1] * (amount - 1)
    while rest > 0:
        free = [i for i in range(amount - 1) if given[i] < bound]
        pool, budget = sum([loads[i] for i in free]), rest
        for i in free:
            extra = min(bound - given[i], max(1, budget * loads[i] // pool), rest)
            given[i] = given[i] + extra
            rest = rest - extra
    return np.array([bound] + given)


def uneven(stream_key, count, total, reach, slope):
    if count == 2:
        one = jax.random.randint(stream_key, (), max(1, total - reach), min(reach, total - 1) + 1)
        return jnp.stack([one, total - one])
    tallies = jnp.asarray(profile(count, total, reach, slope), jnp.int32)
    twos = (count - 1) // 2
    giver, sink = tallies[1:1 + 2 * twos:2], tallies[2:2 + 2 * twos:2]
    room = jnp.minimum(giver - 1, reach - sink)
    moved = jax.random.randint(jax.random.fold_in(stream_key, 1), (twos,), 0, 1 << 20) % (room + 1)
    tallies = tallies.at[1:1 + 2 * twos:2].set(giver - moved).at[2:2 + 2 * twos:2].set(sink + moved)
    return tallies[jax.random.permutation(jax.random.fold_in(stream_key, 2), count)]


def scatter_about(stream_key, extent, scale, most, pieces=(), kind=jnp.bfloat16):
    drawn = scale * jax.random.normal(stream_key, extent, jnp.float32)
    if pieces:
        drawn = drawn * level_of(stream_key, extent, pieces, -0.22, 0.18)
    return jnp.clip(drawn, -most, most).astype(kind)


def setup_inputs(seed: int = 0) -> dict:
    arg_keys = jax.random.split(jax.random.key(seed), 18)
    return {
        "inputs": scatter_about(arg_keys[0], (TOKENS, D), 1.0, 6.0, ((0, 4),)),
        "segments": jax.vmap(lambda own: jnp.searchsorted(jnp.cumsum(uneven(own, 6, LEN, 3 * LEN // 4, 0)), jnp.arange(LEN), side="right"))(jax.random.split(arg_keys[1], NSEQ)).reshape((NSEQ, LEN)).astype(jnp.int32),
        "mixer_gain": jnp.clip(1.0 + 0.1 * jax.random.normal(arg_keys[2], (D,), jnp.float32), 0.5, 1.5),
        "w_query": scatter_about(arg_keys[3], (D, HD), D ** -0.5, 0.125, ((0, 2), (1, 4))),
        "w_key": scatter_about(arg_keys[4], (D, HD), D ** -0.5, 0.125, ((0, 2), (1, 4))),
        "w_value": scatter_about(arg_keys[5], (D, HD), D ** -0.5, 0.125, ((0, 2), (1, 4))),
        "w_beta": scatter_about(arg_keys[6], (D, H), D ** -0.5, 0.125, ((0, 2), (1, 4))),
        "conv_query": scatter_about(arg_keys[7], (HD, CONV), CONV ** -0.5, 3.0, ((0, 8),), jnp.float32),
        "conv_key": scatter_about(arg_keys[8], (HD, CONV), CONV ** -0.5, 3.0, ((0, 8),), jnp.float32),
        "conv_value": scatter_about(arg_keys[9], (HD, CONV), CONV ** -0.5, 3.0, ((0, 8),), jnp.float32),
        "head_gain": jnp.clip(1.0 + 0.1 * jax.random.normal(arg_keys[10], (HEAD_DIM,), jnp.float32), 0.5, 1.5),
        "w_out": scatter_about(arg_keys[11], (HD, D), HD ** -0.5, 0.125, ((0, 4), (1, 2))),
        "feed_gain": jnp.clip(1.0 + 0.1 * jax.random.normal(arg_keys[12], (D,), jnp.float32), 0.5, 1.5),
        "w_gate": scatter_about(arg_keys[13], (D, FF), D ** -0.5, 0.125, ((0, 2), (1, 4))),
        "w_up": scatter_about(arg_keys[14], (D, FF), D ** -0.5, 0.125, ((0, 2), (1, 4))),
        "w_down": scatter_about(arg_keys[15], (FF, D), FF ** -0.5, 0.078125, ((0, 4), (1, 2))),
        "cotangent": scatter_about(arg_keys[16], (TOKENS, D), 1.0, 6.0, ((0, 4),)),
    }


EPSILON = 1e-06
HEAD_FLOOR = 0.02
PRECISE = lax.Precision.HIGHEST

@jax.custom_vjp
def low(v):
    return lax.optimization_barrier(v.astype(jnp.bfloat16)).astype(jnp.float32)

@jax.custom_vjp
def low_back(v):
    return v

def low_keep(v):
    return (low(v), None)

def low_pass(kept, grad):
    return (grad,)

def back_keep(v):
    return (v, None)

def back_low(kept, grad):
    return (low(grad),)
low.defvjp(low_keep, low_pass)
low_back.defvjp(back_keep, back_low)

def rms_rows(values, scales):
    mean_square = lax.optimization_barrier(jnp.mean(values * values, axis=-1, keepdims=True))
    return values * lax.rsqrt(mean_square + EPSILON) * scales

def head_rms(values, scales):
    mean_square = lax.optimization_barrier(jnp.mean(values * values, axis=-1, keepdims=True))
    return values * lax.rsqrt(mean_square + HEAD_FLOOR) * scales

def causal_conv(values, kernel, documents):
    taps_count = kernel.shape[1]
    result = values * kernel[:, taps_count - 1]
    for offset in range(1, taps_count):
        shifted = jnp.concatenate([jnp.zeros((offset, values.shape[1]), jnp.float32), values[:-offset]], 0)
        earlier = jnp.concatenate([jnp.full((offset,), -1, jnp.int32), documents[:-offset]], 0)
        result = result + jnp.where((earlier == documents)[:, None], shifted, 0.0) * kernel[:, taps_count - 1 - offset]
    return result

def span_step(memory, block_item):
    queries, key_vecs, values, strengths, documents, previous = block_item
    query_heads = jnp.transpose(queries, (1, 0, 2))
    key_heads = jnp.transpose(key_vecs, (1, 0, 2))
    value_heads = jnp.transpose(values, (1, 0, 2))
    beta_heads = jnp.transpose(strengths, (1, 0))
    length = documents.shape[0]
    places = jnp.arange(length, dtype=jnp.int32)
    same_doc = (documents[:, None] == documents[None, :]).astype(jnp.float32)
    earlier = (places[:, None] > places[None, :]).astype(jnp.float32)
    inclusive = (places[:, None] >= places[None, :]).astype(jnp.float32)
    carried = (documents == previous).astype(jnp.float32)
    key_gram = jnp.einsum('hik,hjk->hij', key_heads, key_heads, precision=PRECISE)
    system = jnp.eye(length, dtype=jnp.float32)[None] + beta_heads[:, :, None] * key_gram * (same_doc * earlier)[None]
    recalled = jnp.einsum('hck,hvk->hcv', key_heads, memory, precision=PRECISE)
    target = beta_heads[:, :, None] * (value_heads - carried[None, :, None] * recalled)
    writes = lax.linalg.triangular_solve(system, target, left_side=True, lower=True)
    scores = jnp.einsum('hik,hjk->hij', query_heads, key_heads, precision=PRECISE) * (same_doc * inclusive)[None]
    read_old = jnp.einsum('hck,hvk->hcv', query_heads, memory, precision=PRECISE)
    outputs = carried[None, :, None] * read_old + jnp.einsum('hij,hjv->hiv', scores, writes, precision=PRECISE)
    closing = (documents == documents[length - 1]).astype(jnp.float32)
    new_memory = carried[length - 1] * memory + jnp.einsum('hcv,hck->hvk', writes * closing[None, :, None], key_heads, precision=PRECISE)
    return (new_memory, jnp.transpose(outputs, (1, 0, 2)))

def delta_rule(queries, key_vecs, values, strengths, documents):
    tokens, head_count, head_size = queries.shape
    blocks = tokens // SPAN
    preceding = jnp.concatenate([jnp.full((1,), -1, jnp.int32), documents[:-1]], 0)
    start_memory = jnp.zeros((head_count, values.shape[2], head_size), jnp.float32)
    final_memory, outputs = lax.scan(jax.checkpoint(span_step), start_memory, (queries.reshape(blocks, SPAN, head_count, head_size), key_vecs.reshape(blocks, SPAN, head_count, head_size), values.reshape(blocks, SPAN, head_count, -1), strengths.reshape(blocks, SPAN, head_count), documents.reshape(blocks, SPAN), preceding.reshape(blocks, SPAN)[:, 0]))
    return outputs.reshape(tokens, head_count, -1)

def mixer_heads(query_in, key_in, value_in, beta_in, query_kernel, key_kernel, value_kernel, scales, documents):
    tokens = query_in.shape[0]
    head_count = beta_in.shape[1]
    head_size = scales.shape[0]
    queries = jax.nn.silu(causal_conv(query_in, query_kernel, documents)).reshape(tokens, head_count, head_size)
    key_vecs = jax.nn.silu(causal_conv(key_in, key_kernel, documents)).reshape(tokens, head_count, head_size)
    key_vecs = key_vecs * lax.rsqrt(lax.optimization_barrier(jnp.sum(key_vecs * key_vecs, axis=-1, keepdims=True)) + EPSILON)
    values = jax.nn.silu(causal_conv(value_in, value_kernel, documents)).reshape(tokens, head_count, head_size)
    strengths = jax.nn.sigmoid(beta_in)
    mixed = delta_rule(queries, key_vecs, values, strengths, documents)
    return head_rms(mixed, scales).reshape(tokens, head_count * head_size)

def product(left, right):
    return jnp.dot(left, right, precision=PRECISE)

def block_layer(residual, documents, gain_one, query_w, key_w, value_w, beta_w, query_kernel, key_kernel, value_kernel, norm_scales, out_w, gain_two, gate_w, up_w, down_w):
    normed = low(rms_rows(residual, gain_one))
    query_in = low_back(product(normed, query_w))
    key_in = low_back(product(normed, key_w))
    value_in = low_back(product(normed, value_w))
    beta_in = low_back(product(normed, beta_w))
    head_values = low(mixer_heads(query_in, key_in, value_in, beta_in, query_kernel, key_kernel, value_kernel, norm_scales, documents))
    attended = low_back(product(head_values, out_w))
    middle = residual + attended
    normed_two = low(rms_rows(middle, gain_two))
    gate_value = low_back(product(normed_two, gate_w))
    up_value = low_back(product(normed_two, up_w))
    hidden = low(jax.nn.silu(gate_value) * up_value)
    return middle + product(hidden, down_w)

def reference(inputs, segments, mixer_gain, w_query, w_key, w_value, w_beta, conv_query, conv_key, conv_value, head_gain, w_out, feed_gain, w_gate, w_up, w_down, cotangent):
    group_tokens = SEQS * LEN
    params = tuple((weight.astype(jnp.float32) for weight in (mixer_gain, w_query, w_key, w_value, w_beta, conv_query, conv_key, conv_value, head_gain, w_out, feed_gain, w_gate, w_up, w_down)))

    def per_group(totals, block_item):
        block_in, block_seg, block_cot = block_item
        documents = (block_seg + (jnp.arange(SEQS, dtype=jnp.int32) * LEN)[:, None]).reshape(-1).astype(jnp.int32)
        result, pullback = jax.vjp(lambda residual, *weights: block_layer(residual, documents, *weights), block_in.astype(jnp.float32), *params)
        gradients = pullback(block_cot.astype(jnp.float32))
        totals = tuple((total + gradient for total, gradient in zip(totals, gradients[1:])))
        return (totals, (result.astype(jnp.bfloat16), gradients[0].astype(jnp.bfloat16)))
    initial = tuple((jnp.zeros_like(weight) for weight in params))
    totals, (outputs, input_grads) = lax.scan(per_group, initial, (inputs.reshape(N_DP, group_tokens, D), segments.reshape(N_DP, SEQS, LEN), cotangent.reshape(N_DP, group_tokens, D)))
    return (outputs.reshape(-1, D), input_grads.reshape(-1, D), totals[0], totals[1], totals[2], totals[3], totals[4], totals[5], totals[6], totals[7], totals[8], totals[9], totals[10], totals[11], totals[12], totals[13])
```

```python
import functools
import jax
import jax.numpy as jnp
from jax import lax
from jax.experimental import pallas as pl
from jax.experimental.pallas import tpu as pltpu
from jax.sharding import PartitionSpec as P

EPSILON = 1e-06
HEAD_FLOOR = 0.02
CH = 128
HS = 128
F32 = jnp.float32
BF16 = jnp.bfloat16

NN = (((1,), (0,)), ((), ()))
NT = (((1,), (1,)), ((), ()))
TN = (((0,), (0,)), ((), ()))


def dot1(a, b, dims=NN):
    return lax.dot_general(a.astype(BF16), b.astype(BF16), dims, preferred_element_type=F32)


def split(a):
    hi = a.astype(BF16)
    return hi, (a - hi.astype(F32)).astype(BF16)


def dot3s(a, b, dims=NN):
    (ah, al), (bh, bl) = a, b
    d = functools.partial(lax.dot_general, dimension_numbers=dims, preferred_element_type=F32)
    return d(ah, bh) + (d(ah, bl) + d(al, bh))


def dot3(a, b, dims=NN):
    return dot3s(split(a), split(b), dims)


def silu_parts(z):
    s = 1.0 / (1.0 + jnp.exp(-z))
    return s, z * s


def unit_inverse(low, xor, eye, dot):
    inv = eye - jnp.where(xor < 2, low, 0.0)
    size = 2
    while size < CH:
        part = jnp.where((xor >= size) & (xor < 2 * size), low, 0.0)
        inv = inv - dot(dot(inv, part), inv)
        size *= 2
    return inv


def window(ref, c, cols):
    return ref[pl.ds(pl.multiple_of(c * CH, CH), CH + 8), cols]


def conv_chunk(win, taps, masks):
    out = win[8:] * taps[3]
    for j in (1, 2, 3):
        out = out + masks[j - 1] * pltpu.roll(win, j, 0)[8:] * taps[3 - j]
    return out


def chunk_docs(doc_col, doc_row, c):
    col = doc_col[pl.ds(pl.multiple_of(c * CH + 8, 8), CH), :]
    row = doc_row[pl.ds(c, 1), :]
    prev = doc_col[pl.ds(pl.multiple_of(c * CH, 8), 8), :][7:8]
    last = col[CH - 1:CH]
    return col, row, prev, last


def place_rows(place, c):
    return pl.ds(pl.multiple_of(place[c] * CH, CH), CH)


def fill_pad(pad, place, z_ref, chunks, width):
    pad[0:8] = jnp.zeros((8, 3 * width), F32)
    for c in range(chunks):
        pad[c * CH + 8:(c + 1) * CH + 8] = z_ref[place_rows(place, c), :3 * width]


def fwd_kernel(heads, chunks, dotg, doti, dot,
               place, z_ref, taps_ref, doc_col, doc_row, gain_ref,
               out_ref, mixed_ref, t_ref, h_ref, a_ref, qt_ref, w_ref, u_ref,
               pad, pu_s, b_s):
    width = heads * HS
    fill_pad(pad, place, z_ref, chunks, width)
    row_i = lax.broadcasted_iota(jnp.int32, (CH, CH), 0)
    col_i = lax.broadcasted_iota(jnp.int32, (CH, CH), 1)
    xor = row_i ^ col_i
    eye = (xor == 0).astype(F32)

    def one(c, h):
        col, row, prev, last = chunk_docs(doc_col, doc_row, c)
        same = col == row
        strict = same & (row_i > col_i)
        incl = same & (row_i >= col_i)
        carried = (col == prev).astype(F32)
        closing = (col == last).astype(F32)
        keep = (last == prev).astype(F32)
        dwin = doc_col[pl.ds(pl.multiple_of(c * CH, CH), CH + 8), :]
        masks = [(dwin[8 - j:CH + 8 - j] == col).astype(F32) for j in (1, 2, 3)]

        def conv(which):
            cols = slice(which * width + h * HS, which * width + (h + 1) * HS)
            taps = [taps_ref[t:t + 1, cols] for t in range(4)]
            return silu_parts(conv_chunk(window(pad, c, cols), taps, masks))[1]

        q, k, v = conv(0), conv(1), conv(2)
        k = k * lax.rsqrt(jnp.sum(k * k, axis=1, keepdims=True) + EPSILON)
        beta = 1.0 / (1.0 + jnp.exp(-z_ref[place_rows(place, c), 3 * width + h:3 * width + h + 1]))
        gram = dotg(k, k, NT)
        low = jnp.where(strict, beta * gram, 0.0)
        inv = unit_inverse(low, xor, eye, doti)
        w = dot(inv, (carried * beta) * k)
        u = dot(inv, beta * v)
        p = jnp.where(incl, dot(q, k, NT), 0.0)
        qt = carried * q - dot(p, w)
        pu = dot(p, u)
        kcl = closing * k
        a = keep * eye - dot(kcl, w, TN)
        b = dot(kcl, u, TN)
        i = c * heads + h
        t_ref[i] = inv
        qt_ref[i] = qt
        a_ref[i] = a
        w_ref[i] = w
        u_ref[i] = u
        pu_s[i] = pu
        b_s[i] = b

    per = 2

    def phase_one(g, carry):
        for e in range(per):
            for h in range(heads):
                one(g * per + e, h)
        return carry

    lax.fori_loop(0, chunks // per, phase_one, 0)

    def phase_two(c, state):
        new = []
        for h in range(heads):
            i = c * heads + h
            h_ref[i] = state[h]
            new.append(dot(a_ref[i], state[h]) + b_s[i])
        return tuple(new)

    lax.fori_loop(0, chunks, phase_two, tuple(jnp.zeros((HS, HS), F32) for _ in range(heads)))

    def phase_three(c, carry):
        for h in range(heads):
            i = c * heads + h
            rows = pl.ds(pl.multiple_of(c * CH, CH), CH)
            cols = slice(h * HS, (h + 1) * HS)
            mixed = dot(qt_ref[i], h_ref[i]) + pu_s[i]
            mixed_ref[rows, cols] = mixed
            r = lax.rsqrt(jnp.mean(mixed * mixed, axis=1, keepdims=True) + HEAD_FLOOR)
            out_ref[place_rows(place, c), cols] = (mixed * r * gain_ref[...]).astype(BF16)
        return carry

    lax.fori_loop(0, chunks, phase_three, 0)


def vm(n):
    return [pl.BlockSpec(memory_space=pltpu.VMEM)] * n


SMEM = pl.BlockSpec(memory_space=pltpu.SMEM)


def delta_forward(place, z, taps, doc_col, doc_row, gain, dots=(dot3, dot3, dot3)):
    tokens, width = z.shape[0], taps.shape[1] // 3
    heads = width // HS
    chunks = tokens // CH
    n = chunks * heads
    sq = jax.ShapeDtypeStruct((n, CH, HS), F32)
    return pl.pallas_call(
        functools.partial(fwd_kernel, heads, chunks, *dots),
        out_shape=(jax.ShapeDtypeStruct((tokens, width), BF16), jax.ShapeDtypeStruct((tokens, width), F32),
                   sq, sq, sq, sq, sq, sq),
        in_specs=[SMEM] + vm(5), out_specs=tuple(vm(8)),
        scratch_shapes=[pltpu.VMEM((tokens + 8, 3 * width), F32), pltpu.VMEM((n, CH, HS), F32), pltpu.VMEM((n, CH, HS), F32)],
        compiler_params=pltpu.CompilerParams(vmem_limit_bytes=48 * 1024 * 1024),
        cost_estimate=pl.CostEstimate(flops=60_000_000_000, bytes_accessed=16_000_000, transcendentals=0),
        name="delta_forward",
    )(place, z, taps, doc_col, doc_row, gain)


def bwd_kernel(heads, chunks, dotg, dot,
               place, dh_ref, z_ref, taps_ref, doc_col, doc_row, gain_ref,
               mixed_ref, t_ref, h_ref, a_ref, qt_ref, w_ref, u_ref,
               dz_ref, dtaps_ref, dgain_ref,
               pad, do_s, eb_s, e_s, dc_s):
    width = heads * HS
    tokens = chunks * CH
    fill_pad(pad, place, z_ref, chunks, width)
    dz_ref[:, 3 * width:] = jnp.zeros((tokens, dz_ref.shape[1] - 3 * width), BF16)
    dc_s[tokens:] = jnp.zeros((8, 3 * width), F32)
    dtaps_ref[...] = jnp.zeros_like(dtaps_ref)
    row_i = lax.broadcasted_iota(jnp.int32, (CH, CH), 0)
    col_i = lax.broadcasted_iota(jnp.int32, (CH, CH), 1)

    def rows_of(c):
        return pl.ds(pl.multiple_of(c * CH, CH), CH)

    def phase_one(c, total):
        for h in range(heads):
            i = c * heads + h
            cols = slice(h * HS, (h + 1) * HS)
            m = mixed_ref[rows_of(c), cols]
            dy = dh_ref[place_rows(place, c), cols].astype(F32)
            r = lax.rsqrt(jnp.mean(m * m, axis=1, keepdims=True) + HEAD_FLOOR)
            mr = m * r
            total = total + jnp.sum(dy * mr, axis=0, keepdims=True)
            gy = gain_ref[...] * dy
            dm = r * (gy - mr * jnp.mean(mr * gy, axis=1, keepdims=True))
            do_s[i] = dm
            eb_s[i] = dot(qt_ref[i], dm, TN)
        return total

    dgain_ref[...] = lax.fori_loop(0, chunks, phase_one, jnp.zeros((1, HS), F32))

    def phase_two(n, state):
        c = chunks - 1 - n
        new = []
        for h in range(heads):
            i = c * heads + h
            e_s[i] = state[h]
            new.append(dot(a_ref[i], state[h], TN) + eb_s[i])
        return tuple(new)

    lax.fori_loop(0, chunks, phase_two, tuple(jnp.zeros((HS, HS), F32) for _ in range(heads)))

    def one(c, h):
        i = c * heads + h
        col, row, prev, last = chunk_docs(doc_col, doc_row, c)
        same = col == row
        strict = same & (row_i > col_i)
        incl = same & (row_i >= col_i)
        carried = (col == prev).astype(F32)
        closing = (col == last).astype(F32)
        dwin = doc_col[pl.ds(pl.multiple_of(c * CH, CH), CH + 8), :]
        masks = [(dwin[8 - j:CH + 8 - j] == col).astype(F32) for j in (1, 2, 3)]

        def conv(which):
            cols = slice(which * width + h * HS, which * width + (h + 1) * HS)
            taps = [taps_ref[t:t + 1, cols] for t in range(4)]
            z = conv_chunk(window(pad, c, cols), taps, masks)
            s, y = silu_parts(z)
            return y, s + y * (1.0 - s)

        q, q_slope = conv(0)
        k, k_slope = conv(1)
        v, v_slope = conv(2)
        n = lax.rsqrt(jnp.sum(k * k, axis=1, keepdims=True) + EPSILON)
        k = k * n
        beta = 1.0 / (1.0 + jnp.exp(-z_ref[place_rows(place, c), 3 * width + h:3 * width + h + 1]))
        inv, state, w, u, dm, e = t_ref[i], h_ref[i], w_ref[i], u_ref[i], do_s[i], e_s[i]
        gram = dotg(k, k, NT)
        p = jnp.where(incl, dot(q, k, NT), 0.0)
        r = u - dot(w, state)
        y = v - carried * dot(k, state)
        dr = dot(p, dm, TN) + closing * dot(k, e)
        x = dot(inv, dr, TN)
        dp = jnp.where(incl, dot(dm, r, NT), 0.0)
        dq = dot(dp, k) + carried * dot(dm, state, NT)
        dlow = jnp.where(strict, -dot(x, r, NT), 0.0)
        dgram = beta * dlow
        dk = closing * dot(r, e, NT) + dot(dp, q, TN) + dot(dgram, k) + dot(dgram, k, TN) - (carried * beta) * dot(x, state, NT)
        dbeta = jnp.sum(dlow * gram, axis=1, keepdims=True) + jnp.sum(x * y, axis=1, keepdims=True)
        dk = n * (dk - k * jnp.sum(k * dk, axis=1, keepdims=True))
        for which, value in ((0, dq * q_slope), (1, dk * k_slope), (2, beta * x * v_slope)):
            dc_s[rows_of(c), which * width + h * HS:which * width + (h + 1) * HS] = value
        dz_ref[place_rows(place, c), 3 * width + h:3 * width + h + 1] = (dbeta * beta * (1.0 - beta)).astype(BF16)

    per = 2

    def phase_three(g, carry):
        for e in range(per):
            for h in range(heads):
                one(g * per + e, h)
        return carry

    lax.fori_loop(0, chunks // per, phase_three, 0)

    def phase_four(c, carry):
        dwin = doc_col[pl.ds(pl.multiple_of(c * CH, CH), CH + 8), :]
        col = dwin[8:]
        after = doc_col[pl.ds(pl.multiple_of(c * CH + 8, 8), CH + 8), :]
        masks = [(dwin[8 - j:CH + 8 - j] == col).astype(F32) for j in (1, 2, 3)]
        later = [(after[j:CH + j] == col).astype(F32) for j in (1, 2, 3)]
        for b in range(3 * heads):
            cols = slice(b * HS, (b + 1) * HS)
            win = window(pad, c, cols)
            dwn = dc_s[pl.ds(pl.multiple_of(c * CH, CH), CH + 8), cols]
            d = dwn[:CH]
            dz = d * taps_ref[3:4, cols]
            dtaps_ref[3:4, cols] += jnp.sum(d * win[8:], axis=0, keepdims=True)
            for j in (1, 2, 3):
                dz = dz + later[j - 1] * pltpu.roll(dwn, CH + 8 - j, 0)[:CH] * taps_ref[3 - j:4 - j, cols]
                dtaps_ref[3 - j:4 - j, cols] += jnp.sum(masks[j - 1] * pltpu.roll(win, j, 0)[8:] * d, axis=0, keepdims=True)
            dz_ref[place_rows(place, c), cols] = dz.astype(BF16)
        return carry

    lax.fori_loop(0, chunks, phase_four, 0)


def delta_backward(place, dheads, z, taps, doc_col, doc_row, gain, saved, dots=(dot3, dot3)):
    tokens, width = z.shape[0], taps.shape[1] // 3
    heads = width // HS
    chunks = tokens // CH
    n = chunks * heads
    sq = pltpu.VMEM((n, CH, HS), F32)
    return pl.pallas_call(
        functools.partial(bwd_kernel, heads, chunks, *dots),
        out_shape=(jax.ShapeDtypeStruct(z.shape, BF16), jax.ShapeDtypeStruct((4, 3 * width), F32),
                   jax.ShapeDtypeStruct((1, HS), F32)),
        in_specs=[SMEM] + vm(13), out_specs=tuple(vm(3)),
        scratch_shapes=[pltpu.VMEM((tokens + 8, 3 * width), F32), sq, sq, sq, pltpu.VMEM((tokens + 8, 3 * width), F32)],
        compiler_params=pltpu.CompilerParams(vmem_limit_bytes=48 * 1024 * 1024),
        cost_estimate=pl.CostEstimate(flops=50_000_000_000, bytes_accessed=16_000_000, transcendentals=0),
        name="delta_backward",
    )(place, dheads, z, taps, doc_col, doc_row, gain, *saved)


def norm_kernel(chunk_of, half_of, a_ref, b_ref, gain_ref, out_ref):
    half = a_ref.shape[1]
    a, b = a_ref[...].astype(F32), b_ref[...].astype(F32)
    total = jnp.sum(a * a, axis=1, keepdims=True) + jnp.sum(b * b, axis=1, keepdims=True)
    r = lax.rsqrt(total / (2 * half) + EPSILON)
    out_ref[:, :half] = (a * r * gain_ref[:, :half]).astype(BF16)
    out_ref[:, half:] = (b * r * gain_ref[:, half:]).astype(BF16)


def copy_kernel(chunk_of, half_of, a_ref, b_ref, out_ref):
    half = a_ref.shape[1]
    out_ref[:, :half] = a_ref[...]
    out_ref[:, half:] = b_ref[...]


def ordered(kernel, chunk_of, half_of, x, *rest):
    tokens, width = x.shape
    half = width // 2
    return pl.pallas_call(
        kernel,
        grid_spec=pltpu.PrefetchScalarGridSpec(
            num_scalar_prefetch=2,
            grid=(tokens // CH,),
            in_specs=[
                pl.BlockSpec((CH, half), lambda p, ch, hf: (ch[p], hf[0])),
                pl.BlockSpec((CH, half), lambda p, ch, hf: (ch[p], hf[1])),
            ] + [pl.BlockSpec((1, width), lambda p, ch, hf: (0, 0)) for _ in rest],
            out_specs=pl.BlockSpec((CH, width), lambda p, ch, hf: (p, 0)),
        ),
        out_shape=jax.ShapeDtypeStruct((tokens, width), BF16),
        compiler_params=pltpu.CompilerParams(vmem_limit_bytes=32 * 1024 * 1024),
        cost_estimate=pl.CostEstimate(flops=10 * tokens * width, bytes_accessed=4 * tokens * width, transcendentals=0),
        name="ordered_rows",
    )(chunk_of, half_of, x, x, *rest)


def place_kernel(count, chunk_of, half_of, *refs):
    out = refs[2 * count]
    half = out.shape[1] // 2
    for p in range(2 * count):

        @pl.when(pl.program_id(0) == p)
        def _(p=p):
            for h in range(2):
                to = half_of[h] if p < count else half_of[1 - h]
                out[:, pl.ds(pl.multiple_of(to * half, half), half)] = refs[p][:, h * half:(h + 1) * half]


def place(chunk_of, half_of, own, partner):
    count = len(own)
    rows, width = own[0].shape
    return pl.pallas_call(
        functools.partial(place_kernel, count),
        grid_spec=pltpu.PrefetchScalarGridSpec(
            num_scalar_prefetch=2,
            grid=(2 * count,),
            in_specs=[pl.BlockSpec((rows, width), lambda p, ch, hf: (0, 0)) for _ in range(2 * count)],
            out_specs=pl.BlockSpec((rows, width), lambda p, ch, hf: (ch[p], 0)),
        ),
        out_shape=jax.ShapeDtypeStruct((2 * count * rows, width), own[0].dtype),
        compiler_params=pltpu.CompilerParams(vmem_limit_bytes=32 * 1024 * 1024),
        cost_estimate=pl.CostEstimate(flops=0, bytes_accessed=8 * count * rows * width, transcendentals=0),
        name="place_rows",
    )(chunk_of, half_of, *own, *partner)


def mm(left, right, dims=NN):
    return lax.dot_general(left, right, dims, preferred_element_type=F32)


def body(
    inputs, segments, mixer_gain, w_query, w_key, w_value, w_beta, conv_query, conv_key, conv_value,
    head_gain, w_out, feed_gain, w_gate, w_up, w_down, cotangent,
):
    cols, rows, groups = lax.axis_size("col"), lax.axis_size("row"), lax.axis_size("dp")
    c, r, g = lax.axis_index("col"), lax.axis_index("row"), lax.axis_index("dp")
    tokens, width = inputs.shape
    half, mine = width // cols, tokens // cols
    own_width = conv_query.shape[0]
    own_heads = own_width // HS
    feed = w_gate.shape[1]

    def swap(v):
        return lax.ppermute(v, "col", [(i, i ^ 1) for i in range(cols)])

    def to_row(v, k):
        return lax.ppermute(v, "row", [(i, i ^ k) for i in range(rows)])

    def row_sum(blocks):
        total = blocks[0]
        for k in range(rows - 1, 0, -1):
            total = total + to_row(blocks[k], k).astype(F32)
        return total

    def row_gather(own):
        return [own] + [to_row(own, k) for k in range(1, rows)]

    def own_first(v, axis=-1):
        size = v.shape[axis] // 2
        return jnp.concatenate([lax.dynamic_slice_in_dim(v, i * size, size, axis) for i in (c, 1 - c)], axis)

    def group_sum(v, flip=0):
        step, shards = 1, groups
        v = v.astype(BF16)
        while step < groups:
            bit = (g // step) % 2
            if step * 2 == groups:
                bit = bit ^ flip
            parts = v.reshape(shards // 2, 2, -1, v.shape[-1])
            keep = lax.dynamic_index_in_dim(parts, bit, 1, keepdims=False)
            send = lax.dynamic_index_in_dim(parts, 1 - bit, 1, keepdims=False)
            got = lax.ppermute(send, "dp", [(i, i ^ step) for i in range(groups)])
            v = keep.astype(F32) + got.astype(F32)
            step, shards = step * 2, shards // 2
            v = v.reshape(-1, v.shape[-1])
            if step < groups:
                v = v.astype(BF16)
        return v

    def all_sum(v):
        v = v + swap(v)
        k = 1
        while k < rows:
            v = v + to_row(v, k)
            k *= 2
        k = 1
        while k < groups:
            v = v + lax.ppermute(v, "dp", [(i, i ^ k) for i in range(groups)])
            k *= 2
        return v

    order = jnp.arange(cols * rows, dtype=jnp.int32)
    chunk_of = ((order % rows) ^ r) * cols + ((order // rows) ^ c)
    place_of = ((order % cols) ^ c) * rows + ((order // cols) ^ r)
    half_of = jnp.stack([c, 1 - c]).astype(jnp.int32)
    documents = (segments + (jnp.arange(segments.shape[0], dtype=jnp.int32) * segments.shape[1])[:, None]).reshape(-1)
    doc_col = jnp.pad(documents, (8, 8), constant_values=-1)[:, None]
    doc_row = documents.reshape(-1, CH)
    taps = jnp.concatenate([conv_query.T, conv_key.T, conv_value.T], 1)
    gain_row = head_gain[None]
    gain_one, gain_two = own_first(mixer_gain)[None], own_first(feed_gain)[None]

    def columns(i):
        parts = [lax.dynamic_slice_in_dim(w, i * own_width, own_width, 1) for w in (w_query, w_key, w_value)]
        beta = lax.dynamic_slice_in_dim(w_beta, i * own_heads, own_heads, 1)
        return jnp.concatenate(parts + [jnp.pad(beta, ((0, 0), (0, HS - own_heads)))], 1)

    w_own, w_oth = columns(c), columns(1 - c)
    w_own_x = swap(w_oth)
    act = ordered(norm_kernel, chunk_of, half_of, inputs, gain_one)
    z = mm(act[:, :half], w_own) + mm(act[:, half:], w_own_x)
    heads, *saved = delta_forward(place_of, z, taps, doc_col, doc_row, gain_row)
    w_out_x, w_gate_x, w_up_x, w_down_x, w_oth_x = swap(w_out), swap(w_gate), swap(w_up), swap(w_down), swap(w_own)
    w_out_all = jnp.concatenate([own_first(w_out, 0), own_first(w_out_x, 0)], 1)

    heads_0 = jnp.concatenate([heads[:mine], swap(heads[mine:])], 1)
    away = mm(heads_0[CH:], w_out_all).astype(BF16)
    near = mm(heads_0[:CH], w_out_all)
    attended = row_sum([near] + [away[k * CH:(k + 1) * CH] for k in range(rows - 1)])
    cot = ordered(copy_kernel, chunk_of, half_of, cotangent)
    upstream = cot[:CH].astype(F32)
    d_hidden = mm(cot[:mine, :half], w_down, NT) + mm(cot[:mine, half:], w_down_x, NT)

    x_own = own_first(lax.dynamic_slice_in_dim(inputs, chunk_of[0] * CH, CH, 0)).astype(F32)
    middle = x_own + attended
    norm_two = lax.rsqrt(jnp.mean(middle * middle, axis=1, keepdims=True) + EPSILON)
    act_two = jnp.concatenate(row_gather((middle * norm_two * gain_two).astype(BF16)), 0)
    gate = mm(act_two[:, :half], w_gate) + mm(act_two[:, half:], w_gate_x)
    upward = mm(act_two[:, :half], w_up) + mm(act_two[:, half:], w_up_x)
    s = jax.nn.sigmoid(gate)
    hidden = (gate * s * upward).astype(BF16)
    d_gate = (d_hidden * upward * s * (1.0 + gate * (1.0 - s))).astype(BF16)
    d_up = (d_hidden * gate * s).astype(BF16)

    def back_two(a, b):
        return jnp.concatenate([mm(a, w_gate, NT) + mm(b, w_up, NT), mm(a, w_gate_x, NT) + mm(b, w_up_x, NT)], 1)

    away = back_two(d_gate[CH:], d_up[CH:]).astype(BF16)
    near = back_two(d_gate[:CH], d_up[:CH])
    d_act_two = row_sum([near] + [away[k * CH:(k + 1) * CH] for k in range(rows - 1)])

    def norm_back(values, inverse, gains, grads):
        scaled = gains * grads
        normal = values * inverse
        shift = jnp.mean(normal * scaled, axis=1, keepdims=True)
        return inverse * (scaled - normal * shift), jnp.sum(grads * normal, axis=0)

    d_norm, feed_part = norm_back(middle, norm_two, gain_two, d_act_two)
    d_middle = upstream + d_norm
    d_att = jnp.concatenate(row_gather(d_middle.astype(BF16)), 0)
    d_heads = mm(d_att, w_out_all, NT).astype(BF16)
    d_heads = jnp.concatenate([d_heads[:, :own_width], swap(d_heads[:, own_width:])], 0)
    dz, d_taps, head_part = delta_backward(place_of, d_heads, z, taps, doc_col, doc_row, gain_row, saved)

    act_two_x, hidden_x, d_gate_x, d_up_x = swap(act_two[:, half:]), swap(hidden), swap(d_gate), swap(d_up)
    cot_x = cot[mine:, :half]
    down_grad = mm(hidden, cot[:mine, :half], TN) + mm(hidden_x, cot_x, TN)
    gate_grad = mm(act_two[:, :half], d_gate, TN) + mm(act_two_x, d_gate_x, TN)
    up_grad = mm(act_two[:, :half], d_up, TN) + mm(act_two_x, d_up_x, TN)
    down_grad, gate_grad, up_grad = group_sum(down_grad), group_sum(gate_grad), group_sum(up_grad)
    heads_1 = jnp.concatenate([heads[mine:], swap(heads[:mine])], 1)
    out_grad = mm(heads_0, d_att[:, :half], TN) + mm(heads_1, swap(d_att[:, half:]), TN)
    out_grad = group_sum(out_grad, c)

    def feed_out(h):
        return jnp.concatenate([mm(h, w_down), mm(h, w_down_x)], 1)

    away = feed_out(hidden[CH:]).astype(BF16)
    near = feed_out(hidden[:CH])
    output = (middle + row_sum([near] + [away[k * CH:(k + 1) * CH] for k in range(rows - 1)])).astype(BF16)
    output = row_gather(output)
    output = place(chunk_of, half_of, output, [swap(v) for v in output])

    dz_0 = swap(dz[mine:])
    dz_1 = swap(dz[:mine])

    def back_one(a, b):
        return jnp.concatenate([mm(a, w_own, NT) + mm(b, w_oth, NT), mm(a, w_own_x, NT) + mm(b, w_oth_x, NT)], 1)

    away = back_one(dz[CH:mine], dz_0[CH:]).astype(BF16)
    near = back_one(dz[:CH], dz_0[:CH])
    d_act = row_sum([near] + [away[k * CH:(k + 1) * CH] for k in range(rows - 1)])
    norm_one = lax.rsqrt(jnp.mean(x_own * x_own, axis=1, keepdims=True) + EPSILON)
    d_norm, mixer_part = norm_back(x_own, norm_one, gain_one, d_act)
    input_grad = row_gather((d_middle + d_norm).astype(BF16))
    input_grad = place(chunk_of, half_of, input_grad, [swap(v) for v in input_grad])
    grad_own = mm(act[:, :half], dz, TN)
    grad_oth = mm(act[:, :half], jnp.concatenate([dz_0, dz_1], 0), TN)
    grads = group_sum(jnp.concatenate([grad_own, grad_oth], 1))
    span = grads.shape[1] // 2

    def projection(start, size):
        a, b = grads[:, start:start + size], grads[:, span + start:span + start + size]
        return jnp.where(c == 0, jnp.concatenate([a, b], 1), jnp.concatenate([b, a], 1))

    query_grad, key_grad, value_grad = (projection(i * own_width, own_width) for i in range(3))
    beta_grad = projection(3 * own_width, own_heads)

    small = all_sum(jnp.concatenate([own_first(mixer_part), own_first(feed_part), head_part[0]]).reshape(-1, HS)).reshape(-1)
    share = width // groups
    mixer_gain_grad = lax.dynamic_slice_in_dim(small, g * share, share)
    feed_gain_grad = lax.dynamic_slice_in_dim(small, width + g * share, share)
    head_gain_grad = small[2 * width:]
    k = 1
    while k < groups:
        d_taps = d_taps + lax.ppermute(d_taps, "dp", [(i, i ^ k) for i in range(groups)])
        k *= 2
    share = own_width // groups
    conv_grads = [
        lax.dynamic_slice_in_dim(d_taps, i * own_width + g * share, share, 1).T for i in range(3)
    ]
    return (
        output, input_grad, mixer_gain_grad, query_grad, key_grad, value_grad, beta_grad, *conv_grads,
        head_gain_grad, out_grad, feed_gain_grad, gate_grad, up_grad, down_grad,
    )


def solution(mesh):
    weight, swapped = P("col", "row"), P("row", "col")
    taps = P(("row", "col"), None)
    grad, grad_taps = P(("col", "dp"), "row"), P(("row", "col", "dp"), None)
    grad_swapped = P(("row", "dp"), "col")
    tokens = P("dp", None)
    return jax.shard_map(
        body,
        mesh=mesh,
        in_specs=(
            tokens, tokens, P(), weight, weight, weight, weight, taps, taps, taps, P(), swapped, P(), weight, weight,
            swapped, tokens,
        ),
        out_specs=(
            tokens, tokens, P("dp"), grad, grad, grad, grad, grad_taps, grad_taps, grad_taps, P(), grad_swapped, P("dp"),
            grad, grad, grad_swapped,
        ),
        check_vma=False,
    )
```

```python
import functools
import jax
import jax.numpy as jnp
from jax import lax
from jax.experimental import pallas as pl
from jax.experimental.pallas import tpu as pltpu
from jax.sharding import PartitionSpec as P

EPSILON = 1e-06
HEAD_FLOOR = 0.02
CH = 128
HS = 128
F32 = jnp.float32
BF16 = jnp.bfloat16

NN = (((1,), (0,)), ((), ()))
NT = (((1,), (1,)), ((), ()))
TN = (((0,), (0,)), ((), ()))


def dot1(a, b, dims=NN):
    return lax.dot_general(a.astype(BF16), b.astype(BF16), dims, preferred_element_type=F32)


def split(a):
    hi = a.astype(BF16)
    return hi, (a - hi.astype(F32)).astype(BF16)


def dot3s(a, b, dims=NN):
    (ah, al), (bh, bl) = a, b
    ka, kb = dims[0][0][0], dims[0][1][0]
    left = jnp.concatenate([ah, al], ka)
    right = jnp.concatenate([jnp.concatenate([bh, bl], 1 - kb), jnp.concatenate([bh, jnp.zeros_like(bh)], 1 - kb)], kb)
    both = lax.dot_general(left, right, dims, preferred_element_type=F32)
    width = both.shape[1] // 2
    return both[:, :width] + both[:, width:]


def dot3(a, b, dims=NN):
    return dot3s(split(a), split(b), dims)


def silu_parts(z):
    s = 1.0 / (1.0 + jnp.exp(-z))
    return s, z * s


def together(steps):
    steps = list(steps)
    while steps:
        steps = [step for step in steps if next(step, steps) is not steps]


def unit_inverse(low, xor, eye, dot):
    inv = eye - jnp.where(xor < 2, low, 0.0)
    low16 = low.astype(BF16)
    size = 2
    while size < CH:
        part = jnp.where((xor >= size) & (xor < 2 * size), low, 0.0).astype(BF16)
        inv16 = inv.astype(BF16)
        half = dot1(inv16, part)
        yield
        inv = inv - dot1(half, inv16)
        yield
        size *= 2
    parts = split(inv)
    rest = (eye - inv) - dot3s(split(low), parts)
    yield
    return inv + dot3s(parts, split(rest))


def window(ref, c, cols):
    return ref[pl.ds(pl.multiple_of(c * CH, CH), CH + 8), cols]


def conv_chunk(win, taps, masks):
    out = win[8:] * taps[3]
    for j in (1, 2, 3):
        out = out + masks[j - 1] * pltpu.roll(win, j, 0)[8:] * taps[3 - j]
    return out


def chunk_docs(doc_col, doc_row, c):
    col = doc_col[pl.ds(pl.multiple_of(c * CH + 8, 8), CH), :]
    row = doc_row[pl.ds(c, 1), :]
    prev = doc_col[pl.ds(pl.multiple_of(c * CH, 8), 8), :][7:8]
    last = col[CH - 1:CH]
    return col, row, prev, last


def place_rows(place, c):
    return pl.ds(pl.multiple_of(place[c] * CH, CH), CH)


def own_beta(lanes, column, heads, h):
    return jnp.where(column == 0, lanes[:, h:h + 1], lanes[:, heads + h:heads + h + 1])


def fill_pad(pad, place, z_ref, chunks, width):
    pad[0:8] = jnp.zeros((8, 3 * width), F32)
    for c in range(chunks):
        pad[c * CH + 8:(c + 1) * CH + 8] = z_ref[place_rows(place, c), :3 * width]


def fwd_kernel(heads, chunks, dotg, doti, dot,
               place, z_ref, taps_ref, doc_col, doc_row, gain_ref,
               out_ref, mixed_ref, conv_ref, t_ref, h_ref, a_ref, qt_ref, w_ref, u_ref,
               pad, pu_s, b_s):
    width = heads * HS
    fill_pad(pad, place, z_ref, chunks, width)
    row_i = lax.broadcasted_iota(jnp.int32, (CH, CH), 0)
    col_i = lax.broadcasted_iota(jnp.int32, (CH, CH), 1)
    xor = row_i ^ col_i
    eye = (xor == 0).astype(F32)

    def one(c, h):
        col, row, prev, last = chunk_docs(doc_col, doc_row, c)
        same = col == row
        strict = same & (row_i > col_i)
        incl = same & (row_i >= col_i)
        carried = (col == prev).astype(F32)
        closing = (col == last).astype(F32)
        keep = (last == prev).astype(F32)
        dwin = doc_col[pl.ds(pl.multiple_of(c * CH, CH), CH + 8), :]
        masks = [(dwin[8 - j:CH + 8 - j] == col).astype(F32) for j in (1, 2, 3)]

        def conv(which):
            cols = slice(which * width + h * HS, which * width + (h + 1) * HS)
            taps = [taps_ref[t:t + 1, cols] for t in range(4)]
            z = conv_chunk(window(pad, c, cols), taps, masks)
            conv_ref[pl.ds(pl.multiple_of(c * CH, CH), CH), cols] = z
            return silu_parts(z)[1]

        q, k, v = conv(0), conv(1), conv(2)
        k = k * lax.rsqrt(jnp.sum(k * k, axis=1, keepdims=True) + EPSILON)
        beta = 1.0 / (1.0 + jnp.exp(-own_beta(z_ref[place_rows(place, c), 3 * width:], place[chunks], heads, h)))
        yield
        gram = dotg(k, k, NT)
        yield
        low = jnp.where(strict, beta * gram, 0.0)
        yield
        inv = yield from unit_inverse(low, xor, eye, doti)
        yield
        wu = dot(inv, jnp.concatenate([(carried * beta) * k, beta * v], 1))
        w, u = wu[:, :HS], wu[:, HS:]
        yield
        p = jnp.where(incl, dot(q, k, NT), 0.0)
        yield
        wus = split(wu)
        pwu = dot3s(split(p), wus)
        qt = carried * q - pwu[:, :HS]
        pu = pwu[:, HS:]
        yield
        kcl = closing * k
        ab = dot3s(split(kcl), wus, TN)
        a = keep * eye - ab[:, :HS]
        b = ab[:, HS:]
        yield
        i = c * heads + h
        t_ref[i] = inv
        qt_ref[i] = qt
        a_ref[i] = a
        w_ref[i] = w
        u_ref[i] = u
        pu_s[i] = pu
        b_s[i] = b

    per = 4

    def phase_one(g, carry):
        together(one(g * per + e, h) for e in range(per) for h in range(heads))
        return carry

    lax.fori_loop(0, chunks // per, phase_one, 0)

    def phase_two(c, state):
        new = []
        for h in range(heads):
            i = c * heads + h
            h_ref[i] = state[h]
            new.append(dot(a_ref[i], state[h]) + b_s[i])
        return tuple(new)

    lax.fori_loop(0, chunks, phase_two, tuple(jnp.zeros((HS, HS), F32) for _ in range(heads)))

    def phase_three(c, carry):
        for h in range(heads):
            i = c * heads + h
            rows = pl.ds(pl.multiple_of(c * CH, CH), CH)
            cols = slice(h * HS, (h + 1) * HS)
            mixed = dot(qt_ref[i], h_ref[i]) + pu_s[i]
            mixed_ref[rows, cols] = mixed
            r = lax.rsqrt(jnp.mean(mixed * mixed, axis=1, keepdims=True) + HEAD_FLOOR)
            out_ref[place_rows(place, c), cols] = (mixed * r * gain_ref[...]).astype(BF16)
        return carry

    lax.fori_loop(0, chunks, phase_three, 0)


def vm(n):
    return [pl.BlockSpec(memory_space=pltpu.VMEM)] * n


COST = pl.CostEstimate(flops=1000, bytes_accessed=1000, transcendentals=0)
SMEM = pl.BlockSpec(memory_space=pltpu.SMEM)
ANY = pl.BlockSpec(memory_space=pl.ANY)


def after(kernel, count, extra):
    return lambda *refs: kernel(*refs[:count], *refs[count + extra:])


def delta_forward(place, z, taps, doc_col, doc_row, gain, dots=(dot3, dot3, dot3)):
    tokens, width = z.shape[0], taps.shape[1] // 3
    heads = width // HS
    chunks = tokens // CH
    n = chunks * heads
    sq = jax.ShapeDtypeStruct((n, CH, HS), F32)
    return pl.pallas_call(
        functools.partial(fwd_kernel, heads, chunks, *dots),
        out_shape=(jax.ShapeDtypeStruct((tokens, width), BF16), jax.ShapeDtypeStruct((tokens, width), F32),
                   jax.ShapeDtypeStruct((tokens, 3 * width), F32), sq, sq, sq, sq, sq, sq),
        in_specs=[SMEM] + vm(5), out_specs=tuple(vm(9)),
        scratch_shapes=[pltpu.VMEM((tokens + 8, 3 * width), F32), pltpu.VMEM((n, CH, HS), F32), pltpu.VMEM((n, CH, HS), F32)],
        compiler_params=pltpu.CompilerParams(vmem_limit_bytes=48 * 1024 * 1024),
        cost_estimate=COST,
        name="delta_forward",
    )(place, z, taps, doc_col, doc_row, gain)


def bwd_kernel(heads, chunks, dotg, dot,
               place, dh_own, dh_other, z_ref, taps_ref, doc_col, doc_row, gain_ref,
               mixed_ref, conv_ref, t_ref, h_ref, a_ref, qt_ref, w_ref, u_ref,
               dz_ref, dtaps_ref, dgain_ref,
               dh_ref, do_s, eb_s, e_s, dc_s, db_s):
    width = heads * HS
    tokens = chunks * CH
    dh_ref[:tokens // 2] = dh_own[...]
    dh_ref[tokens // 2:] = dh_other[...]
    dc_s[tokens:] = jnp.zeros((8, 3 * width), F32)
    row_i = lax.broadcasted_iota(jnp.int32, (CH, CH), 0)
    col_i = lax.broadcasted_iota(jnp.int32, (CH, CH), 1)

    def rows_of(c):
        return pl.ds(pl.multiple_of(c * CH, CH), CH)

    def phase_one(c, total):
        for h in range(heads):
            i = c * heads + h
            cols = slice(h * HS, (h + 1) * HS)
            m = mixed_ref[rows_of(c), cols]
            dy = dh_ref[place_rows(place, c), cols].astype(F32)
            r = lax.rsqrt(jnp.mean(m * m, axis=1, keepdims=True) + HEAD_FLOOR)
            mr = m * r
            total = total + jnp.sum(dy * mr, axis=0, keepdims=True)
            gy = gain_ref[...] * dy
            dm = r * (gy - mr * jnp.mean(mr * gy, axis=1, keepdims=True))
            do_s[i] = dm
            eb_s[i] = dot(qt_ref[i], dm, TN)
        return total

    dgain_ref[...] = lax.fori_loop(0, chunks, phase_one, jnp.zeros((1, HS), F32))

    def phase_two(n, state):
        c = chunks - 1 - n
        new = []
        for h in range(heads):
            i = c * heads + h
            e_s[i] = state[h]
            new.append(dot(a_ref[i], state[h], TN) + eb_s[i])
        return tuple(new)

    lax.fori_loop(0, chunks, phase_two, tuple(jnp.zeros((HS, HS), F32) for _ in range(heads)))

    def one(c, h):
        i = c * heads + h
        col, row, prev, last = chunk_docs(doc_col, doc_row, c)
        same = col == row
        strict = same & (row_i > col_i)
        incl = same & (row_i >= col_i)
        carried = (col == prev).astype(F32)
        closing = (col == last).astype(F32)

        def conv(which):
            s, y = silu_parts(conv_ref[rows_of(c), which * width + h * HS:which * width + (h + 1) * HS])
            return y, s + y * (1.0 - s)

        q, q_slope = conv(0)
        k, k_slope = conv(1)
        v, v_slope = conv(2)
        n = lax.rsqrt(jnp.sum(k * k, axis=1, keepdims=True) + EPSILON)
        k = k * n
        beta = 1.0 / (1.0 + jnp.exp(-own_beta(z_ref[place_rows(place, c), 3 * width:], place[chunks], heads, h)))
        inv, state, w, u, dm, e = t_ref[i], h_ref[i], w_ref[i], u_ref[i], do_s[i], e_s[i]
        yield
        gram = dotg(k, k, NT)
        yield
        p = jnp.where(incl, dot(q, k, NT), 0.0)
        yield
        r = u - dot(w, state)
        yield
        y = v - carried * dot(k, state)
        yield
        dr = dot(p, dm, TN) + closing * dot(k, e)
        yield
        x = dot(inv, dr, TN)
        yield
        dp = jnp.where(incl, dot(dm, r, NT), 0.0)
        yield
        dq = dot(dp, k) + carried * dot(dm, state, NT)
        yield
        dlow = jnp.where(strict, -dot(x, r, NT), 0.0)
        dgram = beta * dlow
        yield
        dk = closing * dot(r, e, NT) + dot(dp, q, TN)
        yield
        dk = dk + dot(dgram, k) + dot(dgram, k, TN)
        yield
        dk = dk - (carried * beta) * dot(x, state, NT)
        yield
        dbeta = jnp.sum(dlow * gram, axis=1, keepdims=True) + jnp.sum(x * y, axis=1, keepdims=True)
        dk = n * (dk - k * jnp.sum(k * dk, axis=1, keepdims=True))
        for which, value in ((0, dq * q_slope), (1, dk * k_slope), (2, beta * x * v_slope)):
            dc_s[rows_of(c), which * width + h * HS:which * width + (h + 1) * HS] = value
        db_s[h, rows_of(c)] = dbeta * beta * (1.0 - beta)

    per = 4

    def phase_three(g, carry):
        together(one(g * per + e, h) for e in range(per) for h in range(heads))
        return carry

    lax.fori_loop(0, chunks // per, phase_three, 0)

    def phase_four(c, sums):
        col = doc_col[pl.ds(pl.multiple_of(c * CH + 8, 8), CH), :]
        after = doc_col[pl.ds(pl.multiple_of(c * CH + 8, 8), CH + 8), :]
        later = [jnp.broadcast_to((after[j:CH + j] == col).astype(F32), (CH, HS)) for j in (1, 2, 3)]
        new = []
        for b in range(3 * heads):
            cols = slice(b * HS, (b + 1) * HS)
            z = z_ref[place_rows(place, c), cols]
            win = dc_s[pl.ds(pl.multiple_of(c * CH, CH), CH + 8), cols]
            dz = 0.0
            for j in range(4):
                d = win[:CH] if j == 0 else later[j - 1] * pltpu.roll(win, CH + 8 - j, 0)[:CH]
                dz = dz + d * taps_ref[3 - j:4 - j, cols]
                new.append(sums[4 * b + j] + jnp.sum((d * z).reshape(CH // 8, 8, HS), axis=0))
            dz_ref[place_rows(place, c), cols] = dz.astype(BF16)
        lane = lax.broadcasted_iota(jnp.int32, (CH, HS), 1) - place[chunks] * heads
        betas = sum(jnp.where(lane == h, db_s[h, rows_of(c)], 0.0) for h in range(heads))
        dz_ref[place_rows(place, c), 3 * width:] = betas.astype(BF16)
        return tuple(new)

    sums = lax.fori_loop(0, chunks, phase_four, tuple(jnp.zeros((8, HS), F32) for _ in range(12 * heads)))
    for b in range(3 * heads):
        for j in range(4):
            dtaps_ref[3 - j:4 - j, b * HS:(b + 1) * HS] = jnp.sum(sums[4 * b + j], axis=0, keepdims=True)


def delta_backward(place, own, other, z, taps, doc_col, doc_row, gain, saved, ready=(), dots=(dot3, dot3)):
    tokens, width = z.shape[0], taps.shape[1] // 3
    heads = width // HS
    chunks = tokens // CH
    n = chunks * heads
    sq = pltpu.VMEM((n, CH, HS), F32)
    return pl.pallas_call(
        after(functools.partial(bwd_kernel, heads, chunks, *dots), 16, len(ready)),
        out_shape=(jax.ShapeDtypeStruct(z.shape, BF16), jax.ShapeDtypeStruct((4, 3 * width), F32),
                   jax.ShapeDtypeStruct((1, HS), F32)),
        in_specs=[SMEM] + vm(15) + [ANY] * len(ready), out_specs=tuple(vm(3)),
        scratch_shapes=[pltpu.VMEM((tokens, width), BF16), sq, sq, sq, pltpu.VMEM((tokens + 8, 3 * width), F32),
                        pltpu.VMEM((heads, tokens, 1), F32)],
        compiler_params=pltpu.CompilerParams(vmem_limit_bytes=48 * 1024 * 1024),
        cost_estimate=COST,
        name="delta_backward",
    )(place, own, other, z, taps, doc_col, doc_row, gain, *saved, *ready)


def norm_kernel(chunk_of, half_of, a_ref, b_ref, gain_ref, out_ref):
    half = a_ref.shape[1]
    a, b = a_ref[...].astype(F32), b_ref[...].astype(F32)
    total = jnp.sum(a * a, axis=1, keepdims=True) + jnp.sum(b * b, axis=1, keepdims=True)
    r = lax.rsqrt(total / (2 * half) + EPSILON)
    out_ref[:, :half] = (a * r * gain_ref[:, :half]).astype(BF16)
    out_ref[:, half:] = (b * r * gain_ref[:, half:]).astype(BF16)


def copy_kernel(chunk_of, half_of, a_ref, b_ref, out_ref):
    half = a_ref.shape[1]
    out_ref[:, :half] = a_ref[...]
    out_ref[:, half:] = b_ref[...]


def ordered(kernel, chunk_of, half_of, x, *rest, ready=()):
    tokens, width = x.shape
    half = width // 2
    return pl.pallas_call(
        after(kernel, 4 + len(rest), len(ready)),
        grid_spec=pltpu.PrefetchScalarGridSpec(
            num_scalar_prefetch=2,
            grid=(tokens // CH,),
            in_specs=[
                pl.BlockSpec((CH, half), lambda p, ch, hf: (ch[p], hf[0])),
                pl.BlockSpec((CH, half), lambda p, ch, hf: (ch[p], hf[1])),
            ] + [pl.BlockSpec((1, width), lambda p, ch, hf: (0, 0)) for _ in rest] + [ANY] * len(ready),
            out_specs=pl.BlockSpec((CH, width), lambda p, ch, hf: (p, 0)),
        ),
        out_shape=jax.ShapeDtypeStruct((tokens, width), BF16),
        compiler_params=pltpu.CompilerParams(vmem_limit_bytes=32 * 1024 * 1024),
        cost_estimate=COST,
        name="ordered_rows",
    )(chunk_of, half_of, x, x, *rest, *ready)


def place_kernel(count, chunk_of, half_of, *refs):
    out = refs[2 * count]
    half = out.shape[1] // 2
    for p in range(2 * count):

        @pl.when(pl.program_id(0) == p)
        def _(p=p):
            for h in range(2):
                to = half_of[h] if p < count else half_of[1 - h]
                out[:, pl.ds(pl.multiple_of(to * half, half), half)] = refs[p][:, h * half:(h + 1) * half]


def place(chunk_of, half_of, own, partner, ready=()):
    count = len(own)
    rows, width = own[0].shape
    return pl.pallas_call(
        after(functools.partial(place_kernel, count), 2 + 2 * count, len(ready)),
        grid_spec=pltpu.PrefetchScalarGridSpec(
            num_scalar_prefetch=2,
            grid=(2 * count,),
            in_specs=[pl.BlockSpec((rows, width), lambda p, ch, hf: (0, 0)) for _ in range(2 * count)] + [ANY] * len(ready),
            out_specs=pl.BlockSpec((rows, width), lambda p, ch, hf: (ch[p], 0)),
        ),
        out_shape=jax.ShapeDtypeStruct((2 * count * rows, width), own[0].dtype),
        compiler_params=pltpu.CompilerParams(vmem_limit_bytes=32 * 1024 * 1024),
        cost_estimate=COST,
        name="place_rows",
    )(chunk_of, half_of, *own, *partner, *ready)


BIG = pltpu.CompilerParams(vmem_limit_bytes=32 * 1024 * 1024)


def swiglu_kernel(rows, *refs):
    acts, (wg, wgx, wu, wux, dh, out, act_near, act_far) = refs[:rows], refs[rows:]
    half = wg.shape[0]
    near = jnp.concatenate([wg[...], wu[...]], 1)
    far = jnp.concatenate([wgx[...], wux[...]], 1)
    cut = wg.shape[1]
    size = acts[0].shape[0]

    @pl.when(pl.program_id(0) == 0)
    def _():
        for k in range(rows):
            act_near[k * size:(k + 1) * size] = acts[k][:, :half]
            act_far[k * size:(k + 1) * size] = acts[k][:, half:]

    for k in range(rows):
        both = dot1(acts[k][:, :half], near) + dot1(acts[k][:, half:], far)
        gate, up, dhk = both[:, :cut], both[:, cut:], dh[k * size:(k + 1) * size].astype(F32)
        s = 1.0 / (1.0 + jnp.exp(-gate))
        gs = gate * s
        for i, v in enumerate((gs * up, dhk * up * (s + gs * (1.0 - s)), dhk * gs)):
            out[(i * rows + k) * size:(i * rows + k + 1) * size] = v.astype(BF16)


def swiglu(acts, w_gate, w_gate_x, w_up, w_up_x, d_hidden):
    rows = len(acts)
    size, width = acts[0].shape
    half, feed = w_gate.shape
    tile = 128
    tokens = rows * size
    weight = pl.BlockSpec((half, tile), lambda n: (0, n))
    return pl.pallas_call(
        functools.partial(swiglu_kernel, rows),
        grid=(feed // tile,),
        in_specs=[pl.BlockSpec((size, width), lambda n: (0, 0))] * rows + [weight] * 4
        + [pl.BlockSpec((tokens, tile), lambda n: (0, n))],
        out_specs=(pl.BlockSpec((3 * tokens, tile), lambda n: (0, n)),) + (pl.BlockSpec((tokens, half), lambda n: (0, 0)),) * 2,
        out_shape=(jax.ShapeDtypeStruct((3 * tokens, feed), BF16),) + (jax.ShapeDtypeStruct((tokens, half), BF16),) * 2,
        compiler_params=BIG,
        cost_estimate=COST,
        name="swiglu",
    )(*acts, w_gate, w_gate_x, w_up, w_up_x, d_hidden)


def back_kernel(count, parts, *refs):
    lefts, near, far = refs[:count], refs[count:2 * count], refs[2 * count:3 * count]
    outs = refs[3 * count:]

    def store(weights):
        both = sum(dot1(left[...], w[...], NT) for left, w in zip(lefts, weights))
        size = both.shape[0] // parts
        for k in range(parts):
            outs[k][...] = both[k * size:(k + 1) * size].astype(outs[k].dtype)

    steps = pl.num_programs(0) // 2
    pl.when(pl.program_id(0) < steps)(lambda: store(near))
    pl.when(pl.program_id(0) >= steps)(lambda: store(far))


def back(lefts, near, far, parts, tokens, ready=()):
    count = len(lefts)
    half = near[0].shape[0]
    tile = 512
    steps = half // tile
    size = tokens // parts
    return pl.pallas_call(
        after(functools.partial(back_kernel, count, parts), 3 * count, len(ready)),
        grid=(2 * steps,),
        in_specs=[pl.BlockSpec((tokens, v.shape[1]), lambda n, i=i: (i, 0)) for v, i in lefts]
        + [pl.BlockSpec((tile, w.shape[1]), lambda n: (jnp.minimum(n, steps - 1), 0)) for w in near]
        + [pl.BlockSpec((tile, w.shape[1]), lambda n: (jnp.maximum(n - steps, 0), 0)) for w in far] + [ANY] * len(ready),
        out_specs=tuple(pl.BlockSpec((size, tile), lambda n: (0, n)) for _ in range(parts)),
        out_shape=tuple(jax.ShapeDtypeStruct((size, 2 * half), F32 if k == 0 else BF16) for k in range(parts)),
        compiler_params=BIG,
        cost_estimate=COST,
        name="back_product",
    )(*[v for v, _ in lefts], *near, *far, *ready)


def grad_kernel(pairs, bit, *refs):
    lefts, rights = refs[:len(pairs)], refs[len(pairs):-2]
    send, keep = refs[-2:]
    out = jnp.concatenate([
        sum(lax.dot_general(lefts[i][...], rights[j][...], TN, preferred_element_type=F32) for i, j in group)
        for group in zip(*[[(i, j) for j in js] for i, js in enumerate(pairs)])
    ], 1).astype(BF16)
    steps = pl.num_programs(0) // 2

    @pl.when(pl.program_id(0) < steps)
    def _():
        send[0] = out

    @pl.when(pl.program_id(0) >= steps)
    def _():
        keep[0] = out


def weight_grad(bit, lefts, rights, pairs, tokens, columns, shards, ready=()):
    rows = columns // shards
    wide = sum(rights[j][0].shape[1] for j in pairs[0])
    half = shards // 2

    def shard(n, b):
        return (n % half) * 2 + jnp.where(n < half, 1 - b[0], b[0])

    shape = jax.ShapeDtypeStruct((half, rows, wide), BF16)
    return pl.pallas_call(
        after(functools.partial(grad_kernel, pairs), 1 + len(lefts) + len(rights), len(ready)),
        grid_spec=pltpu.PrefetchScalarGridSpec(
            num_scalar_prefetch=1,
            grid=(shards,),
            in_specs=[pl.BlockSpec((tokens, rows), lambda n, b, i=i: (i, shard(n, b))) for _, i in lefts]
            + [pl.BlockSpec((tokens, v.shape[1]), lambda n, b, i=i: (i, 0)) for v, i in rights] + [ANY] * len(ready),
            out_specs=(
                pl.BlockSpec((1, rows, wide), lambda n, b: (jnp.minimum(n, half - 1), 0, 0)),
                pl.BlockSpec((1, rows, wide), lambda n, b: (jnp.maximum(n - half, 0), 0, 0)),
            ),
        ),
        out_shape=(shape, shape),
        compiler_params=BIG,
        cost_estimate=COST,
        name="weight_grad",
    )(bit, *[v for v, _ in lefts], *[v for v, _ in rights], *ready)


def out_kernel(col, own, other, near, far, *outs):
    first, width = col[0], own.shape[1]
    left = jnp.concatenate([own[...], other[...]], 1)
    half = near.shape[1]
    for h, w in enumerate((near, far)):
        right = jnp.concatenate([w[pl.ds(pl.multiple_of(i * width, width), width)] for i in (first, 1 - first)], 0)
        both = dot1(left, right)
        size = outs[0].shape[0]
        for k, out in enumerate(outs):
            out[:, h * half:(h + 1) * half] = both[k * size:(k + 1) * size].astype(out.dtype)


def out_product(col, heads, other, w_out, w_out_x, parts, ready=()):
    tokens, width = other.shape[0] // 2, other.shape[1]
    half = w_out.shape[1]
    size = tokens // parts
    full = lambda v: pl.BlockSpec(v.shape, lambda n, c: (0, 0))
    return pl.pallas_call(
        after(out_kernel, 5, len(ready)),
        grid_spec=pltpu.PrefetchScalarGridSpec(
            num_scalar_prefetch=1,
            grid=(1,),
            in_specs=[
                pl.BlockSpec((tokens, width), lambda n, c: (0, 0)), pl.BlockSpec((tokens, width), lambda n, c: (1, 0)),
                full(w_out), full(w_out_x),
            ] + [ANY] * len(ready),
            out_specs=tuple(pl.BlockSpec((size, 2 * half), lambda n, c: (0, 0)) for _ in range(parts)),
        ),
        out_shape=tuple(jax.ShapeDtypeStruct((size, 2 * half), F32 if k == 0 else BF16) for k in range(parts)),
        compiler_params=BIG,
        cost_estimate=COST,
        name="out_product",
    )(col, heads, other, w_out, w_out_x, *ready)


def head_grad_kernel(parts, col, *refs):
    grads, (near, far, own, other, near_out, far_out) = refs[:parts], refs[parts:]
    width, half = own.shape[1], near.shape[1]
    size = grads[0].shape[0]
    for k in range(parts):
        near_out[k * size:(k + 1) * size] = grads[k][:, :half]
        far_out[k * size:(k + 1) * size] = grads[k][:, half:]
    for i, out in ((col[0], own), (1 - col[0], other)):
        rows = pl.ds(pl.multiple_of(i * width, width), width)
        right = jnp.concatenate([near[rows], far[rows]], 1)
        for k in range(parts):
            out[k * size:(k + 1) * size] = dot1(grads[k][...], right, NT).astype(BF16)


def head_grad(col, grads, w_out, w_out_x, width, ready=()):
    parts, size = len(grads), grads[0].shape[0]
    shape = jax.ShapeDtypeStruct((parts * size, width), BF16)
    shape_two = jax.ShapeDtypeStruct((parts * size, w_out.shape[1]), BF16)
    return pl.pallas_call(
        after(functools.partial(head_grad_kernel, parts), parts + 3, len(ready)),
        in_specs=[SMEM] + vm(parts + 2) + [ANY] * len(ready),
        out_specs=tuple(vm(4)),
        out_shape=(shape, shape, shape_two, shape_two),
        compiler_params=BIG,
        cost_estimate=COST,
        name="head_grad",
    )(col, *grads, w_out, w_out_x, *ready)


def middle_kernel(count, chunk_of, half_of, *refs):
    terms, (a, b, gain, middle, act, own) = refs[:count], refs[count:]
    own[...] = jnp.concatenate([a[...], b[...]], 1)
    total = own[...].astype(F32)
    for term in terms:
        total = total + term[...].astype(F32)
    middle[...] = total
    act[...] = (total * lax.rsqrt(jnp.mean(total * total, axis=1, keepdims=True) + EPSILON) * gain[...]).astype(BF16)


def middle_rows(chunk_of, half_of, terms, x, gain, ready=()):
    count = len(terms)
    rows, width = terms[0].shape
    steps, rows = 4, rows // 4
    whole = pl.BlockSpec((rows, width), lambda n, ch, hf: (n, 0))
    return pl.pallas_call(
        after(functools.partial(middle_kernel, count), count + 5, len(ready)),
        grid_spec=pltpu.PrefetchScalarGridSpec(
            num_scalar_prefetch=2,
            grid=(steps,),
            in_specs=[whole] * count + [
                pl.BlockSpec((rows, width // 2), lambda n, ch, hf: (ch[0] * steps + n, hf[0])),
                pl.BlockSpec((rows, width // 2), lambda n, ch, hf: (ch[0] * steps + n, hf[1])),
                pl.BlockSpec((1, width), lambda n, ch, hf: (0, 0)),
            ] + [ANY] * len(ready),
            out_specs=(whole, whole, whole),
        ),
        out_shape=tuple(jax.ShapeDtypeStruct((steps * rows, width), t) for t in (F32, BF16, BF16)),
        compiler_params=BIG,
        cost_estimate=COST,
        name="middle_rows",
    )(chunk_of, half_of, *terms, x, x, gain, *ready)


def norm_back_kernel(count, *refs):
    terms, (values, gain, upstream, total, low, part) = refs[:count], refs[count:]
    grads = terms[0][...]
    for term in terms[1:]:
        grads = grads + term[...].astype(F32)
    v = values[...].astype(F32)
    r = lax.rsqrt(jnp.mean(v * v, axis=1, keepdims=True) + EPSILON)
    normal = v * r
    scaled = gain[...] * grads
    out = upstream[...].astype(F32) + r * (scaled - normal * jnp.mean(normal * scaled, axis=1, keepdims=True))
    total[...] = out
    low[...] = out.astype(BF16)

    @pl.when(pl.program_id(0) == 0)
    def _():
        part[...] = jnp.zeros_like(part)

    part[...] += jnp.sum(grads * normal, axis=0, keepdims=True)


def norm_back(terms, values, gain, upstream, ready=()):
    count = len(terms)
    rows, width = values.shape
    steps = 4
    whole = pl.BlockSpec((rows // steps, width), lambda n: (n, 0))
    row = pl.BlockSpec((1, width), lambda n: (0, 0))
    return pl.pallas_call(
        after(functools.partial(norm_back_kernel, count), count + 3, len(ready)),
        grid=(steps,),
        in_specs=[whole] * (count + 1) + [row, whole] + [ANY] * len(ready),
        out_specs=(whole, whole, row),
        out_shape=(
            jax.ShapeDtypeStruct((rows, width), F32), jax.ShapeDtypeStruct((rows, width), BF16),
            jax.ShapeDtypeStruct((1, width), F32),
        ),
        compiler_params=BIG,
        cost_estimate=COST,
        name="norm_back",
    )(*terms, values, gain, upstream, *ready)


def split_rows(bit, value, send, keep):
    rows = send.shape[1]
    for j in range(2 * send.shape[0]):
        part = value[j * rows:(j + 1) * rows].astype(BF16)
        for to, same in ((send, False), (keep, True)):

            @pl.when((bit == j % 2) == same)
            def _(to=to, j=j, part=part):
                to[j // 2] = part


def down_kernel(bit, hidden, hidden_x, cot, cot_x, send, keep):
    split_rows(bit[0], dot1(hidden[...], cot[...], TN) + dot1(hidden_x[...], cot_x[...], TN), send, keep)


def down_weight_grad(bit, hidden, hidden_x, cot, half, shards, ready=()):
    tokens, feed = hidden.shape[0] // 3, hidden.shape[1]
    tile = 512
    shape = jax.ShapeDtypeStruct((shards // 2, feed // shards, half), BF16)
    out = pl.BlockSpec((shards // 2, feed // shards, tile), lambda n, b: (0, 0, n))
    return pl.pallas_call(
        after(down_kernel, 5, len(ready)),
        grid_spec=pltpu.PrefetchScalarGridSpec(
            num_scalar_prefetch=1,
            grid=(half // tile,),
            in_specs=[
                pl.BlockSpec((tokens, feed), lambda n, b: (0, 0)),
                pl.BlockSpec((tokens, feed), lambda n, b: (0, 0)),
                pl.BlockSpec((tokens, tile), lambda n, b: (0, n)),
                pl.BlockSpec((tokens, tile), lambda n, b: (1, n)),
            ] + [ANY] * len(ready),
            out_specs=(out, out),
        ),
        out_shape=(shape, shape),
        compiler_params=BIG,
        cost_estimate=COST,
        name="down_weight_grad",
    )(bit, hidden, hidden_x, cot, cot, *ready)


def out_grad_kernel(bit, heads, other, grads, grads_x, send, keep):
    tokens = grads.shape[0]
    g, gx = grads[...], grads_x[...]
    own = dot1(heads[:tokens], g, TN) + dot1(heads[tokens:], gx, TN)
    away = dot1(other[tokens:], g, TN) + dot1(other[:tokens], gx, TN)
    split_rows(bit[0], jnp.concatenate([own, away], 0), send, keep)


def out_weight_grad(bit, heads, other, grads, grads_x, shards, ready=()):
    half, wide = grads_x.shape[1], 2 * other.shape[1]
    shape = jax.ShapeDtypeStruct((shards // 2, wide // shards, half), BF16)
    return pl.pallas_call(
        after(out_grad_kernel, 5, len(ready)),
        in_specs=[SMEM] + vm(4) + [ANY] * len(ready),
        out_specs=tuple(vm(2)),
        out_shape=(shape, shape),
        compiler_params=BIG,
        cost_estimate=COST,
        name="out_weight_grad",
    )(bit, heads, other, grads, grads_x, *ready)


def feed_kernel(parts, hidden, near, far, *outs):
    size = hidden.shape[0] // parts

    def store(w):
        both = dot1(hidden[...], w[...])
        for k in range(parts):
            outs[k][...] = both[k * size:(k + 1) * size].astype(outs[k].dtype)

    pl.when(pl.program_id(0) == 0)(lambda: store(near))
    pl.when(pl.program_id(0) == 1)(lambda: store(far))


def feed_product(hidden, near, far, parts, ready=()):
    tokens, half = hidden.shape[0] // 3, near.shape[1]
    size = tokens // parts
    whole = lambda v: pl.BlockSpec(v.shape, lambda n: (0, 0))
    return pl.pallas_call(
        after(functools.partial(feed_kernel, parts), 3, len(ready)),
        grid=(2,),
        in_specs=[pl.BlockSpec((tokens, hidden.shape[1]), lambda n: (0, 0)), whole(near), whole(far)] + [ANY] * len(ready),
        out_specs=tuple(pl.BlockSpec((size, half), lambda n: (0, n)) for _ in range(parts)),
        out_shape=tuple(jax.ShapeDtypeStruct((size, 2 * half), F32 if k == 0 else BF16) for k in range(parts)),
        compiler_params=BIG,
        cost_estimate=COST,
        name="feed_product",
    )(hidden, near, far, *ready)


def sum_kernel(*refs):
    total = refs[0][...]
    for ref in refs[1:-1]:
        total = total + ref[...].astype(F32)
    refs[-1][...] = total.astype(BF16)


def sum_rows(terms, ready=()):
    return pl.pallas_call(
        after(sum_kernel, len(terms), len(ready)),
        in_specs=vm(len(terms)) + [ANY] * len(ready),
        out_specs=vm(1)[0],
        out_shape=jax.ShapeDtypeStruct(terms[0].shape, BF16),
        compiler_params=BIG,
        cost_estimate=COST,
        name="sum_rows",
    )(*terms, *ready)


def halve_kernel(bit, kept, got, send, keep):
    for out, i in ((send, 1 - bit[0]), (keep, bit[0])):
        out[...] = (kept[pl.ds(i, 1)].astype(F32) + got[pl.ds(i, 1)].astype(F32)).astype(BF16)


def halve(bit, kept, got, ready=()):
    shards, rows, columns = kept.shape
    pair = pl.BlockSpec((2, rows, columns), lambda n, b: (n, 0, 0))
    one = pl.BlockSpec((1, rows, columns), lambda n, b: (n, 0, 0))
    shape = jax.ShapeDtypeStruct((shards // 2, rows, columns), BF16)
    return pl.pallas_call(
        after(halve_kernel, 3, len(ready)),
        grid_spec=pltpu.PrefetchScalarGridSpec(
            num_scalar_prefetch=1, grid=(shards // 2,), in_specs=[pair, pair] + [ANY] * len(ready), out_specs=(one, one),
        ),
        out_shape=(shape, shape),
        compiler_params=BIG,
        cost_estimate=COST,
        name="halve",
    )(bit, kept, got, *ready)


def hold(v, ready):
    def kernel(v_ref, *refs):
        pass

    return pl.pallas_call(
        kernel,
        in_specs=[ANY] * (1 + len(ready)),
        out_specs=ANY,
        out_shape=jax.ShapeDtypeStruct(v.shape, v.dtype),
        input_output_aliases={0: 0},
        cost_estimate=COST,
        name="hold",
    )(v, *ready)


def mm(left, right, dims=NN):
    return lax.dot_general(left, right, dims, preferred_element_type=F32)


def body(
    inputs, segments, mixer_gain, w_query, w_key, w_value, w_beta, conv_query, conv_key, conv_value,
    head_gain, w_out, feed_gain, w_gate, w_up, w_down, cotangent,
):
    cols, rows, groups = lax.axis_size("col"), lax.axis_size("row"), lax.axis_size("dp")
    c, r, g = lax.axis_index("col"), lax.axis_index("row"), lax.axis_index("dp")
    tokens, width = inputs.shape
    half, mine = width // cols, tokens // cols
    own_width = conv_query.shape[0]
    feed = w_gate.shape[1]

    def swap(v):
        return lax.ppermute(v, "col", [(i, i ^ 1) for i in range(cols)])

    def to_row(v, k):
        return lax.ppermute(v, "row", [(i, i ^ k) for i in range(rows)])

    def row_terms(blocks):
        return [blocks[0]] + [to_row(blocks[k], k) for k in range(rows - 1, 0, -1)]

    def row_gather(own):
        return [own] + [to_row(own, k) for k in range(1, rows)]

    def own_first(v, axis=-1):
        size = v.shape[axis] // 2
        return jnp.concatenate([lax.dynamic_slice_in_dim(v, i * size, size, axis) for i in (c, 1 - c)], axis)

    def halves(v, bit):
        parts = v.reshape(v.shape[0] // 2, 2, *v.shape[1:])
        return [lax.dynamic_index_in_dim(parts, i, 1, keepdims=False) for i in (1 - bit, bit)]

    def traded(v, step):
        return lax.ppermute(v, "dp", [(i, i ^ step) for i in range(groups)])

    def group_steps(pair, got, ready, flip=0):
        step = 1
        while step * 2 < groups:
            got = got if step == 1 else traded(pair[0], step)
            step *= 2
            bit = (g // step) % 2
            pair = halve((bit ^ flip if step * 2 == groups else bit).astype(jnp.int32)[None], pair[1], got, ready)
        return pair

    def group_end(pair, got):
        v = pair[1].astype(F32) + got.astype(F32)
        return v.reshape(v.shape[1:])

    def shards_of(v):
        return halves(v.astype(BF16).reshape(groups, -1, v.shape[-1]), g % 2)

    def grads_of(lefts, rights, pairs, columns, ready):
        if columns // groups % 128 == 0:
            return weight_grad(low_bit, lefts, rights, pairs, mine, columns, groups, ready)

        def rows_of(v, i):
            return v[i * mine:(i + 1) * mine]

        return shards_of(jnp.concatenate([
            sum(mm(rows_of(*lefts[i])[:, :columns], rows_of(*rights[j]), TN) for i, j in enumerate(js)) for js in zip(*pairs)
        ], 1))

    def all_sum(v):
        v = v + swap(v)
        k = 1
        while k < rows:
            v = v + to_row(v, k)
            k *= 2
        k = 1
        while k < groups:
            v = v + lax.ppermute(v, "dp", [(i, i ^ k) for i in range(groups)])
            k *= 2
        return v

    order = jnp.arange(cols * rows, dtype=jnp.int32)
    chunk_of = ((order % rows) ^ r) * cols + ((order // rows) ^ c)
    place_of = ((order % cols) ^ c) * rows + ((order // cols) ^ r)
    half_of = jnp.stack([c, 1 - c]).astype(jnp.int32)
    place_of = jnp.concatenate([place_of, half_of[:1]])
    low_bit = (g % 2).astype(jnp.int32)[None]
    documents = (segments + (jnp.arange(segments.shape[0], dtype=jnp.int32) * segments.shape[1])[:, None]).reshape(-1)
    doc_col = jnp.pad(documents, (8, 8), constant_values=-1)[:, None]
    doc_row = documents.reshape(-1, CH)
    taps = jnp.concatenate([conv_query.T, conv_key.T, conv_value.T], 1)
    gain_row = head_gain[None]
    gain_one, gain_two = own_first(mixer_gain)[None], own_first(feed_gain)[None]

    w_beta_wide = jnp.pad(w_beta, ((0, 0), (0, HS - w_beta.shape[1])))

    def columns(i):
        parts = [lax.dynamic_slice_in_dim(w, i * own_width, own_width, 1) for w in (w_query, w_key, w_value)]
        return jnp.concatenate(parts + [w_beta_wide], 1)

    w_own, w_oth = columns(c), columns(1 - c)
    w_own_x = swap(w_oth)
    act = ordered(norm_kernel, chunk_of, half_of, inputs, gain_one)
    z = mm(act[:, :half], w_own) + mm(act[:, half:], w_own_x)
    heads, *saved = delta_forward(place_of, z, taps, doc_col, doc_row, gain_row)
    w_out_x, w_gate_x, w_up_x, w_down_x, w_oth_x = swap(w_out), swap(w_gate), swap(w_up), swap(w_down), swap(w_own)
    col = half_of[:1]

    last = groups // 2
    heads_x = swap(heads)
    attended = row_terms(out_product(col, heads, heads_x, w_out, w_out_x, rows, (w_gate_x, w_up_x, w_down_x, w_oth_x)))
    cot = ordered(copy_kernel, chunk_of, half_of, cotangent, ready=attended[:1])
    d_hidden = mm(cot[:mine, :half], w_down, NT) + mm(cot[:mine, half:], w_down_x, NT)
    middle, act_two, x_own = middle_rows(chunk_of, half_of, attended, inputs, gain_two, (d_hidden, cot))

    act_two = row_gather(act_two)
    feeds, act_near, act_far = swiglu(act_two, w_gate, w_gate_x, w_up, w_up_x, d_hidden)
    feeds_x, act_x = swap(feeds), swap(act_far)
    act_pair = [(act_near, 0), (act_x, 0)]
    feed_blocks = feed_product(feeds, w_down, w_down_x, rows)
    gate_grad = grads_of(act_pair, [(feeds, 1), (feeds_x, 1)], [(0,), (1,)], half, feed_blocks[:1])
    gate_got = traded(gate_grad[0], 1)
    d_act_two = row_terms(back([(feeds, 1), (feeds, 2)], [w_gate, w_up], [w_gate_x, w_up_x], rows, mine, gate_grad[:1]))
    up_grad = grads_of(act_pair, [(feeds, 2), (feeds_x, 2)], [(0,), (1,)], half, d_act_two[:1])
    up_got = traded(up_grad[0], 1)
    gate_grad = group_steps(gate_grad, gate_got, up_grad[:1])
    gate_got = traded(gate_grad[0], last)
    d_middle, d_att, feed_part = norm_back(d_act_two, middle, gain_two, cot, gate_grad[:1])

    down_grad = down_weight_grad(low_bit, feeds, feeds_x, cot, half, groups, (d_att,))
    down_got = traded(down_grad[0], 1)
    up_grad = group_steps(up_grad, up_got, down_grad[:1])
    up_got = traded(up_grad[0], last)
    d_heads, d_heads_x, d_att_near, d_att_x = head_grad(
        col, row_gather(d_att), w_out, w_out_x, own_width, (up_grad[0], gate_got)
    )
    d_heads_x, d_att_x = swap(d_heads_x), swap(d_att_x)
    feed_terms = row_terms(feed_blocks)
    dz, d_taps, head_part = delta_backward(
        place_of, d_heads, d_heads_x, z, taps, doc_col, doc_row, gain_row, saved, (d_att_x,)
    )

    dz = hold(dz, (up_got, down_got, *feed_terms))
    dz_x = swap(dz)
    down_grad = group_steps(down_grad, down_got, (dz,))
    down_got = traded(down_grad[0], last)
    d_act = row_terms(back(
        [(dz, 0), (dz_x, 1)], [w_own, w_oth], [w_own_x, w_oth_x], rows, mine, down_grad[:1]
    ))
    act_pair = [(act, 0), (act, 1)]
    grad_own = grads_of(act_pair, [(dz, 0), (dz, 1)], [(0,), (1,)], half, d_act[:1])
    own_got = traded(grad_own[0], 1)
    grad_oth = grads_of(act_pair, [(dz_x, 1), (dz_x, 0)], [(0,), (1,)], half, grad_own[:1])
    out_grad = out_weight_grad(low_bit, heads, heads_x, d_att_near, d_att_x, groups, grad_oth[:1])
    output = sum_rows([middle] + feed_terms, out_grad[:1])
    _, input_grad, mixer_part = norm_back(d_act, x_own, gain_one, d_middle, (output, down_got))

    oth_got = traded(grad_oth[0], 1)
    grad_own = group_steps(grad_own, own_got, (input_grad,))
    own_got = traded(grad_own[0], last)
    out_got = traded(out_grad[0], 1)
    input_grad = row_gather(input_grad)
    input_grad = place(chunk_of, half_of, input_grad, [swap(v) for v in input_grad], grad_own[:1])
    grad_oth = group_steps(grad_oth, oth_got, (input_grad,))
    oth_got = traded(grad_oth[0], last)
    out_grad = group_steps(out_grad, out_got, grad_oth[:1], c)
    out_got = traded(out_grad[0], last)
    output = row_gather(hold(output, (out_grad[0],)))
    output = place(chunk_of, half_of, output, [swap(v) for v in output])
    gate_grad, up_grad, down_grad, out_grad, grad_own, grad_oth = (
        group_end(pair, got)
        for pair, got in (
            (gate_grad, gate_got), (up_grad, up_got), (down_grad, down_got), (out_grad, out_got),
            (grad_own, own_got), (grad_oth, oth_got),
        )
    )

    def projection(start, size):
        a, b = grad_own[:, start:start + size], grad_oth[:, start:start + size]
        return jnp.where(c == 0, jnp.concatenate([a, b], 1), jnp.concatenate([b, a], 1))

    query_grad, key_grad, value_grad = (projection(i * own_width, own_width) for i in range(3))
    beta_grad = (grad_own[:, 3 * own_width:] + grad_oth[:, 3 * own_width:])[:, :w_beta.shape[1]]

    small = jnp.concatenate([own_first(mixer_part[0]), own_first(feed_part[0]), head_part[0]]).reshape(-1, HS)
    small = hold(small, (output,))
    small = small + swap(small)
    k = 1
    while k < rows:
        small = small + to_row(small, k)
        k *= 2
    small = jnp.concatenate([small.reshape(-1), d_taps.reshape(-1)]).reshape(-1, HS)
    k = 1
    while k < groups:
        small = small + lax.ppermute(small, "dp", [(i, i ^ k) for i in range(groups)])
        k *= 2
    small = small.reshape(-1)
    share = width // groups
    mixer_gain_grad = lax.dynamic_slice_in_dim(small, g * share, share)
    feed_gain_grad = lax.dynamic_slice_in_dim(small, width + g * share, share)
    head_gain_grad = small[2 * width:2 * width + HS]
    d_taps = small[2 * width + HS:].reshape(d_taps.shape)
    share = own_width // groups
    conv_grads = [
        lax.dynamic_slice_in_dim(d_taps, i * own_width + g * share, share, 1).T for i in range(3)
    ]
    return (
        output, input_grad, mixer_gain_grad, query_grad, key_grad, value_grad, beta_grad, *conv_grads,
        head_gain_grad, out_grad, feed_gain_grad, gate_grad, up_grad, down_grad,
    )


def solution(mesh):
    weight, swapped = P("col", "row"), P("row", "col")
    taps = P(("row", "col"), None)
    grad, grad_taps = P(("col", "dp"), "row"), P(("row", "col", "dp"), None)
    grad_swapped = P(("row", "dp"), "col")
    tokens = P("dp", None)
    return jax.shard_map(
        body,
        mesh=mesh,
        in_specs=(
            tokens, tokens, P(), weight, weight, weight, weight, taps, taps, taps, P(), swapped, P(), weight, weight,
            swapped, tokens,
        ),
        out_specs=(
            tokens, tokens, P("dp"), grad, grad, grad, grad, grad_taps, grad_taps, grad_taps, P(), grad_swapped, P("dp"),
            grad, grad, grad_swapped,
        ),
        check_vma=False,
    )
```

```python
import functools
import jax
import jax.numpy as jnp
from jax import lax
from jax.experimental import pallas as pl
from jax.experimental.pallas import tpu as pltpu
from jax.sharding import PartitionSpec as P

EPSILON = 1e-06
HEAD_FLOOR = 0.02
CH = 128
HS = 128
F32 = jnp.float32
BF16 = jnp.bfloat16

NN = (((1,), (0,)), ((), ()))
NT = (((1,), (1,)), ((), ()))
TN = (((0,), (0,)), ((), ()))


def dot1(a, b, dims=NN):
    return lax.dot_general(a.astype(BF16), b.astype(BF16), dims, preferred_element_type=F32)


def split(a):
    hi = a.astype(BF16)
    return hi, (a - hi.astype(F32)).astype(BF16)


def dot3s(a, b, dims=NN):
    (ah, al), (bh, bl) = a, b
    ka, kb = dims[0][0][0], dims[0][1][0]
    left = jnp.concatenate([ah, al], ka)
    right = jnp.concatenate([jnp.concatenate([bh, bl], 1 - kb), jnp.concatenate([bh, jnp.zeros_like(bh)], 1 - kb)], kb)
    both = lax.dot_general(left, right, dims, preferred_element_type=F32)
    width = both.shape[1] // 2
    return both[:, :width] + both[:, width:]


def dot3(a, b, dims=NN):
    return dot3s(split(a), split(b), dims)


def silu_parts(z):
    s = 1.0 / (1.0 + jnp.exp(-z))
    return s, z * s


def together(steps):
    steps = list(steps)
    while steps:
        steps = [step for step in steps if next(step, steps) is not steps]


def unit_inverse(low, xor, eye, dot):
    inv = eye - jnp.where(xor < 2, low, 0.0)
    low16 = low.astype(BF16)
    size = 2
    while size < CH:
        part = jnp.where((xor >= size) & (xor < 2 * size), low, 0.0).astype(BF16)
        inv16 = inv.astype(BF16)
        half = dot1(inv16, part)
        yield
        inv = inv - dot1(half, inv16)
        yield
        size *= 2
    parts = split(inv)
    rest = (eye - inv) - dot3s(split(low), parts)
    yield
    return inv + dot3s(parts, split(rest))


def window(ref, c, cols):
    return ref[pl.ds(pl.multiple_of(c * CH, CH), CH + 8), cols]


def conv_chunk(win, taps, masks):
    out = win[8:] * taps[3]
    for j in (1, 2, 3):
        out = out + masks[j - 1] * pltpu.roll(win, j, 0)[8:] * taps[3 - j]
    return out


def chunk_docs(doc_col, doc_row, c):
    col = doc_col[pl.ds(pl.multiple_of(c * CH + 8, 8), CH), :]
    row = doc_row[pl.ds(c, 1), :]
    prev = doc_col[pl.ds(pl.multiple_of(c * CH, 8), 8), :][7:8]
    last = col[CH - 1:CH]
    return col, row, prev, last


def place_rows(place, c):
    return pl.ds(pl.multiple_of(place[c] * CH, CH), CH)


def own_beta(lanes, column, heads, h):
    return jnp.where(column == 0, lanes[:, h:h + 1], lanes[:, heads + h:heads + h + 1])


def fill_pad(pad, place, z_ref, chunks, width):
    pad[0:8] = jnp.zeros((8, 3 * width), F32)
    for c in range(chunks):
        pad[c * CH + 8:(c + 1) * CH + 8] = z_ref[place_rows(place, c), :3 * width]


def fwd_kernel(heads, chunks, dotg, doti, dot,
               place, z_ref, taps_ref, doc_col, doc_row, gain_ref,
               out_ref, mixed_ref, conv_ref, t_ref, h_ref, a_ref, qt_ref, w_ref, u_ref,
               pad, pu_s, b_s):
    width = heads * HS
    fill_pad(pad, place, z_ref, chunks, width)
    row_i = lax.broadcasted_iota(jnp.int32, (CH, CH), 0)
    col_i = lax.broadcasted_iota(jnp.int32, (CH, CH), 1)
    xor = row_i ^ col_i
    eye = (xor == 0).astype(F32)

    def one(c, h):
        col, row, prev, last = chunk_docs(doc_col, doc_row, c)
        same = col == row
        strict = same & (row_i > col_i)
        incl = same & (row_i >= col_i)
        carried = (col == prev).astype(F32)
        closing = (col == last).astype(F32)
        keep = (last == prev).astype(F32)
        dwin = doc_col[pl.ds(pl.multiple_of(c * CH, CH), CH + 8), :]
        masks = [(dwin[8 - j:CH + 8 - j] == col).astype(F32) for j in (1, 2, 3)]

        def conv(which):
            cols = slice(which * width + h * HS, which * width + (h + 1) * HS)
            taps = [taps_ref[t:t + 1, cols] for t in range(4)]
            z = conv_chunk(window(pad, c, cols), taps, masks)
            conv_ref[pl.ds(pl.multiple_of(c * CH, CH), CH), cols] = z
            return silu_parts(z)[1]

        q, k, v = conv(0), conv(1), conv(2)
        k = k * lax.rsqrt(jnp.sum(k * k, axis=1, keepdims=True) + EPSILON)
        beta = 1.0 / (1.0 + jnp.exp(-own_beta(z_ref[place_rows(place, c), 3 * width:], place[chunks], heads, h)))
        yield
        gram = dotg(k, k, NT)
        yield
        low = jnp.where(strict, beta * gram, 0.0)
        yield
        inv = yield from unit_inverse(low, xor, eye, doti)
        yield
        wu = dot(inv, jnp.concatenate([(carried * beta) * k, beta * v], 1))
        w, u = wu[:, :HS], wu[:, HS:]
        yield
        p = jnp.where(incl, dot(q, k, NT), 0.0)
        yield
        wus = split(wu)
        pwu = dot3s(split(p), wus)
        qt = carried * q - pwu[:, :HS]
        pu = pwu[:, HS:]
        yield
        kcl = closing * k
        ab = dot3s(split(kcl), wus, TN)
        a = keep * eye - ab[:, :HS]
        b = ab[:, HS:]
        yield
        i = c * heads + h
        t_ref[i] = inv
        qt_ref[i] = qt
        a_ref[i] = a
        w_ref[i] = w
        u_ref[i] = u
        pu_s[i] = pu
        b_s[i] = b

    per = 4

    def phase_one(g, carry):
        together(one(g * per + e, h) for e in range(per) for h in range(heads))
        return carry

    lax.fori_loop(0, chunks // per, phase_one, 0)

    def phase_two(c, state):
        new = []
        for h in range(heads):
            i = c * heads + h
            h_ref[i] = state[h]
            new.append(dot(a_ref[i], state[h]) + b_s[i])
        return tuple(new)

    lax.fori_loop(0, chunks, phase_two, tuple(jnp.zeros((HS, HS), F32) for _ in range(heads)))

    def phase_three(c, carry):
        for h in range(heads):
            i = c * heads + h
            rows = pl.ds(pl.multiple_of(c * CH, CH), CH)
            cols = slice(h * HS, (h + 1) * HS)
            mixed = dot(qt_ref[i], h_ref[i]) + pu_s[i]
            mixed_ref[rows, cols] = mixed
            r = lax.rsqrt(jnp.mean(mixed * mixed, axis=1, keepdims=True) + HEAD_FLOOR)
            out_ref[place_rows(place, c), cols] = (mixed * r * gain_ref[...]).astype(BF16)
        return carry

    lax.fori_loop(0, chunks, phase_three, 0)


def vm(n):
    return [pl.BlockSpec(memory_space=pltpu.VMEM)] * n


def spent(us):
    return pl.CostEstimate(flops=int(us * 1_150_000_000), bytes_accessed=1000, transcendentals=0)


COST = pl.CostEstimate(flops=1000, bytes_accessed=1000, transcendentals=0)
SMEM = pl.BlockSpec(memory_space=pltpu.SMEM)
ANY = pl.BlockSpec(memory_space=pl.ANY)


def after(kernel, count, extra):
    return lambda *refs: kernel(*refs[:count], *refs[count + extra:])


def delta_forward(place, z, taps, doc_col, doc_row, gain, dots=(dot3, dot3, dot3)):
    tokens, width = z.shape[0], taps.shape[1] // 3
    heads = width // HS
    chunks = tokens // CH
    n = chunks * heads
    sq = jax.ShapeDtypeStruct((n, CH, HS), F32)
    return pl.pallas_call(
        functools.partial(fwd_kernel, heads, chunks, *dots),
        out_shape=(jax.ShapeDtypeStruct((tokens, width), BF16), jax.ShapeDtypeStruct((tokens, width), F32),
                   jax.ShapeDtypeStruct((tokens, 3 * width), F32), sq, sq, sq, sq, sq, sq),
        in_specs=[SMEM] + vm(5), out_specs=tuple(vm(9)),
        scratch_shapes=[pltpu.VMEM((tokens + 8, 3 * width), F32), pltpu.VMEM((n, CH, HS), F32), pltpu.VMEM((n, CH, HS), F32)],
        compiler_params=pltpu.CompilerParams(vmem_limit_bytes=48 * 1024 * 1024),
        cost_estimate=COST,
        name="delta_forward",
    )(place, z, taps, doc_col, doc_row, gain)


def bwd_kernel(heads, chunks, dotg, dot,
               place, dh_own, dh_other, z_ref, taps_ref, doc_col, doc_row, gain_ref,
               mixed_ref, conv_ref, t_ref, h_ref, a_ref, qt_ref, w_ref, u_ref,
               dz_own, dz_other, dtaps_ref, dgain_ref,
               dz_ref, dh_ref, do_s, eb_s, e_s, dc_s, db_s):
    width = heads * HS
    tokens = chunks * CH
    dh_ref[:tokens // 2] = dh_own[...]
    dh_ref[tokens // 2:] = dh_other[...]
    dc_s[tokens:] = jnp.zeros((8, 3 * width), F32)
    row_i = lax.broadcasted_iota(jnp.int32, (CH, CH), 0)
    col_i = lax.broadcasted_iota(jnp.int32, (CH, CH), 1)

    def rows_of(c):
        return pl.ds(pl.multiple_of(c * CH, CH), CH)

    def phase_one(c, total):
        for h in range(heads):
            i = c * heads + h
            cols = slice(h * HS, (h + 1) * HS)
            m = mixed_ref[rows_of(c), cols]
            dy = dh_ref[place_rows(place, c), cols].astype(F32)
            r = lax.rsqrt(jnp.mean(m * m, axis=1, keepdims=True) + HEAD_FLOOR)
            mr = m * r
            total = total + jnp.sum(dy * mr, axis=0, keepdims=True)
            gy = gain_ref[...] * dy
            dm = r * (gy - mr * jnp.mean(mr * gy, axis=1, keepdims=True))
            do_s[i] = dm
            eb_s[i] = dot(qt_ref[i], dm, TN)
        return total

    dgain_ref[...] = lax.fori_loop(0, chunks, phase_one, jnp.zeros((1, HS), F32))

    def phase_two(n, state):
        c = chunks - 1 - n
        new = []
        for h in range(heads):
            i = c * heads + h
            e_s[i] = state[h]
            new.append(dot(a_ref[i], state[h], TN) + eb_s[i])
        return tuple(new)

    lax.fori_loop(0, chunks, phase_two, tuple(jnp.zeros((HS, HS), F32) for _ in range(heads)))

    def one(c, h):
        i = c * heads + h
        col, row, prev, last = chunk_docs(doc_col, doc_row, c)
        same = col == row
        strict = same & (row_i > col_i)
        incl = same & (row_i >= col_i)
        carried = (col == prev).astype(F32)
        closing = (col == last).astype(F32)

        def conv(which):
            s, y = silu_parts(conv_ref[rows_of(c), which * width + h * HS:which * width + (h + 1) * HS])
            return y, s + y * (1.0 - s)

        q, q_slope = conv(0)
        k, k_slope = conv(1)
        v, v_slope = conv(2)
        n = lax.rsqrt(jnp.sum(k * k, axis=1, keepdims=True) + EPSILON)
        k = k * n
        beta = 1.0 / (1.0 + jnp.exp(-own_beta(z_ref[place_rows(place, c), 3 * width:], place[chunks], heads, h)))
        inv, state, w, u, dm, e = t_ref[i], h_ref[i], w_ref[i], u_ref[i], do_s[i], e_s[i]
        yield
        gram = dotg(k, k, NT)
        yield
        p = jnp.where(incl, dot(q, k, NT), 0.0)
        yield
        r = u - dot(w, state)
        yield
        y = v - carried * dot(k, state)
        yield
        dr = dot(p, dm, TN) + closing * dot(k, e)
        yield
        x = dot(inv, dr, TN)
        yield
        dp = jnp.where(incl, dot(dm, r, NT), 0.0)
        yield
        dq = dot(dp, k) + carried * dot(dm, state, NT)
        yield
        dlow = jnp.where(strict, -dot(x, r, NT), 0.0)
        dgram = beta * dlow
        yield
        dk = closing * dot(r, e, NT) + dot(dp, q, TN)
        yield
        dk = dk + dot(dgram, k) + dot(dgram, k, TN)
        yield
        dk = dk - (carried * beta) * dot(x, state, NT)
        yield
        dbeta = jnp.sum(dlow * gram, axis=1, keepdims=True) + jnp.sum(x * y, axis=1, keepdims=True)
        dk = n * (dk - k * jnp.sum(k * dk, axis=1, keepdims=True))
        for which, value in ((0, dq * q_slope), (1, dk * k_slope), (2, beta * x * v_slope)):
            dc_s[rows_of(c), which * width + h * HS:which * width + (h + 1) * HS] = value
        db_s[h, rows_of(c)] = dbeta * beta * (1.0 - beta)

    per = 4

    def phase_three(g, carry):
        together(one(g * per + e, h) for e in range(per) for h in range(heads))
        return carry

    lax.fori_loop(0, chunks // per, phase_three, 0)

    def phase_four(c, sums):
        col = doc_col[pl.ds(pl.multiple_of(c * CH + 8, 8), CH), :]
        after = doc_col[pl.ds(pl.multiple_of(c * CH + 8, 8), CH + 8), :]
        later = [jnp.broadcast_to((after[j:CH + j] == col).astype(F32), (CH, HS)) for j in (1, 2, 3)]
        new = []
        for b in range(3 * heads):
            cols = slice(b * HS, (b + 1) * HS)
            z = z_ref[place_rows(place, c), cols]
            win = dc_s[pl.ds(pl.multiple_of(c * CH, CH), CH + 8), cols]
            dz = 0.0
            for j in range(4):
                d = win[:CH] if j == 0 else later[j - 1] * pltpu.roll(win, CH + 8 - j, 0)[:CH]
                dz = dz + d * taps_ref[3 - j:4 - j, cols]
                new.append(sums[4 * b + j] + jnp.sum((d * z).reshape(CH // 8, 8, HS), axis=0))
            dz_ref[place_rows(place, c), cols] = dz.astype(BF16)
        lane = lax.broadcasted_iota(jnp.int32, (CH, HS), 1) - place[chunks] * heads
        betas = sum(jnp.where(lane == h, db_s[h, rows_of(c)], 0.0) for h in range(heads))
        dz_ref[place_rows(place, c), 3 * width:] = betas.astype(BF16)
        return tuple(new)

    sums = lax.fori_loop(0, chunks, phase_four, tuple(jnp.zeros((8, HS), F32) for _ in range(12 * heads)))
    for b in range(3 * heads):
        for j in range(4):
            dtaps_ref[3 - j:4 - j, b * HS:(b + 1) * HS] = jnp.sum(sums[4 * b + j], axis=0, keepdims=True)
    dz_own[...] = dz_ref[:tokens // 2]
    dz_other[...] = dz_ref[tokens // 2:]


def delta_backward(place, own, other, z, taps, doc_col, doc_row, gain, saved, ready=(), dots=(dot3, dot3)):
    tokens, width = z.shape[0], taps.shape[1] // 3
    heads = width // HS
    chunks = tokens // CH
    n = chunks * heads
    sq = pltpu.VMEM((n, CH, HS), F32)
    return pl.pallas_call(
        after(functools.partial(bwd_kernel, heads, chunks, *dots), 16, len(ready)),
        out_shape=(jax.ShapeDtypeStruct((tokens // 2, z.shape[1]), BF16), jax.ShapeDtypeStruct((tokens // 2, z.shape[1]), BF16),
                   jax.ShapeDtypeStruct((4, 3 * width), F32),
                   jax.ShapeDtypeStruct((1, HS), F32)),
        in_specs=[SMEM] + vm(15) + [ANY] * len(ready), out_specs=tuple(vm(4)),
        scratch_shapes=[pltpu.VMEM(z.shape, BF16), pltpu.VMEM((tokens, width), BF16), sq, sq, sq, pltpu.VMEM((tokens + 8, 3 * width), F32),
                        pltpu.VMEM((heads, tokens, 1), F32)],
        compiler_params=pltpu.CompilerParams(vmem_limit_bytes=48 * 1024 * 1024),
        cost_estimate=COST,
        name="delta_backward",
    )(place, own, other, z, taps, doc_col, doc_row, gain, *saved, *ready)


def norm_kernel(chunk_of, half_of, a_ref, b_ref, gain_ref, out_ref):
    half = a_ref.shape[1]
    a, b = a_ref[...].astype(F32), b_ref[...].astype(F32)
    total = jnp.sum(a * a, axis=1, keepdims=True) + jnp.sum(b * b, axis=1, keepdims=True)
    r = lax.rsqrt(total / (2 * half) + EPSILON)
    out_ref[:, :half] = (a * r * gain_ref[:, :half]).astype(BF16)
    out_ref[:, half:] = (b * r * gain_ref[:, half:]).astype(BF16)


def copy_kernel(chunk_of, half_of, a_ref, b_ref, out_ref):
    half = a_ref.shape[1]
    out_ref[:, :half] = a_ref[...]
    out_ref[:, half:] = b_ref[...]


def ordered(kernel, chunk_of, half_of, x, *rest, ready=()):
    tokens, width = x.shape
    half = width // 2
    return pl.pallas_call(
        after(kernel, 4 + len(rest), len(ready)),
        grid_spec=pltpu.PrefetchScalarGridSpec(
            num_scalar_prefetch=2,
            grid=(tokens // CH,),
            in_specs=[
                pl.BlockSpec((CH, half), lambda p, ch, hf: (ch[p], hf[0])),
                pl.BlockSpec((CH, half), lambda p, ch, hf: (ch[p], hf[1])),
            ] + [pl.BlockSpec((1, width), lambda p, ch, hf: (0, 0)) for _ in rest] + [ANY] * len(ready),
            out_specs=pl.BlockSpec((CH, width), lambda p, ch, hf: (p, 0)),
        ),
        out_shape=jax.ShapeDtypeStruct((tokens, width), BF16),
        compiler_params=pltpu.CompilerParams(vmem_limit_bytes=32 * 1024 * 1024),
        cost_estimate=COST,
        name="ordered_rows",
    )(chunk_of, half_of, x, x, *rest, *ready)


def place_kernel(count, chunk_of, half_of, *refs):
    out, token = refs[2 * count:]
    half = out.shape[1] // 2
    token[...] = jnp.zeros_like(token)
    for p in range(2 * count):

        @pl.when(pl.program_id(0) == p)
        def _(p=p):
            for h in range(2):
                to = half_of[h] if p < count else half_of[1 - h]
                out[:, pl.ds(pl.multiple_of(to * half, half), half)] = refs[p][:, h * half:(h + 1) * half]


def place(chunk_of, half_of, own, partner, ready=()):
    count = len(own)
    rows, width = CH, own[0].shape[1]
    return pl.pallas_call(
        after(functools.partial(place_kernel, count), 2 + 2 * count, len(ready)),
        grid_spec=pltpu.PrefetchScalarGridSpec(
            num_scalar_prefetch=2,
            grid=(2 * count,),
            in_specs=[pl.BlockSpec((rows, width), lambda p, ch, hf: (0, 0)) for _ in range(2 * count)] + [ANY] * len(ready),
            out_specs=(
                pl.BlockSpec((rows, width), lambda p, ch, hf: (ch[p], 0)), pl.BlockSpec((8, HS), lambda p, ch, hf: (0, 0)),
            ),
        ),
        out_shape=(
            jax.ShapeDtypeStruct((2 * count * rows, width), own[0].dtype), jax.ShapeDtypeStruct((8, HS), F32),
        ),
        compiler_params=pltpu.CompilerParams(vmem_limit_bytes=32 * 1024 * 1024),
        cost_estimate=COST,
        name="place_rows",
    )(chunk_of, half_of, *own, *partner, *ready)


BIG = pltpu.CompilerParams(vmem_limit_bytes=32 * 1024 * 1024)


def swiglu_kernel(rows, *refs):
    acts, (wg, wgx, wu, wux, dh, d_gate, out, act_near, act_far) = refs[:rows], refs[rows:]
    half = wg.shape[0]
    near = jnp.concatenate([wg[...], wu[...]], 1)
    far = jnp.concatenate([wgx[...], wux[...]], 1)
    cut = wg.shape[1]
    size = acts[0].shape[0]

    @pl.when(pl.program_id(0) == 0)
    def _():
        for k in range(rows):
            act_near[k * size:(k + 1) * size] = acts[k][:, :half]
            act_far[k * size:(k + 1) * size] = acts[k][:, half:]

    for k in range(rows):
        both = dot1(acts[k][:, :half], near) + dot1(acts[k][:, half:], far)
        gate, up, dhk = both[:, :cut], both[:, cut:], dh[k * size:(k + 1) * size].astype(F32)
        s = 1.0 / (1.0 + jnp.exp(-gate))
        gs = gate * s
        d_gate[k * size:(k + 1) * size] = (dhk * up * (s + gs * (1.0 - s))).astype(BF16)
        for i, v in enumerate((gs * up, dhk * gs)):
            out[(i * rows + k) * size:(i * rows + k + 1) * size] = v.astype(BF16)


def swiglu(acts, w_gate, w_gate_x, w_up, w_up_x, d_hidden):
    rows = len(acts)
    size, width = acts[0].shape
    half, feed = w_gate.shape
    tile = 128
    tokens = rows * size
    weight = pl.BlockSpec((half, tile), lambda n: (0, n))
    return pl.pallas_call(
        functools.partial(swiglu_kernel, rows),
        grid=(feed // tile,),
        in_specs=[pl.BlockSpec((size, width), lambda n: (0, 0))] * rows + [weight] * 4
        + [pl.BlockSpec((tokens, tile), lambda n: (0, n))],
        out_specs=(pl.BlockSpec((tokens, tile), lambda n: (0, n)), pl.BlockSpec((2 * tokens, tile), lambda n: (0, n)))
        + (pl.BlockSpec((tokens, half), lambda n: (0, 0)),) * 2,
        out_shape=(jax.ShapeDtypeStruct((tokens, feed), BF16), jax.ShapeDtypeStruct((2 * tokens, feed), BF16))
        + (jax.ShapeDtypeStruct((tokens, half), BF16), jax.ShapeDtypeStruct((tokens, half), BF16)),
        compiler_params=BIG,
        cost_estimate=COST,
        name="swiglu",
    )(*acts, w_gate, w_gate_x, w_up, w_up_x, d_hidden)


def back_kernel(count, parts, *refs):
    lefts, near, far = refs[:count], refs[count:2 * count], refs[2 * count:3 * count]
    outs = refs[3 * count:]

    def store(weights):
        both = sum(dot1(left[...], w[...], NT) for left, w in zip(lefts, weights))
        size = both.shape[0] // parts
        for k in range(parts):
            outs[k][...] = both[k * size:(k + 1) * size].astype(outs[k].dtype)

    steps = pl.num_programs(0) // 2
    pl.when(pl.program_id(0) < steps)(lambda: store(near))
    pl.when(pl.program_id(0) >= steps)(lambda: store(far))


def back(lefts, near, far, parts, tokens, ready=()):
    count = len(lefts)
    half = near[0].shape[0]
    tile = 512
    steps = half // tile
    size = tokens // parts
    return pl.pallas_call(
        after(functools.partial(back_kernel, count, parts), 3 * count, len(ready)),
        grid=(2 * steps,),
        in_specs=[pl.BlockSpec((tokens, v.shape[1]), lambda n, i=i: (i, 0)) for v, i in lefts]
        + [pl.BlockSpec((tile, w.shape[1]), lambda n: (jnp.minimum(n, steps - 1), 0)) for w in near]
        + [pl.BlockSpec((tile, w.shape[1]), lambda n: (jnp.maximum(n - steps, 0), 0)) for w in far] + [ANY] * len(ready),
        out_specs=tuple(pl.BlockSpec((size, tile), lambda n: (0, n)) for _ in range(parts)),
        out_shape=tuple(jax.ShapeDtypeStruct((size, 2 * half), F32) if k == 0 else jax.ShapeDtypeStruct((size, 2 * half), BF16) for k in range(parts)),
        compiler_params=BIG,
        cost_estimate=COST,
        name="back_product",
    )(*[v for v, _ in lefts], *near, *far, *ready)


def grad_kernel(pairs, bit, *refs):
    lefts, rights = refs[:len(pairs)], refs[len(pairs):-2]
    send, keep = refs[-2:]
    out = jnp.concatenate([
        sum(lax.dot_general(lefts[i][...], rights[j][...], TN, preferred_element_type=F32) for i, j in group)
        for group in zip(*[[(i, j) for j in js] for i, js in enumerate(pairs)])
    ], 1).astype(BF16)
    steps = pl.num_programs(0) // 2

    @pl.when(pl.program_id(0) < steps)
    def _():
        send[0] = out

    @pl.when(pl.program_id(0) >= steps)
    def _():
        keep[0] = out


def weight_grad(bit, lefts, rights, pairs, tokens, columns, shards, ready=()):
    rows = columns // shards
    wide = sum(rights[j][0].shape[1] for j in pairs[0])
    half = shards // 2

    def shard(n, b):
        return (n % half) * 2 + jnp.where(n < half, 1 - b[0], b[0])

    shape = jax.ShapeDtypeStruct((half, rows, wide), BF16)
    return pl.pallas_call(
        after(functools.partial(grad_kernel, pairs), 1 + len(lefts) + len(rights), len(ready)),
        grid_spec=pltpu.PrefetchScalarGridSpec(
            num_scalar_prefetch=1,
            grid=(shards,),
            in_specs=[pl.BlockSpec((tokens, rows), lambda n, b, i=i: (i, shard(n, b))) for _, i in lefts]
            + [pl.BlockSpec((tokens, v.shape[1]), lambda n, b, i=i: (i, 0)) for v, i in rights] + [ANY] * len(ready),
            out_specs=(
                pl.BlockSpec((1, rows, wide), lambda n, b: (jnp.minimum(n, half - 1), 0, 0)),
                pl.BlockSpec((1, rows, wide), lambda n, b: (jnp.maximum(n - half, 0), 0, 0)),
            ),
        ),
        out_shape=(jax.ShapeDtypeStruct(shape.shape, BF16), shape),
        compiler_params=BIG,
        cost_estimate=COST,
        name="weight_grad",
    )(bit, *[v for v, _ in lefts], *[v for v, _ in rights], *ready)


def out_kernel(col, own, other, near, far, *outs):
    first, width = col[0], own.shape[1]
    left = jnp.concatenate([own[...], other[...]], 1)
    half = near.shape[1]
    for h, w in enumerate((near, far)):
        right = jnp.concatenate([w[pl.ds(pl.multiple_of(i * width, width), width)] for i in (first, 1 - first)], 0)
        both = dot1(left, right)
        size = outs[0].shape[0]
        for k, out in enumerate(outs):
            out[:, h * half:(h + 1) * half] = both[k * size:(k + 1) * size].astype(out.dtype)


def out_product(col, heads, other, w_out, w_out_x, parts, ready=()):
    tokens, width = other.shape[0] // 2, other.shape[1]
    half = w_out.shape[1]
    size = tokens // parts
    full = lambda v: pl.BlockSpec(v.shape, lambda n, c: (0, 0))
    return pl.pallas_call(
        after(out_kernel, 5, len(ready)),
        grid_spec=pltpu.PrefetchScalarGridSpec(
            num_scalar_prefetch=1,
            grid=(1,),
            in_specs=[
                pl.BlockSpec((tokens, width), lambda n, c: (0, 0)), pl.BlockSpec((tokens, width), lambda n, c: (1, 0)),
                full(w_out), full(w_out_x),
            ] + [ANY] * len(ready),
            out_specs=tuple(pl.BlockSpec((size, 2 * half), lambda n, c: (0, 0)) for _ in range(parts)),
        ),
        out_shape=tuple(jax.ShapeDtypeStruct((size, 2 * half), F32) if k == 0 else jax.ShapeDtypeStruct((size, 2 * half), BF16) for k in range(parts)),
        compiler_params=BIG,
        cost_estimate=COST,
        name="out_product",
    )(col, heads, other, w_out, w_out_x, *ready)


def head_grad_kernel(parts, col, *refs):
    grads, (near, far, own, other, near_out, far_out) = refs[:parts], refs[parts:]
    width, half = own.shape[1], near.shape[1]
    size = grads[0].shape[0]
    for k in range(parts):
        near_out[k * size:(k + 1) * size] = grads[k][:, :half]
        far_out[k * size:(k + 1) * size] = grads[k][:, half:]
    for i, out in ((col[0], own), (1 - col[0], other)):
        rows = pl.ds(pl.multiple_of(i * width, width), width)
        right = jnp.concatenate([near[rows], far[rows]], 1)
        for k in range(parts):
            out[k * size:(k + 1) * size] = dot1(grads[k][...], right, NT).astype(BF16)


def head_grad(col, grads, w_out, w_out_x, width, ready=()):
    parts, size = len(grads), grads[0].shape[0]
    shape = jax.ShapeDtypeStruct((parts * size, width), BF16)
    shape_two = jax.ShapeDtypeStruct((parts * size, w_out.shape[1]), BF16)
    return pl.pallas_call(
        after(functools.partial(head_grad_kernel, parts), parts + 3, len(ready)),
        in_specs=[SMEM] + vm(parts + 2) + [ANY] * len(ready),
        out_specs=tuple(vm(4)),
        out_shape=(shape, jax.ShapeDtypeStruct(shape.shape, BF16), shape_two, jax.ShapeDtypeStruct(shape_two.shape, BF16)),
        compiler_params=BIG,
        cost_estimate=COST,
        name="head_grad",
    )(col, *grads, w_out, w_out_x, *ready)


def middle_kernel(count, chunk_of, half_of, *refs):
    terms, (a, b, gain, middle, act, own) = refs[:count], refs[count:]
    own[...] = jnp.concatenate([a[...], b[...]], 1)
    total = own[...].astype(F32)
    for term in terms:
        total = total + term[...].astype(F32)
    middle[...] = total
    act[...] = (total * lax.rsqrt(jnp.mean(total * total, axis=1, keepdims=True) + EPSILON) * gain[...]).astype(BF16)


def middle_rows(chunk_of, half_of, terms, x, gain, ready=()):
    count = len(terms)
    rows, width = terms[0].shape
    steps, rows = 4, rows // 4
    whole = pl.BlockSpec((rows, width), lambda n, ch, hf: (n, 0))
    return pl.pallas_call(
        after(functools.partial(middle_kernel, count), count + 5, len(ready)),
        grid_spec=pltpu.PrefetchScalarGridSpec(
            num_scalar_prefetch=2,
            grid=(steps,),
            in_specs=[whole] * count + [
                pl.BlockSpec((rows, width // 2), lambda n, ch, hf: (ch[0] * steps + n, hf[0])),
                pl.BlockSpec((rows, width // 2), lambda n, ch, hf: (ch[0] * steps + n, hf[1])),
                pl.BlockSpec((1, width), lambda n, ch, hf: (0, 0)),
            ] + [ANY] * len(ready),
            out_specs=(whole, whole, whole),
        ),
        out_shape=(
            jax.ShapeDtypeStruct((steps * rows, width), F32), jax.ShapeDtypeStruct((steps * rows, width), BF16),
            jax.ShapeDtypeStruct((steps * rows, width), BF16),
        ),
        compiler_params=BIG,
        cost_estimate=COST,
        name="middle_rows",
    )(chunk_of, half_of, *terms, x, x, gain, *ready)


def norm_back_kernel(count, *refs):
    terms, (values, gain, upstream, total, low, part) = refs[:count], refs[count:]
    grads = terms[0][...]
    for term in terms[1:]:
        grads = grads + term[...].astype(F32)
    v = values[...].astype(F32)
    r = lax.rsqrt(jnp.mean(v * v, axis=1, keepdims=True) + EPSILON)
    normal = v * r
    scaled = gain[...] * grads
    out = upstream[...].astype(F32) + r * (scaled - normal * jnp.mean(normal * scaled, axis=1, keepdims=True))
    total[...] = out
    low[...] = out.astype(BF16)

    @pl.when(pl.program_id(0) == 0)
    def _():
        part[...] = jnp.zeros_like(part)

    part[...] += jnp.sum(grads * normal, axis=0, keepdims=True)


def norm_back(terms, values, gain, upstream, ready=(), cost=COST):
    count = len(terms)
    rows, width = values.shape
    steps = 4
    whole = pl.BlockSpec((rows // steps, width), lambda n: (n, 0))
    row = pl.BlockSpec((1, width), lambda n: (0, 0))
    return pl.pallas_call(
        after(functools.partial(norm_back_kernel, count), count + 3, len(ready)),
        grid=(steps,),
        in_specs=[whole] * (count + 1) + [row, whole] + [ANY] * len(ready),
        out_specs=(whole, whole, row),
        out_shape=(
            jax.ShapeDtypeStruct((rows, width), F32), jax.ShapeDtypeStruct((rows, width), BF16),
            jax.ShapeDtypeStruct((1, width), F32),
        ),
        compiler_params=BIG,
        cost_estimate=cost,
        name="norm_back",
    )(*terms, values, gain, upstream, *ready)


def split_rows(bit, value, send, keep):
    rows = send.shape[1]
    for j in range(2 * send.shape[0]):
        part = value[j * rows:(j + 1) * rows].astype(BF16)
        for to, same in ((send, False), (keep, True)):

            @pl.when((bit == j % 2) == same)
            def _(to=to, j=j, part=part):
                to[j // 2] = part


def down_kernel(bit, hidden, hidden_x, cot, cot_x, send, keep):
    split_rows(bit[0], dot1(hidden[...], cot[...], TN) + dot1(hidden_x[...], cot_x[...], TN), send, keep)


def down_weight_grad(bit, hidden, hidden_x, cot, half, shards, ready=()):
    tokens, feed = hidden.shape[0] // 2, hidden.shape[1]
    tile = 512
    shape = jax.ShapeDtypeStruct((shards // 2, feed // shards, half), BF16)
    out = pl.BlockSpec((shards // 2, feed // shards, tile), lambda n, b: (0, 0, n))
    return pl.pallas_call(
        after(down_kernel, 5, len(ready)),
        grid_spec=pltpu.PrefetchScalarGridSpec(
            num_scalar_prefetch=1,
            grid=(half // tile,),
            in_specs=[
                pl.BlockSpec((tokens, feed), lambda n, b: (0, 0)),
                pl.BlockSpec((tokens, feed), lambda n, b: (0, 0)),
                pl.BlockSpec((tokens, tile), lambda n, b: (0, n)),
                pl.BlockSpec((tokens, tile), lambda n, b: (1, n)),
            ] + [ANY] * len(ready),
            out_specs=(out, out),
        ),
        out_shape=(jax.ShapeDtypeStruct(shape.shape, BF16), shape),
        compiler_params=BIG,
        cost_estimate=COST,
        name="down_weight_grad",
    )(bit, hidden, hidden_x, cot, cot, *ready)


def blocks_of(v):
    return jnp.concatenate([v[:, j:j + HS] for j in range(0, v.shape[1], HS)], 0)


def other_grad_kernel(flip, bit, act, act_far, dz, dz_far, heads, other, grads, grads_x, send, keep, rows_out):
    steps = pl.num_programs(0)
    tokens = grads.shape[0]

    @pl.when(pl.program_id(0) == 0)
    def _():
        g, gx = grads[...], grads_x[...]
        own = dot1(heads[:tokens], g, TN) + dot1(heads[tokens:], gx, TN)
        away = dot1(other[tokens:], g, TN) + dot1(other[:tokens], gx, TN)
        rows_out[...] = jnp.concatenate([own, away], 0).astype(BF16)

    n = pl.program_id(0)
    half = steps // 2
    shard = (n % half) * 2 + jnp.where(n < half, 1 - bit[0], bit[0])
    size = rows_out.shape[0] // steps
    place = (shard + flip[0] * half) % steps
    part = rows_out[pl.ds(pl.multiple_of(place * size, size), size)]
    value = (dot1(act[...], dz[...], TN) + dot1(act_far[...], dz_far[...], TN)).astype(BF16)
    value = jnp.concatenate([blocks_of(value), blocks_of(part)], 0)
    pl.when(n < half)(lambda: send.__setitem__(0, value))
    pl.when(n >= half)(lambda: keep.__setitem__(0, value))


def other_grads(flip, bit, act, dz, dz_far, heads, other, grads, grads_x, columns, shards, ready=()):
    tokens, wide = dz.shape
    rows, half = columns // shards, shards // 2
    out_rows, out_wide = 2 * heads.shape[1], grads.shape[1]
    deep = rows * (wide // HS) + out_rows // shards * (out_wide // HS)

    def shard(n, b):
        return (n % half) * 2 + jnp.where(n < half, 1 - b[0], b[0])

    whole = lambda v: pl.BlockSpec(v.shape, lambda n, f, b: (0, 0))
    shape = jax.ShapeDtypeStruct((half, deep, HS), BF16)
    return pl.pallas_call(
        after(other_grad_kernel, 10, len(ready)),
        grid_spec=pltpu.PrefetchScalarGridSpec(
            num_scalar_prefetch=2,
            grid=(shards,),
            in_specs=[pl.BlockSpec((tokens, rows), lambda n, f, b, i=i: (i, shard(n, b))) for i in range(2)]
            + [whole(v) for v in (dz, dz_far, heads, other, grads, grads_x)] + [ANY] * len(ready),
            out_specs=(
                pl.BlockSpec((1, deep, HS), lambda n, f, b: (jnp.minimum(n, half - 1), 0, 0)),
                pl.BlockSpec((1, deep, HS), lambda n, f, b: (jnp.maximum(n - half, 0), 0, 0)),
            ),
            scratch_shapes=[pltpu.VMEM((out_rows, out_wide), BF16)],
        ),
        out_shape=(jax.ShapeDtypeStruct(shape.shape, BF16), shape),
        compiler_params=BIG,
        cost_estimate=COST,
        name="other_grads",
    )(flip, bit, act, act, dz, dz_far, heads, other, grads, grads_x, *ready)


def feed_kernel(parts, hidden, near, far, keep, send):
    size = hidden.shape[0] // parts

    def store(w):
        both = dot1(hidden[...], w[...])
        for k in range(0, parts, 2):
            keep[k // 2 * size:(k // 2 + 1) * size] = both[k * size:(k + 1) * size]
            send[k // 2 * size:(k // 2 + 1) * size] = both[(k + 1) * size:(k + 2) * size].astype(BF16)

    pl.when(pl.program_id(0) == 0)(lambda: store(near))
    pl.when(pl.program_id(0) == 1)(lambda: store(far))


def feed_product(hidden, near, far, parts, ready=()):
    tokens, half = hidden.shape[0] // 2, near.shape[1]
    whole = lambda v: pl.BlockSpec(v.shape, lambda n: (0, 0))
    return pl.pallas_call(
        after(functools.partial(feed_kernel, parts), 3, len(ready)),
        grid=(2,),
        in_specs=[pl.BlockSpec((tokens, hidden.shape[1]), lambda n: (0, 0)), whole(near), whole(far)] + [ANY] * len(ready),
        out_specs=(pl.BlockSpec((tokens // 2, half), lambda n: (0, n)),) * 2,
        out_shape=(jax.ShapeDtypeStruct((tokens // 2, 2 * half), F32), jax.ShapeDtypeStruct((tokens // 2, 2 * half), BF16)),
        compiler_params=BIG,
        cost_estimate=COST,
        name="feed_product",
    )(hidden, near, far, *ready)


def pair_kernel(kept, got, keep, send):
    size = keep.shape[0]
    keep[...] = kept[:size] + got[:size].astype(F32)
    send[...] = (kept[size:] + got[size:].astype(F32)).astype(BF16)


def pair_rows(kept, got, ready=()):
    rows, width = kept.shape
    return pl.pallas_call(
        after(pair_kernel, 2, len(ready)),
        in_specs=vm(2) + [ANY] * len(ready),
        out_specs=tuple(vm(2)),
        out_shape=(jax.ShapeDtypeStruct((rows // 2, width), F32), jax.ShapeDtypeStruct((rows // 2, width), BF16)),
        compiler_params=BIG,
        cost_estimate=COST,
        name="pair_rows",
    )(kept, got, *ready)


def split_row(v):
    hi = v.astype(BF16).astype(F32)
    return jnp.concatenate([hi, v - hi], 0)


def last_norm_kernel(count, *refs):
    terms, (values, gain, upstream, feed_part, head_part, out) = refs[:count], refs[count:]
    grads = terms[0][...]
    for term in terms[1:]:
        grads = grads + term[...].astype(F32)
    v = values[...].astype(F32)
    r = lax.rsqrt(jnp.mean(v * v, axis=1, keepdims=True) + EPSILON)
    normal = v * r
    scaled = gain[...] * grads
    rows, width = v.shape
    out[:rows] = (upstream[...] + r * (scaled - normal * jnp.mean(normal * scaled, axis=1, keepdims=True))).astype(BF16)
    part = jnp.sum(grads * normal, axis=0, keepdims=True)
    head = jnp.concatenate([head_part[...], jnp.zeros((1, width - HS), F32)], 1)
    extra = [split_row(part), split_row(feed_part[...]), split_row(head), jnp.zeros((10, width), F32)]
    out[rows:] = jnp.concatenate(extra, 0).astype(BF16)


def last_norm_back(terms, values, gain, upstream, feed_part, head_part, ready=()):
    count = len(terms)
    rows, width = values.shape
    return pl.pallas_call(
        after(functools.partial(last_norm_kernel, count), count + 5, len(ready)),
        in_specs=vm(count + 5) + [ANY] * len(ready),
        out_specs=vm(1)[0],
        out_shape=jax.ShapeDtypeStruct((rows + 16, width), BF16),
        compiler_params=BIG,
        cost_estimate=spent(4),
        name="last_norm_back",
    )(*terms, values, gain, upstream, feed_part, head_part, *ready)


def total_kernel(half_of, *refs):
    pieces, out = refs[:-1], refs[-1]
    half = out.shape[1] // 2
    count = len(pieces) // 2
    for h in range(2):
        own = sum(ref[...].astype(F32)[:, h * half:(h + 1) * half] for ref in pieces[:count])
        oth = sum(ref[...].astype(F32)[:, (1 - h) * half:(2 - h) * half] for ref in pieces[count:])
        total = own + oth
        out[:, pl.ds(pl.multiple_of(half_of[h] * half, half), half)] = jnp.concatenate(
            [total[n:n + 1] + total[n + 1:n + 2] for n in (0, 2)] + [jnp.zeros((6, half), F32)], 0)
    heads = sum(ref[...].astype(F32)[4:6, :HS] for ref in pieces)
    out[2:3, :HS] = heads[0:1] + heads[1:2]


def totals(half_of, own, partner):
    rows, width = own[0].shape
    at = (rows - 16) // 16
    return pl.pallas_call(
        total_kernel,
        grid_spec=pltpu.PrefetchScalarGridSpec(
            num_scalar_prefetch=1,
            grid=(1,),
            in_specs=[pl.BlockSpec((16, width), lambda n, hf: (at, 0))] * (2 * len(own)),
            out_specs=pl.BlockSpec((8, width), lambda n, hf: (0, 0)),
        ),
        out_shape=jax.ShapeDtypeStruct((8, width), F32),
        compiler_params=BIG,
        cost_estimate=COST,
        name="totals",
    )(half_of, *own, *partner)


def sum_kernel(*refs):
    total = refs[0][...]
    for ref in refs[1:-1]:
        total = total + ref[...].astype(F32)
    refs[-1][...] = total.astype(BF16)


def sum_rows(terms, ready=()):
    return pl.pallas_call(
        after(sum_kernel, len(terms), len(ready)),
        in_specs=vm(len(terms)) + [ANY] * len(ready),
        out_specs=vm(1)[0],
        out_shape=jax.ShapeDtypeStruct(terms[0].shape, BF16),
        compiler_params=BIG,
        cost_estimate=COST,
        name="sum_rows",
    )(*terms, *ready)


def halve_kernel(bit, kept, got, send, keep):
    for out, i in ((send, 1 - bit[0]), (keep, bit[0])):
        out[...] = (kept[pl.ds(i, 1)].astype(F32) + got[pl.ds(i, 1)].astype(F32)).astype(BF16)


def halve(bit, kept, got, ready=()):
    shards, rows, columns = kept.shape
    pair = pl.BlockSpec((2, rows, columns), lambda n, b: (n, 0, 0))
    one = pl.BlockSpec((1, rows, columns), lambda n, b: (n, 0, 0))
    shape = jax.ShapeDtypeStruct((shards // 2, rows, columns), BF16)
    return pl.pallas_call(
        after(halve_kernel, 3, len(ready)),
        grid_spec=pltpu.PrefetchScalarGridSpec(
            num_scalar_prefetch=1, grid=(shards // 2,), in_specs=[pair, pair] + [ANY] * len(ready), out_specs=(one, one),
        ),
        out_shape=(jax.ShapeDtypeStruct(shape.shape, BF16), shape),
        compiler_params=BIG,
        cost_estimate=COST,
        name="halve",
    )(bit, kept, got, *ready)


def add_kernel(a, b, out):
    out[...] = a[...] + b[...]


def add(a, b, ready):
    return pl.pallas_call(
        after(add_kernel, 2, len(ready)),
        in_specs=vm(2) + [ANY] * len(ready),
        out_specs=vm(1)[0],
        out_shape=jax.ShapeDtypeStruct(a.shape, a.dtype),
        cost_estimate=COST,
        name="add",
    )(a, b, *ready)


def hold(v, ready):
    def kernel(v_ref, *refs):
        pass

    return pl.pallas_call(
        kernel,
        in_specs=[ANY] + [ANY] * len(ready),
        out_specs=ANY,
        out_shape=jax.ShapeDtypeStruct(v.shape, v.dtype),
        input_output_aliases={0: 0},
        cost_estimate=COST,
        name="hold",
    )(v, *ready)


def finish_kernel(kept, got, out):
    out[...] = kept[0].astype(F32) + got[0].astype(F32)


def finish(kept, got, ready=()):
    _, rows, columns = kept.shape
    steps = 2 if rows % 32 == 0 else 1
    part = pl.BlockSpec((1, rows // steps, columns), lambda n: (0, n, 0))
    return pl.pallas_call(
        after(finish_kernel, 2, len(ready)),
        grid=(steps,),
        in_specs=[part, part] + [ANY] * len(ready),
        out_specs=pl.BlockSpec((rows // steps, columns), lambda n: (n, 0)),
        out_shape=jax.ShapeDtypeStruct((rows, columns), F32),
        compiler_params=BIG,
        cost_estimate=COST,
        name="finish",
    )(kept, got, *ready)


def finish_pair_kernel(col, own_kept, own_got, oth_kept, oth_got, *outs):
    own = own_kept[0].astype(F32) + own_got[0].astype(F32)
    oth = oth_kept[0].astype(F32) + oth_got[0].astype(F32)
    rows, wide = own.shape
    width = outs[0].shape[1] // 2
    blocks = wide // HS
    rest = oth[blocks * rows:]
    oth = jnp.concatenate([oth[j * rows:(j + 1) * rows] for j in range(blocks)], 1)
    for n, out in enumerate(outs[:3]):
        for i, v in ((col[0], own), (1 - col[0], oth)):
            out[:, pl.ds(pl.multiple_of(i * width, width), width)] = v[:, n * width:(n + 1) * width]
    outs[3][...] = own[:, 3 * width:] + oth[:, 3 * width:]
    size = outs[4].shape[0]
    outs[4][...] = jnp.concatenate([rest[j * size:(j + 1) * size] for j in range(rest.shape[0] // size)], 1)


def finish_pair(col, own_kept, own_got, oth_kept, oth_got, width, out_rows, ready=()):
    _, rows, columns = own_kept.shape
    blocks = (oth_kept.shape[1] - rows * (columns // HS)) // out_rows
    shapes = [(rows, 2 * width)] * 3 + [(rows, columns - 3 * width), (out_rows, blocks * HS)]
    return pl.pallas_call(
        after(finish_pair_kernel, 5, len(ready)),
        in_specs=[SMEM] + vm(4) + [ANY] * len(ready),
        out_specs=tuple(vm(5)),
        out_shape=tuple(jax.ShapeDtypeStruct(shape, F32) for shape in shapes),
        compiler_params=BIG,
        cost_estimate=COST,
        name="finish_pair",
    )(col, own_kept, own_got, oth_kept, oth_got, *ready)


def mm(left, right, dims=NN):
    return lax.dot_general(left, right, dims, preferred_element_type=F32)


def body(
    inputs, segments, mixer_gain, w_query, w_key, w_value, w_beta, conv_query, conv_key, conv_value,
    head_gain, w_out, feed_gain, w_gate, w_up, w_down, cotangent,
):
    cols, rows, groups = lax.axis_size("col"), lax.axis_size("row"), lax.axis_size("dp")
    c, r, g = lax.axis_index("col"), lax.axis_index("row"), lax.axis_index("dp")
    tokens, width = inputs.shape
    half, mine = width // cols, tokens // cols
    own_width = conv_query.shape[0]
    feed = w_gate.shape[1]

    def swap(v):
        return lax.ppermute(v, "col", [(i, i ^ 1) for i in range(cols)])

    def to_row(v, k):
        return lax.ppermute(v, "row", [(i, i ^ k) for i in range(rows)])

    def row_terms(blocks):
        return [blocks[0]] + [to_row(blocks[k], k) for k in range(rows - 1, 0, -1)]

    def row_gather(own):
        return [own] + [to_row(own, k) for k in range(1, rows)]

    def own_first(v, axis=-1):
        size = v.shape[axis] // 2
        return jnp.concatenate([lax.dynamic_slice_in_dim(v, i * size, size, axis) for i in (c, 1 - c)], axis)

    def halves(v, bit):
        parts = v.reshape(v.shape[0] // 2, 2, *v.shape[1:])
        return [lax.dynamic_index_in_dim(parts, i, 1, keepdims=False) for i in (1 - bit, bit)]

    def traded(v, step):
        return lax.ppermute(v, "dp", [(i, i ^ step) for i in range(groups)])

    def group_steps(pair, got, ready):
        step = 1
        while step * 2 < groups:
            got = got if step == 1 else traded(pair[0], step)
            step *= 2
            pair = halve(((g // step) % 2).astype(jnp.int32)[None], pair[1], got, ready)
        return pair

    def shards_of(v):
        return halves(v.astype(BF16).reshape(groups, -1, v.shape[-1]), g % 2)

    def grads_of(lefts, rights, pairs, columns, ready):
        if columns // groups % 128 == 0:
            return weight_grad(low_bit, lefts, rights, pairs, mine, columns, groups, ready)

        def rows_of(v, i):
            return v[i * mine:(i + 1) * mine]

        return shards_of(jnp.concatenate([
            sum(mm(rows_of(*lefts[i])[:, :columns], rows_of(*rights[j]), TN) for i, j in enumerate(js)) for js in zip(*pairs)
        ], 1))

    def all_sum(v):
        v = v + swap(v)
        k = 1
        while k < rows:
            v = v + to_row(v, k)
            k *= 2
        k = 1
        while k < groups:
            v = v + lax.ppermute(v, "dp", [(i, i ^ k) for i in range(groups)])
            k *= 2
        return v

    order = jnp.arange(cols * rows, dtype=jnp.int32)
    chunk_of = ((order % rows) ^ r) * cols + ((order // rows) ^ c)
    place_of = ((order % cols) ^ c) * rows + ((order // cols) ^ r)
    half_of = jnp.stack([c, 1 - c]).astype(jnp.int32)
    place_of = jnp.concatenate([place_of, half_of[:1]])
    low_bit = (g % 2).astype(jnp.int32)[None]
    documents = (segments + (jnp.arange(segments.shape[0], dtype=jnp.int32) * segments.shape[1])[:, None]).reshape(-1)
    doc_col = jnp.pad(documents, (8, 8), constant_values=-1)[:, None]
    doc_row = documents.reshape(-1, CH)
    taps = jnp.concatenate([conv_query.T, conv_key.T, conv_value.T], 1)
    gain_row = head_gain[None]
    gain_one, gain_two = own_first(mixer_gain)[None], own_first(feed_gain)[None]

    w_beta_wide = jnp.pad(w_beta, ((0, 0), (0, HS - w_beta.shape[1])))

    def columns(i):
        parts = [lax.dynamic_slice_in_dim(w, i * own_width, own_width, 1) for w in (w_query, w_key, w_value)]
        return jnp.concatenate(parts + [w_beta_wide], 1)

    w_own, w_oth = columns(c), columns(1 - c)
    w_own_x = swap(w_oth)
    act = ordered(norm_kernel, chunk_of, half_of, inputs, gain_one)
    z = mm(act[:, :half], w_own) + mm(act[:, half:], w_own_x)
    heads, *saved = delta_forward(place_of, z, taps, doc_col, doc_row, gain_row)
    w_out_x, w_gate_x, w_up_x, w_down_x, w_oth_x = swap(w_out), swap(w_gate), swap(w_up), swap(w_down), swap(w_own)
    col = half_of[:1]

    last = groups // 2
    heads_x = swap(heads)
    attended = row_terms(out_product(col, heads, heads_x, w_out, w_out_x, rows, (w_gate_x, w_up_x, w_down_x, w_oth_x)))
    cot = ordered(copy_kernel, chunk_of, half_of, cotangent, ready=attended[:1])
    d_hidden = mm(cot[:mine, :half], w_down, NT) + mm(cot[:mine, half:], w_down_x, NT)
    middle, act_two, x_own = middle_rows(chunk_of, half_of, attended, inputs, gain_two, (d_hidden, cot))

    act_two = row_gather(act_two)
    d_gate, feeds, act_near, act_far = swiglu(act_two, w_gate, w_gate_x, w_up, w_up_x, d_hidden)
    act_x, d_gate_x = swap(act_far), swap(d_gate)
    feeds_x = swap(hold(feeds, (act_x, d_gate_x)))
    act_pair = [(act_near, 0), (act_x, 0)]
    gate_grad = grads_of(act_pair, [(d_gate, 0), (d_gate_x, 0)], [(0,), (1,)], half, ())
    gate_got = traded(gate_grad[0], 1)
    d_act_two = row_terms(back([(d_gate, 0), (feeds, 1)], [w_gate, w_up], [w_gate_x, w_up_x], rows, mine, gate_grad[:1]))
    up_grad = grads_of(act_pair, [(feeds, 1), (feeds_x, 1)], [(0,), (1,)], half, d_act_two[:1])
    up_got = traded(up_grad[0], 1)
    feed_keep, feed_send = feed_product(feeds, w_down, w_down_x, rows, up_grad[:1])
    gate_grad = group_steps(gate_grad, gate_got, (feed_send,))
    gate_got = traded(gate_grad[0], last)
    d_middle, d_att, feed_part = norm_back(d_act_two, middle, gain_two, cot, gate_grad[:1], cost=spent(4))

    down_grad = down_weight_grad(low_bit, feeds, feeds_x, cot, half, groups, (d_att,))
    down_got = traded(down_grad[0], 1)
    up_grad = group_steps(up_grad, up_got, down_grad[:1])
    up_got = traded(up_grad[0], last)
    d_heads, d_heads_x, d_att_near, d_att_x = head_grad(
        col, row_gather(d_att), w_out, w_out_x, own_width, (up_grad[0], gate_got)
    )
    d_heads_x, d_att_x = swap(d_heads_x), swap(d_att_x)
    feed_got = to_row(feed_send, 1)
    dz, dz_far, d_taps, head_part = delta_backward(
        place_of, d_heads, d_heads_x, z, taps, doc_col, doc_row, gain_row, saved, (d_att_x,)
    )

    dz_far = hold(dz_far, (up_got, feed_got))
    dz_x, dz_far_x = swap(dz_far), swap(dz)
    act_pair = [(act, 0), (act, 1)]
    grad_own = grads_of(act_pair, [(dz, 0), (dz_far, 0)], [(0,), (1,)], half, ())
    own_got = traded(grad_own[0], 1)
    feed_keep, feed_send = pair_rows(feed_keep, feed_got, grad_own[:1])
    feed_got = to_row(feed_send, 2)
    dz_x = hold(dz_x, (down_got, feed_send))
    down_grad = group_steps(down_grad, down_got, (dz_x,))
    down_got = traded(down_grad[0], last)
    d_act = row_terms(back(
        [(dz, 0), (dz_x, 0)], [w_own, w_oth], [w_own_x, w_oth_x], rows, mine, (down_grad[0], feed_got, dz_far_x)
    ))
    if half // groups % 128 == 0:
        grad_oth = other_grads(
            col, low_bit, act, dz_x, dz_far_x, heads, heads_x, d_att_near, d_att_x, half, groups, d_act[:1]
        )
    else:
        def shard_blocks(v):
            v = v.reshape(groups, v.shape[0] // groups, v.shape[1] // HS, HS)
            return jnp.swapaxes(v, 1, 2).reshape(groups, -1, HS)

        projected = mm(act[:mine, :half], dz_x, TN) + mm(act[mine:, :half], dz_far_x, TN)
        first = mm(heads[:mine], d_att_near, TN) + mm(heads[mine:], d_att_x, TN)
        second = mm(heads_x[mine:], d_att_near, TN) + mm(heads_x[:mine], d_att_x, TN)
        outs = jnp.where(c == 0, jnp.concatenate([first, second], 0), jnp.concatenate([second, first], 0))
        grad_oth = halves(jnp.concatenate([shard_blocks(projected), shard_blocks(outs)], 1).astype(BF16), g % 2)
    oth_got = traded(grad_oth[0], 1)
    grad_own = group_steps(grad_own, own_got, (grad_oth[0],))
    own_got = traded(grad_own[0], last)
    output = sum_rows([middle, feed_keep, feed_got], grad_own[:1])
    input_grad = last_norm_back(d_act, x_own, gain_one, d_middle, feed_part, head_part, (output, down_got))

    input_grad = row_gather(input_grad)
    input_grad[0] = hold(input_grad[0], (own_got, oth_got))
    grad_oth = group_steps(grad_oth, oth_got, (input_grad[0],))
    oth_got = traded(grad_oth[0], last)
    input_grad_x = [swap(v) for v in input_grad]
    small = totals(half_of, input_grad, input_grad_x)
    output = row_gather(hold(output, (small, grad_oth[0])))
    input_grad, token = place(chunk_of, half_of, input_grad, input_grad_x, (grad_oth[0], small))
    output[0] = hold(output[0], (token,))
    small = hold(jnp.concatenate([small[:3].reshape(-1), d_taps.reshape(-1)]).reshape(-1, HS), (token,))
    k = 1
    while 2 * k < groups:
        small = add(small, traded(small, k), ())
        k *= 2
    small_got = traded(small, last)
    gate_grad = finish(gate_grad[1], gate_got, (token,))
    up_grad = finish(up_grad[1], up_got, (token,))
    down_grad = finish(down_grad[1], down_got, (token,))
    output, token = place(chunk_of, half_of, output, [swap(v) for v in output], (token,))
    *projections, beta_grad, out_grad = finish_pair(
        col, grad_own[1], own_got, grad_oth[1], oth_got, own_width, w_out.shape[0] // groups, (token,)
    )
    small = add(small, small_got, (beta_grad,))
    beta_grad = beta_grad[:, :w_beta.shape[1]]
    small = small.reshape(-1)
    share = width // groups
    mixer_gain_grad = lax.dynamic_slice_in_dim(small, g * share, share)
    feed_gain_grad = lax.dynamic_slice_in_dim(small, width + g * share, share)
    head_gain_grad = small[2 * width:2 * width + HS]
    d_taps = small[3 * width:].reshape(d_taps.shape)
    share = own_width // groups
    conv_grads = [
        lax.dynamic_slice_in_dim(d_taps, i * own_width + g * share, share, 1).T for i in range(3)
    ]
    return (
        output, input_grad, mixer_gain_grad, *projections, beta_grad, *conv_grads,
        head_gain_grad, out_grad, feed_gain_grad, gate_grad, up_grad, down_grad,
    )


def solution(mesh):
    weight, swapped = P("col", "row"), P("row", "col")
    taps = P(("row", "col"), None)
    grad, grad_taps = P(("col", "dp"), "row"), P(("row", "col", "dp"), None)
    grad_swapped = P(("row", "dp"), "col")
    tokens = P("dp", None)
    return jax.shard_map(
        body,
        mesh=mesh,
        in_specs=(
            tokens, tokens, P(), weight, weight, weight, weight, taps, taps, taps, P(), swapped, P(), weight, weight,
            swapped, tokens,
        ),
        out_specs=(
            tokens, tokens, P("dp"), grad, grad, grad, grad, grad_taps, grad_taps, grad_taps, P(), grad_swapped, P("dp"),
            grad, grad, grad_swapped,
        ),
        check_vma=False,
    )
```

```python
import functools
import jax
import jax.numpy as jnp
from jax import lax
from jax.experimental import pallas as pl
from jax.experimental.pallas import tpu as pltpu
from jax.sharding import PartitionSpec as P

EPSILON = 1e-06
HEAD_FLOOR = 0.02
CH = 128
HS = 128
F32 = jnp.float32
BF16 = jnp.bfloat16

NN = (((1,), (0,)), ((), ()))
NT = (((1,), (1,)), ((), ()))
TN = (((0,), (0,)), ((), ()))


def dot1(a, b, dims=NN):
    return lax.dot_general(a.astype(BF16), b.astype(BF16), dims, preferred_element_type=F32)


def split(a):
    hi = a.astype(BF16)
    return hi, (a - hi.astype(F32)).astype(BF16)


def dot3s(a, b, dims=NN):
    (ah, al), (bh, bl) = a, b
    ka, kb = dims[0][0][0], dims[0][1][0]
    left = jnp.concatenate([ah, al], ka)
    right = jnp.concatenate([jnp.concatenate([bh, bl], 1 - kb), jnp.concatenate([bh, jnp.zeros_like(bh)], 1 - kb)], kb)
    both = lax.dot_general(left, right, dims, preferred_element_type=F32)
    width = both.shape[1] // 2
    return both[:, :width] + both[:, width:]


def dot3(a, b, dims=NN):
    return dot3s(split(a), split(b), dims)


def silu_parts(z):
    s = 1.0 / (1.0 + jnp.exp(-z))
    return s, z * s


def together(steps):
    steps = list(steps)
    while steps:
        steps = [step for step in steps if next(step, steps) is not steps]


def unit_inverse(low, xor, eye, dot):
    inv = eye - jnp.where(xor < 2, low, 0.0)
    low16 = low.astype(BF16)
    size = 2
    while size < CH:
        part = jnp.where((xor >= size) & (xor < 2 * size), low, 0.0).astype(BF16)
        inv16 = inv.astype(BF16)
        half = dot1(inv16, part)
        yield
        inv = inv - dot1(half, inv16)
        yield
        size *= 2
    parts = split(inv)
    rest = (eye - inv) - dot3s(split(low), parts)
    yield
    return inv + dot3s(parts, split(rest))


def window(ref, c, cols):
    return ref[pl.ds(pl.multiple_of(c * CH, CH), CH + 8), cols]


def conv_chunk(win, taps, masks):
    out = win[8:] * taps[3]
    for j in (1, 2, 3):
        out = out + masks[j - 1] * pltpu.roll(win, j, 0)[8:] * taps[3 - j]
    return out


def chunk_docs(doc_col, doc_row, c):
    col = doc_col[pl.ds(pl.multiple_of(c * CH + 8, 8), CH), :]
    row = doc_row[pl.ds(c, 1), :]
    prev = doc_col[pl.ds(pl.multiple_of(c * CH, 8), 8), :][7:8]
    last = col[CH - 1:CH]
    return col, row, prev, last


def place_rows(place, c):
    return pl.ds(pl.multiple_of(place[c] * CH, CH), CH)


def own_beta(lanes, column, heads, h):
    return jnp.where(column == 0, lanes[:, h:h + 1], lanes[:, heads + h:heads + h + 1])


def fill_pad(pad, place, z_ref, chunks, width):
    pad[0:8] = jnp.zeros((8, 3 * width), F32)
    for c in range(chunks):
        pad[c * CH + 8:(c + 1) * CH + 8] = z_ref[place_rows(place, c), :3 * width]


def fwd_kernel(heads, chunks, dotg, doti, dot,
               place, z_ref, taps_ref, doc_col, doc_row, gain_ref,
               out_ref, mixed_ref, conv_ref, t_ref, h_ref, a_ref, qt_ref, w_ref, u_ref,
               pad, pu_s, b_s):
    width = heads * HS
    fill_pad(pad, place, z_ref, chunks, width)
    row_i = lax.broadcasted_iota(jnp.int32, (CH, CH), 0)
    col_i = lax.broadcasted_iota(jnp.int32, (CH, CH), 1)
    xor = row_i ^ col_i
    eye = (xor == 0).astype(F32)

    def one(c, h):
        col, row, prev, last = chunk_docs(doc_col, doc_row, c)
        same = col == row
        strict = same & (row_i > col_i)
        incl = same & (row_i >= col_i)
        carried = (col == prev).astype(F32)
        closing = (col == last).astype(F32)
        keep = (last == prev).astype(F32)
        dwin = doc_col[pl.ds(pl.multiple_of(c * CH, CH), CH + 8), :]
        masks = [(dwin[8 - j:CH + 8 - j] == col).astype(F32) for j in (1, 2, 3)]

        def conv(which):
            cols = slice(which * width + h * HS, which * width + (h + 1) * HS)
            taps = [taps_ref[t:t + 1, cols] for t in range(4)]
            z = conv_chunk(window(pad, c, cols), taps, masks)
            conv_ref[pl.ds(pl.multiple_of(c * CH, CH), CH), cols] = z
            return silu_parts(z)[1]

        q, k, v = conv(0), conv(1), conv(2)
        k = k * lax.rsqrt(jnp.sum(k * k, axis=1, keepdims=True) + EPSILON)
        beta = 1.0 / (1.0 + jnp.exp(-own_beta(z_ref[place_rows(place, c), 3 * width:], place[chunks], heads, h)))
        yield
        gram = dotg(k, k, NT)
        yield
        low = jnp.where(strict, beta * gram, 0.0)
        yield
        inv = yield from unit_inverse(low, xor, eye, doti)
        yield
        wu = dot(inv, jnp.concatenate([(carried * beta) * k, beta * v], 1))
        w, u = wu[:, :HS], wu[:, HS:]
        yield
        p = jnp.where(incl, dot(q, k, NT), 0.0)
        yield
        wus = split(wu)
        pwu = dot3s(split(p), wus)
        qt = carried * q - pwu[:, :HS]
        pu = pwu[:, HS:]
        yield
        kcl = closing * k
        ab = dot3s(split(kcl), wus, TN)
        a = keep * eye - ab[:, :HS]
        b = ab[:, HS:]
        yield
        i = c * heads + h
        t_ref[i] = inv
        qt_ref[i] = qt
        a_ref[i] = a
        w_ref[i] = w
        u_ref[i] = u
        pu_s[i] = pu
        b_s[i] = b

    per = 4

    def phase_one(g, carry):
        together(one(g * per + e, h) for e in range(per) for h in range(heads))
        return carry

    lax.fori_loop(0, chunks // per, phase_one, 0)

    def phase_two(c, state):
        new = []
        for h in range(heads):
            i = c * heads + h
            h_ref[i] = state[h]
            new.append(dot(a_ref[i], state[h]) + b_s[i])
        return tuple(new)

    lax.fori_loop(0, chunks, phase_two, tuple(jnp.zeros((HS, HS), F32) for _ in range(heads)))

    def phase_three(c, carry):
        for h in range(heads):
            i = c * heads + h
            rows = pl.ds(pl.multiple_of(c * CH, CH), CH)
            cols = slice(h * HS, (h + 1) * HS)
            mixed = dot(qt_ref[i], h_ref[i]) + pu_s[i]
            mixed_ref[rows, cols] = mixed
            r = lax.rsqrt(jnp.mean(mixed * mixed, axis=1, keepdims=True) + HEAD_FLOOR)
            out_ref[place_rows(place, c), cols] = (mixed * r * gain_ref[...]).astype(BF16)
        return carry

    lax.fori_loop(0, chunks, phase_three, 0)


def vm(n):
    return [pl.BlockSpec(memory_space=pltpu.VMEM)] * n


def spent(us):
    return pl.CostEstimate(flops=int(us * 1_150_000_000), bytes_accessed=1000, transcendentals=0)


COST = pl.CostEstimate(flops=1000, bytes_accessed=1000, transcendentals=0)
SMEM = pl.BlockSpec(memory_space=pltpu.SMEM)
ANY = pl.BlockSpec(memory_space=pl.ANY)


def after(kernel, count, extra):
    return lambda *refs: kernel(*refs[:count], *refs[count + extra:])


def delta_forward(place, z, taps, doc_col, doc_row, gain, dots=(dot3, dot3, dot3)):
    tokens, width = z.shape[0], taps.shape[1] // 3
    heads = width // HS
    chunks = tokens // CH
    n = chunks * heads
    sq = jax.ShapeDtypeStruct((n, CH, HS), F32)
    return pl.pallas_call(
        functools.partial(fwd_kernel, heads, chunks, *dots),
        out_shape=(jax.ShapeDtypeStruct((tokens, width), BF16), jax.ShapeDtypeStruct((tokens, width), F32),
                   jax.ShapeDtypeStruct((tokens, 3 * width), F32), sq, sq, sq, sq, sq, sq),
        in_specs=[SMEM] + vm(5), out_specs=tuple(vm(9)),
        scratch_shapes=[pltpu.VMEM((tokens + 8, 3 * width), F32), pltpu.VMEM((n, CH, HS), F32), pltpu.VMEM((n, CH, HS), F32)],
        compiler_params=pltpu.CompilerParams(vmem_limit_bytes=48 * 1024 * 1024),
        cost_estimate=COST,
        name="delta_forward",
    )(place, z, taps, doc_col, doc_row, gain)


def bwd_kernel(heads, chunks, dotg, dot,
               place, dh_own, dh_other, z_ref, taps_ref, doc_col, doc_row, gain_ref,
               mixed_ref, conv_ref, t_ref, h_ref, a_ref, qt_ref, w_ref, u_ref,
               dz_own, dz_other, dtaps_ref, dgain_ref,
               dz_ref, dh_ref, do_s, eb_s, e_s, dc_s, db_s):
    width = heads * HS
    tokens = chunks * CH
    dh_ref[:tokens // 2] = dh_own[...]
    dh_ref[tokens // 2:] = dh_other[...]
    dc_s[tokens:] = jnp.zeros((8, 3 * width), F32)
    row_i = lax.broadcasted_iota(jnp.int32, (CH, CH), 0)
    col_i = lax.broadcasted_iota(jnp.int32, (CH, CH), 1)

    def rows_of(c):
        return pl.ds(pl.multiple_of(c * CH, CH), CH)

    def phase_one(c, total):
        for h in range(heads):
            i = c * heads + h
            cols = slice(h * HS, (h + 1) * HS)
            m = mixed_ref[rows_of(c), cols]
            dy = dh_ref[place_rows(place, c), cols].astype(F32)
            r = lax.rsqrt(jnp.mean(m * m, axis=1, keepdims=True) + HEAD_FLOOR)
            mr = m * r
            total = total + jnp.sum(dy * mr, axis=0, keepdims=True)
            gy = gain_ref[...] * dy
            dm = r * (gy - mr * jnp.mean(mr * gy, axis=1, keepdims=True))
            do_s[i] = dm
            eb_s[i] = dot(qt_ref[i], dm, TN)
        return total

    dgain_ref[...] = lax.fori_loop(0, chunks, phase_one, jnp.zeros((1, HS), F32))

    def phase_two(n, state):
        c = chunks - 1 - n
        new = []
        for h in range(heads):
            i = c * heads + h
            e_s[i] = state[h]
            new.append(dot(a_ref[i], state[h], TN) + eb_s[i])
        return tuple(new)

    lax.fori_loop(0, chunks, phase_two, tuple(jnp.zeros((HS, HS), F32) for _ in range(heads)))

    def one(c, h):
        i = c * heads + h
        col, row, prev, last = chunk_docs(doc_col, doc_row, c)
        same = col == row
        strict = same & (row_i > col_i)
        incl = same & (row_i >= col_i)
        carried = (col == prev).astype(F32)
        closing = (col == last).astype(F32)

        def conv(which):
            s, y = silu_parts(conv_ref[rows_of(c), which * width + h * HS:which * width + (h + 1) * HS])
            return y, s + y * (1.0 - s)

        q, q_slope = conv(0)
        k, k_slope = conv(1)
        v, v_slope = conv(2)
        n = lax.rsqrt(jnp.sum(k * k, axis=1, keepdims=True) + EPSILON)
        k = k * n
        beta = 1.0 / (1.0 + jnp.exp(-own_beta(z_ref[place_rows(place, c), 3 * width:], place[chunks], heads, h)))
        inv, state, w, u, dm, e = t_ref[i], h_ref[i], w_ref[i], u_ref[i], do_s[i], e_s[i]
        yield
        gram = dotg(k, k, NT)
        yield
        p = jnp.where(incl, dot(q, k, NT), 0.0)
        yield
        r = u - dot(w, state)
        yield
        y = v - carried * dot(k, state)
        yield
        dr = dot(p, dm, TN) + closing * dot(k, e)
        yield
        x = dot(inv, dr, TN)
        yield
        dp = jnp.where(incl, dot(dm, r, NT), 0.0)
        yield
        dq = dot(dp, k) + carried * dot(dm, state, NT)
        yield
        dlow = jnp.where(strict, -dot(x, r, NT), 0.0)
        dgram = beta * dlow
        yield
        dk = closing * dot(r, e, NT) + dot(dp, q, TN)
        yield
        dk = dk + dot(dgram, k) + dot(dgram, k, TN)
        yield
        dk = dk - (carried * beta) * dot(x, state, NT)
        yield
        dbeta = jnp.sum(dlow * gram, axis=1, keepdims=True) + jnp.sum(x * y, axis=1, keepdims=True)
        dk = n * (dk - k * jnp.sum(k * dk, axis=1, keepdims=True))
        for which, value in ((0, dq * q_slope), (1, dk * k_slope), (2, beta * x * v_slope)):
            dc_s[rows_of(c), which * width + h * HS:which * width + (h + 1) * HS] = value
        db_s[h, rows_of(c)] = dbeta * beta * (1.0 - beta)

    per = 4

    def phase_three(g, carry):
        together(one(g * per + e, h) for e in range(per) for h in range(heads))
        return carry

    lax.fori_loop(0, chunks // per, phase_three, 0)

    def phase_four(c, sums):
        col = doc_col[pl.ds(pl.multiple_of(c * CH + 8, 8), CH), :]
        after = doc_col[pl.ds(pl.multiple_of(c * CH + 8, 8), CH + 8), :]
        later = [jnp.broadcast_to((after[j:CH + j] == col).astype(F32), (CH, HS)) for j in (1, 2, 3)]
        new = []
        for b in range(3 * heads):
            cols = slice(b * HS, (b + 1) * HS)
            z = z_ref[place_rows(place, c), cols]
            win = dc_s[pl.ds(pl.multiple_of(c * CH, CH), CH + 8), cols]
            dz = 0.0
            for j in range(4):
                d = win[:CH] if j == 0 else later[j - 1] * pltpu.roll(win, CH + 8 - j, 0)[:CH]
                dz = dz + d * taps_ref[3 - j:4 - j, cols]
                new.append(sums[4 * b + j] + jnp.sum((d * z).reshape(CH // 8, 8, HS), axis=0))
            dz_ref[place_rows(place, c), cols] = dz.astype(BF16)
        lane = lax.broadcasted_iota(jnp.int32, (CH, HS), 1) - place[chunks] * heads
        betas = sum(jnp.where(lane == h, db_s[h, rows_of(c)], 0.0) for h in range(heads))
        dz_ref[place_rows(place, c), 3 * width:] = betas.astype(BF16)
        return tuple(new)

    sums = lax.fori_loop(0, chunks, phase_four, tuple(jnp.zeros((8, HS), F32) for _ in range(12 * heads)))
    for b in range(3 * heads):
        for j in range(4):
            dtaps_ref[3 - j:4 - j, b * HS:(b + 1) * HS] = jnp.sum(sums[4 * b + j], axis=0, keepdims=True)
    dz_own[...] = dz_ref[:tokens // 2]
    dz_other[...] = dz_ref[tokens // 2:]


def delta_backward(place, own, other, z, taps, doc_col, doc_row, gain, saved, ready=(), dots=(dot3, dot3)):
    tokens, width = z.shape[0], taps.shape[1] // 3
    heads = width // HS
    chunks = tokens // CH
    n = chunks * heads
    sq = pltpu.VMEM((n, CH, HS), F32)
    return pl.pallas_call(
        after(functools.partial(bwd_kernel, heads, chunks, *dots), 16, len(ready)),
        out_shape=(jax.ShapeDtypeStruct((tokens // 2, z.shape[1]), BF16), jax.ShapeDtypeStruct((tokens // 2, z.shape[1]), BF16),
                   jax.ShapeDtypeStruct((4, 3 * width), F32),
                   jax.ShapeDtypeStruct((1, HS), F32)),
        in_specs=[SMEM] + vm(15) + [ANY] * len(ready), out_specs=tuple(vm(4)),
        scratch_shapes=[pltpu.VMEM(z.shape, BF16), pltpu.VMEM((tokens, width), BF16), sq, sq, sq, pltpu.VMEM((tokens + 8, 3 * width), F32),
                        pltpu.VMEM((heads, tokens, 1), F32)],
        compiler_params=pltpu.CompilerParams(vmem_limit_bytes=48 * 1024 * 1024),
        cost_estimate=COST,
        name="delta_backward",
    )(place, own, other, z, taps, doc_col, doc_row, gain, *saved, *ready)


def norm_kernel(chunk_of, half_of, a_ref, b_ref, gain_ref, out_ref):
    half = a_ref.shape[1]
    a, b = a_ref[...].astype(F32), b_ref[...].astype(F32)
    total = jnp.sum(a * a, axis=1, keepdims=True) + jnp.sum(b * b, axis=1, keepdims=True)
    r = lax.rsqrt(total / (2 * half) + EPSILON)
    out_ref[:, :half] = (a * r * gain_ref[:, :half]).astype(BF16)
    out_ref[:, half:] = (b * r * gain_ref[:, half:]).astype(BF16)


def copy_kernel(chunk_of, half_of, a_ref, b_ref, out_ref):
    half = a_ref.shape[1]
    out_ref[:, :half] = a_ref[...]
    out_ref[:, half:] = b_ref[...]


def ordered(kernel, chunk_of, half_of, x, *rest, ready=()):
    tokens, width = x.shape
    half = width // 2
    return pl.pallas_call(
        after(kernel, 4 + len(rest), len(ready)),
        grid_spec=pltpu.PrefetchScalarGridSpec(
            num_scalar_prefetch=2,
            grid=(tokens // CH,),
            in_specs=[
                pl.BlockSpec((CH, half), lambda p, ch, hf: (ch[p], hf[0])),
                pl.BlockSpec((CH, half), lambda p, ch, hf: (ch[p], hf[1])),
            ] + [pl.BlockSpec((1, width), lambda p, ch, hf: (0, 0)) for _ in rest] + [ANY] * len(ready),
            out_specs=pl.BlockSpec((CH, width), lambda p, ch, hf: (p, 0)),
        ),
        out_shape=jax.ShapeDtypeStruct((tokens, width), BF16),
        compiler_params=pltpu.CompilerParams(vmem_limit_bytes=32 * 1024 * 1024),
        cost_estimate=COST,
        name="ordered_rows",
    )(chunk_of, half_of, x, x, *rest, *ready)


def place_kernel(count, first, chunk_of, half_of, *refs):
    out, token = refs[-2:]
    half = out.shape[1] // 2
    token[...] = jnp.zeros_like(token)
    for p in range(count):

        @pl.when(pl.program_id(0) == p)
        def _(p=p):
            for h in range(2):
                to = half_of[h] if first == 0 else half_of[1 - h]
                out[:, pl.ds(pl.multiple_of(to * half, half), half)] = refs[p][:, h * half:(h + 1) * half]


def place(chunk_of, half_of, pieces, rest=None, ready=()):
    count = len(pieces)
    rows, width = CH, pieces[0].shape[1]
    first = 0 if rest is None else count
    extra = () if rest is None else (rest,)
    return pl.pallas_call(
        after(functools.partial(place_kernel, count, first), 2 + count, len(extra) + len(ready)),
        grid_spec=pltpu.PrefetchScalarGridSpec(
            num_scalar_prefetch=2,
            grid=(count,),
            in_specs=[pl.BlockSpec((rows, width), lambda p, ch, hf: (0, 0)) for _ in range(count)]
            + [ANY] * (len(extra) + len(ready)),
            out_specs=(
                pl.BlockSpec((rows, width), lambda p, ch, hf: (ch[p + first], 0)),
                pl.BlockSpec((8, HS), lambda p, ch, hf: (0, 0)),
            ),
        ),
        out_shape=(
            jax.ShapeDtypeStruct((2 * count * rows, width), pieces[0].dtype), jax.ShapeDtypeStruct((8, HS), F32),
        ),
        input_output_aliases={} if rest is None else {2 + count: 0},
        compiler_params=pltpu.CompilerParams(vmem_limit_bytes=32 * 1024 * 1024),
        cost_estimate=COST,
        name="place_rows",
    )(chunk_of, half_of, *pieces, *extra, *ready)


BIG = pltpu.CompilerParams(vmem_limit_bytes=32 * 1024 * 1024)


def swiglu_kernel(rows, *refs):
    acts, (wg, wgx, wu, wux, dh, d_gate, out, act_near, act_far) = refs[:rows], refs[rows:]
    half = wg.shape[0]
    near = jnp.concatenate([wg[...], wu[...]], 1)
    far = jnp.concatenate([wgx[...], wux[...]], 1)
    cut = wg.shape[1]
    size = acts[0].shape[0]

    @pl.when(pl.program_id(0) == 0)
    def _():
        for k in range(rows):
            act_near[k * size:(k + 1) * size] = acts[k][:, :half]
            act_far[k * size:(k + 1) * size] = acts[k][:, half:]

    for k in range(rows):
        both = dot1(acts[k][:, :half], near) + dot1(acts[k][:, half:], far)
        gate, up, dhk = both[:, :cut], both[:, cut:], dh[k * size:(k + 1) * size].astype(F32)
        s = 1.0 / (1.0 + jnp.exp(-gate))
        gs = gate * s
        d_gate[k * size:(k + 1) * size] = (dhk * up * (s + gs * (1.0 - s))).astype(BF16)
        for i, v in enumerate((gs * up, dhk * gs)):
            out[(i * rows + k) * size:(i * rows + k + 1) * size] = v.astype(BF16)


def swiglu(acts, w_gate, w_gate_x, w_up, w_up_x, d_hidden):
    rows = len(acts)
    size, width = acts[0].shape
    half, feed = w_gate.shape
    tile = 128
    tokens = rows * size
    weight = pl.BlockSpec((half, tile), lambda n: (0, n))
    return pl.pallas_call(
        functools.partial(swiglu_kernel, rows),
        grid=(feed // tile,),
        in_specs=[pl.BlockSpec((size, width), lambda n: (0, 0))] * rows + [weight] * 4
        + [pl.BlockSpec((tokens, tile), lambda n: (0, n))],
        out_specs=(pl.BlockSpec((tokens, tile), lambda n: (0, n)), pl.BlockSpec((2 * tokens, tile), lambda n: (0, n)))
        + (pl.BlockSpec((tokens, half), lambda n: (0, 0)),) * 2,
        out_shape=(jax.ShapeDtypeStruct((tokens, feed), BF16), jax.ShapeDtypeStruct((2 * tokens, feed), BF16))
        + (jax.ShapeDtypeStruct((tokens, half), BF16), jax.ShapeDtypeStruct((tokens, half), BF16)),
        compiler_params=BIG,
        cost_estimate=COST,
        name="swiglu",
    )(*acts, w_gate, w_gate_x, w_up, w_up_x, d_hidden)


def back_kernel(count, parts, *refs):
    lefts, near, far = refs[:count], refs[count:2 * count], refs[2 * count:3 * count]
    outs = refs[3 * count:]

    def store(weights):
        both = sum(dot1(left[...], w[...], NT) for left, w in zip(lefts, weights))
        size = both.shape[0] // parts
        for k in range(parts):
            outs[k][...] = both[k * size:(k + 1) * size].astype(outs[k].dtype)

    steps = pl.num_programs(0) // 2
    pl.when(pl.program_id(0) < steps)(lambda: store(near))
    pl.when(pl.program_id(0) >= steps)(lambda: store(far))


def back(lefts, near, far, parts, tokens, ready=()):
    count = len(lefts)
    half = near[0].shape[0]
    tile = 512
    steps = half // tile
    size = tokens // parts
    return pl.pallas_call(
        after(functools.partial(back_kernel, count, parts), 3 * count, len(ready)),
        grid=(2 * steps,),
        in_specs=[pl.BlockSpec((tokens, v.shape[1]), lambda n, i=i: (i, 0)) for v, i in lefts]
        + [pl.BlockSpec((tile, w.shape[1]), lambda n: (jnp.minimum(n, steps - 1), 0)) for w in near]
        + [pl.BlockSpec((tile, w.shape[1]), lambda n: (jnp.maximum(n - steps, 0), 0)) for w in far] + [ANY] * len(ready),
        out_specs=tuple(pl.BlockSpec((size, tile), lambda n: (0, n)) for _ in range(parts)),
        out_shape=tuple(jax.ShapeDtypeStruct((size, 2 * half), F32) if k == 0 else jax.ShapeDtypeStruct((size, 2 * half), BF16) for k in range(parts)),
        compiler_params=BIG,
        cost_estimate=COST,
        name="back_product",
    )(*[v for v, _ in lefts], *near, *far, *ready)


def grad_kernel(pairs, bit, *refs):
    lefts, rights = refs[:len(pairs)], refs[len(pairs):-2]
    send, keep = refs[-2:]
    out = jnp.concatenate([
        sum(lax.dot_general(lefts[i][...], rights[j][...], TN, preferred_element_type=F32) for i, j in group)
        for group in zip(*[[(i, j) for j in js] for i, js in enumerate(pairs)])
    ], 1).astype(BF16)
    steps = pl.num_programs(0) // 2

    @pl.when(pl.program_id(0) < steps)
    def _():
        send[0] = out

    @pl.when(pl.program_id(0) >= steps)
    def _():
        keep[0] = out


def weight_grad(bit, lefts, rights, pairs, tokens, columns, shards, ready=()):
    rows = columns // shards
    wide = sum(rights[j][0].shape[1] for j in pairs[0])
    half = shards // 2

    def shard(n, b):
        return (n % half) * 2 + jnp.where(n < half, 1 - b[0], b[0])

    shape = jax.ShapeDtypeStruct((half, rows, wide), BF16)
    return pl.pallas_call(
        after(functools.partial(grad_kernel, pairs), 1 + len(lefts) + len(rights), len(ready)),
        grid_spec=pltpu.PrefetchScalarGridSpec(
            num_scalar_prefetch=1,
            grid=(shards,),
            in_specs=[pl.BlockSpec((tokens, rows), lambda n, b, i=i: (i, shard(n, b))) for _, i in lefts]
            + [pl.BlockSpec((tokens, v.shape[1]), lambda n, b, i=i: (i, 0)) for v, i in rights] + [ANY] * len(ready),
            out_specs=(
                pl.BlockSpec((1, rows, wide), lambda n, b: (jnp.minimum(n, half - 1), 0, 0)),
                pl.BlockSpec((1, rows, wide), lambda n, b: (jnp.maximum(n - half, 0), 0, 0)),
            ),
        ),
        out_shape=(jax.ShapeDtypeStruct(shape.shape, BF16), shape),
        compiler_params=BIG,
        cost_estimate=COST,
        name="weight_grad",
    )(bit, *[v for v, _ in lefts], *[v for v, _ in rights], *ready)


def out_kernel(col, own, other, near, far, *outs):
    first, width = col[0], own.shape[1]
    left = jnp.concatenate([own[...], other[...]], 1)
    half = near.shape[1]
    for h, w in enumerate((near, far)):
        right = jnp.concatenate([w[pl.ds(pl.multiple_of(i * width, width), width)] for i in (first, 1 - first)], 0)
        both = dot1(left, right)
        size = outs[0].shape[0]
        for k, out in enumerate(outs):
            out[:, h * half:(h + 1) * half] = both[k * size:(k + 1) * size].astype(out.dtype)


def out_product(col, heads, other, w_out, w_out_x, parts, ready=()):
    tokens, width = other.shape[0] // 2, other.shape[1]
    half = w_out.shape[1]
    size = tokens // parts
    full = lambda v: pl.BlockSpec(v.shape, lambda n, c: (0, 0))
    return pl.pallas_call(
        after(out_kernel, 5, len(ready)),
        grid_spec=pltpu.PrefetchScalarGridSpec(
            num_scalar_prefetch=1,
            grid=(1,),
            in_specs=[
                pl.BlockSpec((tokens, width), lambda n, c: (0, 0)), pl.BlockSpec((tokens, width), lambda n, c: (1, 0)),
                full(w_out), full(w_out_x),
            ] + [ANY] * len(ready),
            out_specs=tuple(pl.BlockSpec((size, 2 * half), lambda n, c: (0, 0)) for _ in range(parts)),
        ),
        out_shape=tuple(jax.ShapeDtypeStruct((size, 2 * half), F32) if k == 0 else jax.ShapeDtypeStruct((size, 2 * half), BF16) for k in range(parts)),
        compiler_params=BIG,
        cost_estimate=COST,
        name="out_product",
    )(col, heads, other, w_out, w_out_x, *ready)


def head_grad_kernel(parts, col, *refs):
    grads, (near, far, own, other, near_out, far_out) = refs[:parts], refs[parts:]
    width, half = own.shape[1], near.shape[1]
    size = grads[0].shape[0]
    for k in range(parts):
        near_out[k * size:(k + 1) * size] = grads[k][:, :half]
        far_out[k * size:(k + 1) * size] = grads[k][:, half:]
    for i, out in ((col[0], own), (1 - col[0], other)):
        rows = pl.ds(pl.multiple_of(i * width, width), width)
        right = jnp.concatenate([near[rows], far[rows]], 1)
        for k in range(parts):
            out[k * size:(k + 1) * size] = dot1(grads[k][...], right, NT).astype(BF16)


def head_grad(col, grads, w_out, w_out_x, width, ready=()):
    parts, size = len(grads), grads[0].shape[0]
    shape = jax.ShapeDtypeStruct((parts * size, width), BF16)
    shape_two = jax.ShapeDtypeStruct((parts * size, w_out.shape[1]), BF16)
    return pl.pallas_call(
        after(functools.partial(head_grad_kernel, parts), parts + 3, len(ready)),
        in_specs=[SMEM] + vm(parts + 2) + [ANY] * len(ready),
        out_specs=tuple(vm(4)),
        out_shape=(shape, jax.ShapeDtypeStruct(shape.shape, BF16), shape_two, jax.ShapeDtypeStruct(shape_two.shape, BF16)),
        compiler_params=BIG,
        cost_estimate=COST,
        name="head_grad",
    )(col, *grads, w_out, w_out_x, *ready)


def middle_kernel(count, chunk_of, half_of, *refs):
    terms, (a, b, gain, middle, act, own) = refs[:count], refs[count:]
    own[...] = jnp.concatenate([a[...], b[...]], 1)
    total = own[...].astype(F32)
    for term in terms:
        total = total + term[...].astype(F32)
    middle[...] = total
    act[...] = (total * lax.rsqrt(jnp.mean(total * total, axis=1, keepdims=True) + EPSILON) * gain[...]).astype(BF16)


def middle_rows(chunk_of, half_of, terms, x, gain, ready=()):
    count = len(terms)
    rows, width = terms[0].shape
    steps, rows = 4, rows // 4
    whole = pl.BlockSpec((rows, width), lambda n, ch, hf: (n, 0))
    return pl.pallas_call(
        after(functools.partial(middle_kernel, count), count + 5, len(ready)),
        grid_spec=pltpu.PrefetchScalarGridSpec(
            num_scalar_prefetch=2,
            grid=(steps,),
            in_specs=[whole] * count + [
                pl.BlockSpec((rows, width // 2), lambda n, ch, hf: (ch[0] * steps + n, hf[0])),
                pl.BlockSpec((rows, width // 2), lambda n, ch, hf: (ch[0] * steps + n, hf[1])),
                pl.BlockSpec((1, width), lambda n, ch, hf: (0, 0)),
            ] + [ANY] * len(ready),
            out_specs=(whole, whole, whole),
        ),
        out_shape=(
            jax.ShapeDtypeStruct((steps * rows, width), F32), jax.ShapeDtypeStruct((steps * rows, width), BF16),
            jax.ShapeDtypeStruct((steps * rows, width), BF16),
        ),
        compiler_params=BIG,
        cost_estimate=COST,
        name="middle_rows",
    )(chunk_of, half_of, *terms, x, x, gain, *ready)


def norm_back_kernel(count, *refs):
    terms, (values, gain, upstream, total, low, part) = refs[:count], refs[count:]
    grads = terms[0][...]
    for term in terms[1:]:
        grads = grads + term[...].astype(F32)
    v = values[...].astype(F32)
    r = lax.rsqrt(jnp.mean(v * v, axis=1, keepdims=True) + EPSILON)
    normal = v * r
    scaled = gain[...] * grads
    out = upstream[...].astype(F32) + r * (scaled - normal * jnp.mean(normal * scaled, axis=1, keepdims=True))
    total[...] = out
    low[...] = out.astype(BF16)

    @pl.when(pl.program_id(0) == 0)
    def _():
        part[...] = jnp.zeros_like(part)

    part[...] += jnp.sum(grads * normal, axis=0, keepdims=True)


def norm_back(terms, values, gain, upstream, ready=(), cost=COST):
    count = len(terms)
    rows, width = values.shape
    steps = 4
    whole = pl.BlockSpec((rows // steps, width), lambda n: (n, 0))
    row = pl.BlockSpec((1, width), lambda n: (0, 0))
    return pl.pallas_call(
        after(functools.partial(norm_back_kernel, count), count + 3, len(ready)),
        grid=(steps,),
        in_specs=[whole] * (count + 1) + [row, whole] + [ANY] * len(ready),
        out_specs=(whole, whole, row),
        out_shape=(
            jax.ShapeDtypeStruct((rows, width), F32), jax.ShapeDtypeStruct((rows, width), BF16),
            jax.ShapeDtypeStruct((1, width), F32),
        ),
        compiler_params=BIG,
        cost_estimate=cost,
        name="norm_back",
    )(*terms, values, gain, upstream, *ready)


def split_rows(bit, value, send, keep):
    rows = send.shape[1]
    for j in range(2 * send.shape[0]):
        part = value[j * rows:(j + 1) * rows].astype(BF16)
        for to, same in ((send, False), (keep, True)):

            @pl.when((bit == j % 2) == same)
            def _(to=to, j=j, part=part):
                to[j // 2] = part


def down_kernel(bit, hidden, hidden_x, cot, cot_x, send, keep):
    split_rows(bit[0], dot1(hidden[...], cot[...], TN) + dot1(hidden_x[...], cot_x[...], TN), send, keep)


def down_weight_grad(bit, hidden, hidden_x, cot, half, shards, ready=()):
    tokens, feed = hidden.shape[0] // 2, hidden.shape[1]
    tile = 512
    shape = jax.ShapeDtypeStruct((shards // 2, feed // shards, half), BF16)
    out = pl.BlockSpec((shards // 2, feed // shards, tile), lambda n, b: (0, 0, n))
    return pl.pallas_call(
        after(down_kernel, 5, len(ready)),
        grid_spec=pltpu.PrefetchScalarGridSpec(
            num_scalar_prefetch=1,
            grid=(half // tile,),
            in_specs=[
                pl.BlockSpec((tokens, feed), lambda n, b: (0, 0)),
                pl.BlockSpec((tokens, feed), lambda n, b: (0, 0)),
                pl.BlockSpec((tokens, tile), lambda n, b: (0, n)),
                pl.BlockSpec((tokens, tile), lambda n, b: (1, n)),
            ] + [ANY] * len(ready),
            out_specs=(out, out),
        ),
        out_shape=(jax.ShapeDtypeStruct(shape.shape, BF16), shape),
        compiler_params=BIG,
        cost_estimate=COST,
        name="down_weight_grad",
    )(bit, hidden, hidden_x, cot, cot, *ready)


def blocks_of(v):
    return jnp.concatenate([v[:, j:j + HS] for j in range(0, v.shape[1], HS)], 0)


def other_grad_kernel(flip, bit, act, act_far, dz, dz_far, heads, other, grads, grads_x, send, keep, rows_out):
    steps = pl.num_programs(0)
    tokens = grads.shape[0]

    @pl.when(pl.program_id(0) == 0)
    def _():
        g, gx = grads[...], grads_x[...]
        own = dot1(heads[:tokens], g, TN) + dot1(heads[tokens:], gx, TN)
        away = dot1(other[tokens:], g, TN) + dot1(other[:tokens], gx, TN)
        rows_out[...] = jnp.concatenate([own, away], 0).astype(BF16)

    n = pl.program_id(0)
    half = steps // 2
    shard = (n % half) * 2 + jnp.where(n < half, 1 - bit[0], bit[0])
    size = rows_out.shape[0] // steps
    place = (shard + flip[0] * half) % steps
    part = rows_out[pl.ds(pl.multiple_of(place * size, size), size)]
    value = (dot1(act[...], dz[...], TN) + dot1(act_far[...], dz_far[...], TN)).astype(BF16)
    value = jnp.concatenate([blocks_of(value), blocks_of(part)], 0)
    pl.when(n < half)(lambda: send.__setitem__(0, value))
    pl.when(n >= half)(lambda: keep.__setitem__(0, value))


def other_grads(flip, bit, act, dz, dz_far, heads, other, grads, grads_x, columns, shards, ready=()):
    tokens, wide = dz.shape
    rows, half = columns // shards, shards // 2
    out_rows, out_wide = 2 * heads.shape[1], grads.shape[1]
    deep = rows * (wide // HS) + out_rows // shards * (out_wide // HS)

    def shard(n, b):
        return (n % half) * 2 + jnp.where(n < half, 1 - b[0], b[0])

    whole = lambda v: pl.BlockSpec(v.shape, lambda n, f, b: (0, 0))
    shape = jax.ShapeDtypeStruct((half, deep, HS), BF16)
    return pl.pallas_call(
        after(other_grad_kernel, 10, len(ready)),
        grid_spec=pltpu.PrefetchScalarGridSpec(
            num_scalar_prefetch=2,
            grid=(shards,),
            in_specs=[pl.BlockSpec((tokens, rows), lambda n, f, b, i=i: (i, shard(n, b))) for i in range(2)]
            + [whole(v) for v in (dz, dz_far, heads, other, grads, grads_x)] + [ANY] * len(ready),
            out_specs=(
                pl.BlockSpec((1, deep, HS), lambda n, f, b: (jnp.minimum(n, half - 1), 0, 0)),
                pl.BlockSpec((1, deep, HS), lambda n, f, b: (jnp.maximum(n - half, 0), 0, 0)),
            ),
            scratch_shapes=[pltpu.VMEM((out_rows, out_wide), BF16)],
        ),
        out_shape=(jax.ShapeDtypeStruct(shape.shape, BF16), shape),
        compiler_params=BIG,
        cost_estimate=COST,
        name="other_grads",
    )(flip, bit, act, act, dz, dz_far, heads, other, grads, grads_x, *ready)


def feed_kernel(parts, hidden, near, far, keep, send):
    size = hidden.shape[0] // parts

    def store(w):
        both = dot1(hidden[...], w[...])
        for k in range(0, parts, 2):
            keep[k // 2 * size:(k // 2 + 1) * size] = both[k * size:(k + 1) * size]
            send[k // 2 * size:(k // 2 + 1) * size] = both[(k + 1) * size:(k + 2) * size].astype(BF16)

    pl.when(pl.program_id(0) == 0)(lambda: store(near))
    pl.when(pl.program_id(0) == 1)(lambda: store(far))


def feed_product(hidden, near, far, parts, ready=()):
    tokens, half = hidden.shape[0] // 2, near.shape[1]
    whole = lambda v: pl.BlockSpec(v.shape, lambda n: (0, 0))
    return pl.pallas_call(
        after(functools.partial(feed_kernel, parts), 3, len(ready)),
        grid=(2,),
        in_specs=[pl.BlockSpec((tokens, hidden.shape[1]), lambda n: (0, 0)), whole(near), whole(far)] + [ANY] * len(ready),
        out_specs=(pl.BlockSpec((tokens // 2, half), lambda n: (0, n)),) * 2,
        out_shape=(jax.ShapeDtypeStruct((tokens // 2, 2 * half), F32), jax.ShapeDtypeStruct((tokens // 2, 2 * half), BF16)),
        compiler_params=BIG,
        cost_estimate=COST,
        name="feed_product",
    )(hidden, near, far, *ready)


def pair_kernel(kept, got, keep, send):
    size = keep.shape[0]
    keep[...] = kept[:size] + got[:size].astype(F32)
    send[...] = (kept[size:] + got[size:].astype(F32)).astype(BF16)


def pair_rows(kept, got, ready=()):
    rows, width = kept.shape
    return pl.pallas_call(
        after(pair_kernel, 2, len(ready)),
        in_specs=vm(2) + [ANY] * len(ready),
        out_specs=tuple(vm(2)),
        out_shape=(jax.ShapeDtypeStruct((rows // 2, width), F32), jax.ShapeDtypeStruct((rows // 2, width), BF16)),
        compiler_params=BIG,
        cost_estimate=COST,
        name="pair_rows",
    )(kept, got, *ready)


def split_row(v):
    hi = v.astype(BF16).astype(F32)
    return jnp.concatenate([hi, v - hi], 0)


def last_norm_kernel(count, *refs):
    terms, (values, gain, upstream, feed_part, head_part, out) = refs[:count], refs[count:]
    grads = terms[0][...]
    for term in terms[1:]:
        grads = grads + term[...].astype(F32)
    v = values[...].astype(F32)
    r = lax.rsqrt(jnp.mean(v * v, axis=1, keepdims=True) + EPSILON)
    normal = v * r
    scaled = gain[...] * grads
    rows, width = v.shape
    out[:rows] = (upstream[...] + r * (scaled - normal * jnp.mean(normal * scaled, axis=1, keepdims=True))).astype(BF16)
    part = jnp.sum(grads * normal, axis=0, keepdims=True)
    head = jnp.concatenate([head_part[...], jnp.zeros((1, width - HS), F32)], 1)
    extra = [split_row(part), split_row(feed_part[...]), split_row(head), jnp.zeros((10, width), F32)]
    out[rows:] = jnp.concatenate(extra, 0).astype(BF16)


def last_norm_back(terms, values, gain, upstream, feed_part, head_part, ready=()):
    count = len(terms)
    rows, width = values.shape
    return pl.pallas_call(
        after(functools.partial(last_norm_kernel, count), count + 5, len(ready)),
        in_specs=vm(count + 5) + [ANY] * len(ready),
        out_specs=vm(1)[0],
        out_shape=jax.ShapeDtypeStruct((rows + 16, width), BF16),
        compiler_params=BIG,
        cost_estimate=spent(4),
        name="last_norm_back",
    )(*terms, values, gain, upstream, feed_part, head_part, *ready)


def total_kernel(half_of, *refs):
    pieces, out = refs[:-1], refs[-1]
    half = out.shape[1] // 2
    count = len(pieces) // 2
    for h in range(2):
        own = sum(ref[...].astype(F32)[:, h * half:(h + 1) * half] for ref in pieces[:count])
        oth = sum(ref[...].astype(F32)[:, (1 - h) * half:(2 - h) * half] for ref in pieces[count:])
        total = own + oth
        out[:, pl.ds(pl.multiple_of(half_of[h] * half, half), half)] = jnp.concatenate(
            [total[n:n + 1] + total[n + 1:n + 2] for n in (0, 2)] + [jnp.zeros((6, half), F32)], 0)
    heads = sum(ref[...].astype(F32)[4:6, :HS] for ref in pieces)
    out[2:3, :HS] = heads[0:1] + heads[1:2]


def totals(half_of, own, partner, ready=()):
    rows, width = own[0].shape
    at = (rows - 16) // 16
    return pl.pallas_call(
        after(total_kernel, 1 + 2 * len(own), len(ready)),
        grid_spec=pltpu.PrefetchScalarGridSpec(
            num_scalar_prefetch=1,
            grid=(1,),
            in_specs=[pl.BlockSpec((16, width), lambda n, hf: (at, 0))] * (2 * len(own)) + [ANY] * len(ready),
            out_specs=pl.BlockSpec((8, width), lambda n, hf: (0, 0)),
        ),
        out_shape=jax.ShapeDtypeStruct((8, width), F32),
        compiler_params=BIG,
        cost_estimate=COST,
        name="totals",
    )(half_of, *own, *partner, *ready)


def sum_kernel(*refs):
    total = refs[0][...]
    for ref in refs[1:-1]:
        total = total + ref[...].astype(F32)
    refs[-1][...] = total.astype(BF16)


def sum_rows(terms, ready=()):
    return pl.pallas_call(
        after(sum_kernel, len(terms), len(ready)),
        in_specs=vm(len(terms)) + [ANY] * len(ready),
        out_specs=vm(1)[0],
        out_shape=jax.ShapeDtypeStruct(terms[0].shape, BF16),
        compiler_params=BIG,
        cost_estimate=COST,
        name="sum_rows",
    )(*terms, *ready)


def halve_kernel(bit, kept, got, send, keep):
    for out, i in ((send, 1 - bit[0]), (keep, bit[0])):
        out[...] = (kept[pl.ds(i, 1)].astype(F32) + got[pl.ds(i, 1)].astype(F32)).astype(BF16)


def halve(bit, kept, got, ready=()):
    shards, rows, columns = kept.shape
    pair = pl.BlockSpec((2, rows, columns), lambda n, b: (n, 0, 0))
    one = pl.BlockSpec((1, rows, columns), lambda n, b: (n, 0, 0))
    shape = jax.ShapeDtypeStruct((shards // 2, rows, columns), BF16)
    return pl.pallas_call(
        after(halve_kernel, 3, len(ready)),
        grid_spec=pltpu.PrefetchScalarGridSpec(
            num_scalar_prefetch=1, grid=(shards // 2,), in_specs=[pair, pair] + [ANY] * len(ready), out_specs=(one, one),
        ),
        out_shape=(jax.ShapeDtypeStruct(shape.shape, BF16), shape),
        compiler_params=BIG,
        cost_estimate=COST,
        name="halve",
    )(bit, kept, got, *ready)


def add_kernel(a, b, out):
    out[...] = a[...] + b[...]


def add(a, b, ready):
    return pl.pallas_call(
        after(add_kernel, 2, len(ready)),
        in_specs=vm(2) + [ANY] * len(ready),
        out_specs=vm(1)[0],
        out_shape=jax.ShapeDtypeStruct(a.shape, a.dtype),
        cost_estimate=COST,
        name="add",
    )(a, b, *ready)


def hold(v, ready):
    def kernel(v_ref, *refs):
        pass

    return pl.pallas_call(
        kernel,
        in_specs=[ANY] + [ANY] * len(ready),
        out_specs=ANY,
        out_shape=jax.ShapeDtypeStruct(v.shape, v.dtype),
        input_output_aliases={0: 0},
        cost_estimate=COST,
        name="hold",
    )(v, *ready)


def finish_kernel(kept, got, out, token):
    out[...] = kept[0].astype(F32) + got[0].astype(F32)
    token[...] = jnp.zeros_like(token)


def finish(kept, got, ready=()):
    _, rows, columns = kept.shape
    steps = 2 if rows % 32 == 0 else 1
    part = pl.BlockSpec((1, rows // steps, columns), lambda n: (0, n, 0))
    return pl.pallas_call(
        after(finish_kernel, 2, len(ready)),
        grid=(steps,),
        in_specs=[part, part] + [ANY] * len(ready),
        out_specs=(pl.BlockSpec((rows // steps, columns), lambda n: (n, 0)), pl.BlockSpec((8, HS), lambda n: (0, 0))),
        out_shape=(jax.ShapeDtypeStruct((rows, columns), F32), jax.ShapeDtypeStruct((8, HS), F32)),
        compiler_params=BIG,
        cost_estimate=COST,
        name="finish",
    )(kept, got, *ready)


def finish_small_kernel(gains, share, group, small, got, mixer, feed, head, *taps):
    i = group[0]
    total = small[...] + got[...]
    per, steps = gains // HS, mixer.shape[0]
    mixer[...] = sum(jnp.where(i == n, total[n * steps:(n + 1) * steps], 0.0) for n in range(per // steps))
    feed[...] = sum(jnp.where(i == n, total[per + n * steps:per + (n + 1) * steps], 0.0) for n in range(per // steps))
    head[...] = total[2 * per:2 * per + 1]
    tiles = share * (per // steps) // HS
    for which, out in enumerate(taps):
        rows = []
        for t in range(out.shape[0]):
            at = 3 * per + (t * len(taps) + which) * tiles
            rows.append(sum(
                jnp.where(i == n, total[at + n * share // HS:at + n * share // HS + 1, n * share % HS:n * share % HS + share], 0.0)
                for n in range(per // steps)
            ))
        out[...] = jnp.concatenate(rows, 0)


def finish_small(group, small, got, gains, tap_shape, shares, ready=()):
    taps, wide = tap_shape
    share = wide // 3 // shares
    shapes = [(gains // HS // shares, HS)] * 2 + [(1, HS)] + [(taps, share)] * 3
    return pl.pallas_call(
        after(functools.partial(finish_small_kernel, gains, share), 3, len(ready)),
        in_specs=[SMEM] + vm(2) + [ANY] * len(ready),
        out_specs=tuple(vm(6)),
        out_shape=tuple(jax.ShapeDtypeStruct(shape, F32) for shape in shapes),
        compiler_params=BIG,
        cost_estimate=COST,
        name="finish_small",
    )(group, small, got, *ready)


def finish_pair_kernel(col, own_kept, own_got, oth_kept, oth_got, *outs):
    own = own_kept[0].astype(F32) + own_got[0].astype(F32)
    oth = oth_kept[0].astype(F32) + oth_got[0].astype(F32)
    rows, wide = own.shape
    width = outs[0].shape[1] // 2
    blocks = wide // HS
    rest = oth[blocks * rows:]
    oth = jnp.concatenate([oth[j * rows:(j + 1) * rows] for j in range(blocks)], 1)
    for n, out in enumerate(outs[:3]):
        for i, v in ((col[0], own), (1 - col[0], oth)):
            out[:, pl.ds(pl.multiple_of(i * width, width), width)] = v[:, n * width:(n + 1) * width]
    outs[3][...] = own[:, 3 * width:] + oth[:, 3 * width:]
    size = outs[4].shape[0]
    outs[4][...] = jnp.concatenate([rest[j * size:(j + 1) * size] for j in range(rest.shape[0] // size)], 1)


def finish_pair(col, own_kept, own_got, oth_kept, oth_got, width, out_rows, ready=()):
    _, rows, columns = own_kept.shape
    blocks = (oth_kept.shape[1] - rows * (columns // HS)) // out_rows
    shapes = [(rows, 2 * width)] * 3 + [(rows, columns - 3 * width), (out_rows, blocks * HS)]
    return pl.pallas_call(
        after(finish_pair_kernel, 5, len(ready)),
        in_specs=[SMEM] + vm(4) + [ANY] * len(ready),
        out_specs=tuple(vm(5)),
        out_shape=tuple(jax.ShapeDtypeStruct(shape, F32) for shape in shapes),
        compiler_params=BIG,
        cost_estimate=COST,
        name="finish_pair",
    )(col, own_kept, own_got, oth_kept, oth_got, *ready)


def mm(left, right, dims=NN):
    return lax.dot_general(left, right, dims, preferred_element_type=F32)


def body(
    inputs, segments, mixer_gain, w_query, w_key, w_value, w_beta, conv_query, conv_key, conv_value,
    head_gain, w_out, feed_gain, w_gate, w_up, w_down, cotangent,
):
    cols, rows, groups = lax.axis_size("col"), lax.axis_size("row"), lax.axis_size("dp")
    c, r, g = lax.axis_index("col"), lax.axis_index("row"), lax.axis_index("dp")
    tokens, width = inputs.shape
    half, mine = width // cols, tokens // cols
    own_width = conv_query.shape[0]
    feed = w_gate.shape[1]

    def swap(v):
        return lax.ppermute(v, "col", [(i, i ^ 1) for i in range(cols)])

    def to_row(v, k):
        return lax.ppermute(v, "row", [(i, i ^ k) for i in range(rows)])

    def row_terms(blocks):
        return [blocks[0]] + [to_row(blocks[k], k) for k in range(rows - 1, 0, -1)]

    def row_gather(own):
        return [own] + [to_row(own, k) for k in range(1, rows)]

    def own_first(v, axis=-1):
        size = v.shape[axis] // 2
        return jnp.concatenate([lax.dynamic_slice_in_dim(v, i * size, size, axis) for i in (c, 1 - c)], axis)

    def halves(v, bit):
        parts = v.reshape(v.shape[0] // 2, 2, *v.shape[1:])
        return [lax.dynamic_index_in_dim(parts, i, 1, keepdims=False) for i in (1 - bit, bit)]

    def traded(v, step):
        return lax.ppermute(v, "dp", [(i, i ^ step) for i in range(groups)])

    def group_steps(pair, got, ready):
        step = 1
        while step * 2 < groups:
            got = got if step == 1 else traded(pair[0], step)
            step *= 2
            pair = halve(((g // step) % 2).astype(jnp.int32)[None], pair[1], got, ready)
        return pair

    def shards_of(v):
        return halves(v.astype(BF16).reshape(groups, -1, v.shape[-1]), g % 2)

    def grads_of(lefts, rights, pairs, columns, ready):
        if columns // groups % 128 == 0:
            return weight_grad(low_bit, lefts, rights, pairs, mine, columns, groups, ready)

        def rows_of(v, i):
            return v[i * mine:(i + 1) * mine]

        return shards_of(jnp.concatenate([
            sum(mm(rows_of(*lefts[i])[:, :columns], rows_of(*rights[j]), TN) for i, j in enumerate(js)) for js in zip(*pairs)
        ], 1))

    def all_sum(v):
        v = v + swap(v)
        k = 1
        while k < rows:
            v = v + to_row(v, k)
            k *= 2
        k = 1
        while k < groups:
            v = v + lax.ppermute(v, "dp", [(i, i ^ k) for i in range(groups)])
            k *= 2
        return v

    order = jnp.arange(cols * rows, dtype=jnp.int32)
    chunk_of = ((order % rows) ^ r) * cols + ((order // rows) ^ c)
    place_of = ((order % cols) ^ c) * rows + ((order // cols) ^ r)
    half_of = jnp.stack([c, 1 - c]).astype(jnp.int32)
    place_of = jnp.concatenate([place_of, half_of[:1]])
    low_bit = (g % 2).astype(jnp.int32)[None]
    documents = (segments + (jnp.arange(segments.shape[0], dtype=jnp.int32) * segments.shape[1])[:, None]).reshape(-1)
    doc_col = jnp.pad(documents, (8, 8), constant_values=-1)[:, None]
    doc_row = documents.reshape(-1, CH)
    taps = jnp.concatenate([conv_query.T, conv_key.T, conv_value.T], 1)
    gain_row = head_gain[None]
    gain_one, gain_two = own_first(mixer_gain)[None], own_first(feed_gain)[None]

    w_beta_wide = jnp.pad(w_beta, ((0, 0), (0, HS - w_beta.shape[1])))

    def columns(i):
        parts = [lax.dynamic_slice_in_dim(w, i * own_width, own_width, 1) for w in (w_query, w_key, w_value)]
        return jnp.concatenate(parts + [w_beta_wide], 1)

    w_own, w_oth = columns(c), columns(1 - c)
    w_own_x = swap(w_oth)
    act = ordered(norm_kernel, chunk_of, half_of, inputs, gain_one)
    z = mm(act[:, :half], w_own) + mm(act[:, half:], w_own_x)
    heads, *saved = delta_forward(place_of, z, taps, doc_col, doc_row, gain_row)
    w_out_x, w_gate_x, w_up_x, w_down_x, w_oth_x = swap(w_out), swap(w_gate), swap(w_up), swap(w_down), swap(w_own)
    col = half_of[:1]

    last = groups // 2
    heads_x = swap(heads)
    attended = row_terms(out_product(col, heads, heads_x, w_out, w_out_x, rows, (w_gate_x, w_up_x, w_down_x, w_oth_x)))
    cot = ordered(copy_kernel, chunk_of, half_of, cotangent, ready=attended[:1])
    d_hidden = mm(cot[:mine, :half], w_down, NT) + mm(cot[:mine, half:], w_down_x, NT)
    middle, act_two, x_own = middle_rows(chunk_of, half_of, attended, inputs, gain_two, (d_hidden, cot))

    act_two = row_gather(act_two)
    d_gate, feeds, act_near, act_far = swiglu(act_two, w_gate, w_gate_x, w_up, w_up_x, d_hidden)
    act_x, d_gate_x = swap(act_far), swap(d_gate)
    feeds_x = swap(hold(feeds, (act_x, d_gate_x)))
    act_pair = [(act_near, 0), (act_x, 0)]
    gate_grad = grads_of(act_pair, [(d_gate, 0), (d_gate_x, 0)], [(0,), (1,)], half, ())
    gate_got = traded(gate_grad[0], 1)
    d_act_two = row_terms(back([(d_gate, 0), (feeds, 1)], [w_gate, w_up], [w_gate_x, w_up_x], rows, mine, gate_grad[:1]))
    up_grad = grads_of(act_pair, [(feeds, 1), (feeds_x, 1)], [(0,), (1,)], half, d_act_two[:1])
    up_got = traded(up_grad[0], 1)
    feed_keep, feed_send = feed_product(feeds, w_down, w_down_x, rows, up_grad[:1])
    gate_grad = group_steps(gate_grad, gate_got, (feed_send,))
    gate_got = traded(gate_grad[0], last)
    d_middle, d_att, feed_part = norm_back(d_act_two, middle, gain_two, cot, gate_grad[:1], cost=spent(4))

    down_grad = down_weight_grad(low_bit, feeds, feeds_x, cot, half, groups, (d_att,))
    down_got = traded(down_grad[0], 1)
    up_grad = group_steps(up_grad, up_got, down_grad[:1])
    up_got = traded(up_grad[0], last)
    d_heads, d_heads_x, d_att_near, d_att_x = head_grad(
        col, row_gather(d_att), w_out, w_out_x, own_width, (up_grad[0], gate_got)
    )
    d_heads_x, d_att_x = swap(d_heads_x), swap(d_att_x)
    feed_got = to_row(feed_send, 1)
    dz, dz_far, d_taps, head_part = delta_backward(
        place_of, d_heads, d_heads_x, z, taps, doc_col, doc_row, gain_row, saved, (d_att_x,)
    )

    feed_keep, feed_send = pair_rows(feed_keep, feed_got, (dz_far, up_got))
    feed_got = to_row(feed_send, 2)
    dz_x, dz_far_x = swap(dz_far), swap(dz)
    act_pair = [(act, 0), (act, 1)]
    grad_own = grads_of(act_pair, [(dz, 0), (dz_far, 0)], [(0,), (1,)], half, (feed_send,))
    own_got = traded(grad_own[0], 1)
    down_grad = group_steps(down_grad, down_got, (grad_own[0],))
    down_got = traded(down_grad[0], last)
    d_act = row_terms(back(
        [(dz, 0), (dz_x, 0)], [w_own, w_oth], [w_own_x, w_oth_x], rows, mine, (down_grad[0], feed_got, dz_far_x)
    ))
    if half // groups % 128 == 0:
        grad_oth = other_grads(
            col, low_bit, act, dz_x, dz_far_x, heads, heads_x, d_att_near, d_att_x, half, groups, d_act[:1]
        )
    else:
        def shard_blocks(v):
            v = v.reshape(groups, v.shape[0] // groups, v.shape[1] // HS, HS)
            return jnp.swapaxes(v, 1, 2).reshape(groups, -1, HS)

        projected = mm(act[:mine, :half], dz_x, TN) + mm(act[mine:, :half], dz_far_x, TN)
        first = mm(heads[:mine], d_att_near, TN) + mm(heads[mine:], d_att_x, TN)
        second = mm(heads_x[mine:], d_att_near, TN) + mm(heads_x[:mine], d_att_x, TN)
        outs = jnp.where(c == 0, jnp.concatenate([first, second], 0), jnp.concatenate([second, first], 0))
        grad_oth = halves(jnp.concatenate([shard_blocks(projected), shard_blocks(outs)], 1).astype(BF16), g % 2)
    oth_got = traded(grad_oth[0], 1)
    grad_own = group_steps(grad_own, own_got, (grad_oth[0],))
    own_got = traded(grad_own[0], last)
    output = sum_rows([middle, feed_keep, feed_got], grad_own[:1])
    input_grad = last_norm_back(d_act, x_own, gain_one, d_middle, feed_part, head_part, (output, down_got))

    input_grad = row_gather(input_grad)
    grad_oth = group_steps(grad_oth, oth_got, (own_got,))
    oth_got = traded(grad_oth[0], last)
    input_grad_x = [swap(v) for v in input_grad]
    placed, token = place(chunk_of, half_of, input_grad, None, (grad_oth[0],))
    small = totals(half_of, input_grad, input_grad_x, (token,))
    output = row_gather(hold(output, (small,)))
    input_grad, token = place(chunk_of, half_of, input_grad_x, placed, (small,))
    small = hold(jnp.concatenate([small[:3].reshape(-1), d_taps.reshape(-1)]).reshape(-1, HS), (token,))
    k = 1
    while 2 * k < groups:
        small = add(small, traded(small, k), ())
        k *= 2
    small_got = traded(small, last)
    gate_grad, token_gate = finish(gate_grad[1], gate_got, (token,))
    up_grad, token_up = finish(up_grad[1], up_got, (token_gate,))
    down_grad, token = finish(down_grad[1], down_got, (token_up,))
    output[0] = hold(output[0], (token,))
    output_x = [swap(v) for v in output]
    placed, token = place(chunk_of, half_of, output, None, (token,))
    output, token = place(chunk_of, half_of, output_x, placed, (token,))
    *projections, beta_grad, out_grad = finish_pair(
        col, grad_own[1], own_got, grad_oth[1], oth_got, own_width, w_out.shape[0] // groups, (token,)
    )
    mixer_gain_grad, feed_gain_grad, head_gain_grad, *conv_grads = finish_small(
        g.astype(jnp.int32)[None], small, small_got, width, d_taps.shape, groups, (beta_grad,)
    )
    beta_grad = beta_grad[:, :w_beta.shape[1]]
    mixer_gain_grad, feed_gain_grad, head_gain_grad = (
        v.reshape(-1) for v in (mixer_gain_grad, feed_gain_grad, head_gain_grad)
    )
    conv_grads = [v.T for v in conv_grads]
    return (
        output, input_grad, mixer_gain_grad, *projections, beta_grad, *conv_grads,
        head_gain_grad, out_grad, feed_gain_grad, gate_grad, up_grad, down_grad,
    )


def solution(mesh):
    weight, swapped = P("col", "row"), P("row", "col")
    taps = P(("row", "col"), None)
    grad, grad_taps = P(("col", "dp"), "row"), P(("row", "col", "dp"), None)
    grad_swapped = P(("row", "dp"), "col")
    tokens = P("dp", None)
    return jax.shard_map(
        body,
        mesh=mesh,
        in_specs=(
            tokens, tokens, P(), weight, weight, weight, weight, taps, taps, taps, P(), swapped, P(), weight, weight,
            swapped, tokens,
        ),
        out_specs=(
            tokens, tokens, P("dp"), grad, grad, grad, grad, grad_taps, grad_taps, grad_taps, P(), grad_swapped, P("dp"),
            grad, grad, grad_swapped,
        ),
        check_vma=False,
    )
```

```python
import functools
import jax
import jax.numpy as jnp
from jax import lax
from jax.experimental import pallas as pl
from jax.experimental.pallas import tpu as pltpu
from jax.sharding import PartitionSpec as P

EPSILON = 1e-06
HEAD_FLOOR = 0.02
CH = 128
HS = 128
F32 = jnp.float32
BF16 = jnp.bfloat16

NN = (((1,), (0,)), ((), ()))
NT = (((1,), (1,)), ((), ()))
TN = (((0,), (0,)), ((), ()))


def dot1(a, b, dims=NN):
    return lax.dot_general(a.astype(BF16), b.astype(BF16), dims, preferred_element_type=F32)


def split(a):
    hi = a.astype(BF16)
    return hi, (a - hi.astype(F32)).astype(BF16)


def dot3s(a, b, dims=NN):
    (ah, al), (bh, bl) = a, b
    ka, kb = dims[0][0][0], dims[0][1][0]
    left = jnp.concatenate([ah, al], ka)
    right = jnp.concatenate([jnp.concatenate([bh, bl], 1 - kb), jnp.concatenate([bh, jnp.zeros_like(bh)], 1 - kb)], kb)
    both = lax.dot_general(left, right, dims, preferred_element_type=F32)
    width = both.shape[1] // 2
    return both[:, :width] + both[:, width:]


def dot3(a, b, dims=NN):
    return dot3s(split(a), split(b), dims)


def silu_parts(z):
    s = 1.0 / (1.0 + jnp.exp(-z))
    return s, z * s


def together(steps):
    steps = list(steps)
    while steps:
        steps = [step for step in steps if next(step, steps) is not steps]


def unit_inverse(low, xor, eye, dot):
    inv = eye - jnp.where(xor < 2, low, 0.0)
    low16 = low.astype(BF16)
    size = 2
    while size < CH:
        part = jnp.where((xor >= size) & (xor < 2 * size), low, 0.0).astype(BF16)
        inv16 = inv.astype(BF16)
        half = dot1(inv16, part)
        yield
        inv = inv - dot1(half, inv16)
        yield
        size *= 2
    parts = split(inv)
    rest = (eye - inv) - dot3s(split(low), parts)
    yield
    return inv + dot3s(parts, split(rest))


def window(ref, c, cols):
    return ref[pl.ds(pl.multiple_of(c * CH, CH), CH + 8), cols]


def conv_chunk(win, taps, masks):
    out = win[8:] * taps[3]
    for j in (1, 2, 3):
        out = out + masks[j - 1] * pltpu.roll(win, j, 0)[8:] * taps[3 - j]
    return out


def chunk_docs(doc_col, doc_row, c):
    col = doc_col[pl.ds(pl.multiple_of(c * CH + 8, 8), CH), :]
    row = doc_row[pl.ds(c, 1), :]
    prev = doc_col[pl.ds(pl.multiple_of(c * CH, 8), 8), :][7:8]
    last = col[CH - 1:CH]
    return col, row, prev, last


def place_rows(place, c):
    return pl.ds(pl.multiple_of(place[c] * CH, CH), CH)


def own_beta(lanes, column, heads, h):
    return jnp.where(column == 0, lanes[:, h:h + 1], lanes[:, heads + h:heads + h + 1])


def fill_pad(pad, place, z_ref, chunks, width):
    pad[0:8] = jnp.zeros((8, 3 * width), F32)
    for c in range(chunks):
        pad[c * CH + 8:(c + 1) * CH + 8] = z_ref[place_rows(place, c), :3 * width]


def fwd_kernel(heads, chunks, dotg, doti, dot,
               place, z_ref, taps_ref, doc_col, doc_row, gain_ref,
               out_ref, mixed_ref, conv_ref, t_ref, h_ref, a_ref, qt_ref, w_ref, u_ref,
               pad, pu_s, b_s):
    width = heads * HS
    fill_pad(pad, place, z_ref, chunks, width)
    row_i = lax.broadcasted_iota(jnp.int32, (CH, CH), 0)
    col_i = lax.broadcasted_iota(jnp.int32, (CH, CH), 1)
    xor = row_i ^ col_i
    eye = (xor == 0).astype(F32)

    def one(c, h):
        col, row, prev, last = chunk_docs(doc_col, doc_row, c)
        same = col == row
        strict = same & (row_i > col_i)
        incl = same & (row_i >= col_i)
        carried = (col == prev).astype(F32)
        closing = (col == last).astype(F32)
        keep = (last == prev).astype(F32)
        dwin = doc_col[pl.ds(pl.multiple_of(c * CH, CH), CH + 8), :]
        masks = [(dwin[8 - j:CH + 8 - j] == col).astype(F32) for j in (1, 2, 3)]

        def conv(which):
            cols = slice(which * width + h * HS, which * width + (h + 1) * HS)
            taps = [taps_ref[t:t + 1, cols] for t in range(4)]
            z = conv_chunk(window(pad, c, cols), taps, masks)
            conv_ref[pl.ds(pl.multiple_of(c * CH, CH), CH), cols] = z
            return silu_parts(z)[1]

        q, k, v = conv(0), conv(1), conv(2)
        k = k * lax.rsqrt(jnp.sum(k * k, axis=1, keepdims=True) + EPSILON)
        beta = 1.0 / (1.0 + jnp.exp(-own_beta(z_ref[place_rows(place, c), 3 * width:], place[chunks], heads, h)))
        yield
        gram = dotg(k, k, NT)
        yield
        low = jnp.where(strict, beta * gram, 0.0)
        yield
        inv = yield from unit_inverse(low, xor, eye, doti)
        yield
        wu = dot(inv, jnp.concatenate([(carried * beta) * k, beta * v], 1))
        w, u = wu[:, :HS], wu[:, HS:]
        yield
        p = jnp.where(incl, dot(q, k, NT), 0.0)
        yield
        wus = split(wu)
        pwu = dot3s(split(p), wus)
        qt = carried * q - pwu[:, :HS]
        pu = pwu[:, HS:]
        yield
        kcl = closing * k
        ab = dot3s(split(kcl), wus, TN)
        a = keep * eye - ab[:, :HS]
        b = ab[:, HS:]
        yield
        i = c * heads + h
        t_ref[i] = inv
        qt_ref[i] = qt
        a_ref[i] = a
        w_ref[i] = w
        u_ref[i] = u
        pu_s[i] = pu
        b_s[i] = b

    per = 4

    def phase_one(g, carry):
        together(one(g * per + e, h) for e in range(per) for h in range(heads))
        return carry

    lax.fori_loop(0, chunks // per, phase_one, 0)

    def phase_two(c, state):
        new = []
        for h in range(heads):
            i = c * heads + h
            h_ref[i] = state[h]
            new.append(dot(a_ref[i], state[h]) + b_s[i])
        return tuple(new)

    lax.fori_loop(0, chunks, phase_two, tuple(jnp.zeros((HS, HS), F32) for _ in range(heads)))

    def phase_three(c, carry):
        for h in range(heads):
            i = c * heads + h
            rows = pl.ds(pl.multiple_of(c * CH, CH), CH)
            cols = slice(h * HS, (h + 1) * HS)
            mixed = dot(qt_ref[i], h_ref[i]) + pu_s[i]
            mixed_ref[rows, cols] = mixed
            r = lax.rsqrt(jnp.mean(mixed * mixed, axis=1, keepdims=True) + HEAD_FLOOR)
            out_ref[place_rows(place, c), cols] = (mixed * r * gain_ref[...]).astype(BF16)
        return carry

    lax.fori_loop(0, chunks, phase_three, 0)


def vm(n):
    return [pl.BlockSpec(memory_space=pltpu.VMEM)] * n


def spent(us):
    return pl.CostEstimate(flops=int(us * 1_150_000_000), bytes_accessed=1000, transcendentals=0)


COST = pl.CostEstimate(flops=1000, bytes_accessed=1000, transcendentals=0)
SMEM = pl.BlockSpec(memory_space=pltpu.SMEM)
ANY = pl.BlockSpec(memory_space=pl.ANY)


def after(kernel, count, extra):
    return lambda *refs: kernel(*refs[:count], *refs[count + extra:])


def delta_forward(place, z, taps, doc_col, doc_row, gain, dots=(dot3, dot3, dot3)):
    tokens, width = z.shape[0], taps.shape[1] // 3
    heads = width // HS
    chunks = tokens // CH
    n = chunks * heads
    sq = jax.ShapeDtypeStruct((n, CH, HS), F32)
    return pl.pallas_call(
        functools.partial(fwd_kernel, heads, chunks, *dots),
        out_shape=(jax.ShapeDtypeStruct((tokens, width), BF16), jax.ShapeDtypeStruct((tokens, width), F32),
                   jax.ShapeDtypeStruct((tokens, 3 * width), F32), sq, sq, sq, sq, sq, sq),
        in_specs=[SMEM] + vm(5), out_specs=tuple(vm(9)),
        scratch_shapes=[pltpu.VMEM((tokens + 8, 3 * width), F32), pltpu.VMEM((n, CH, HS), F32), pltpu.VMEM((n, CH, HS), F32)],
        compiler_params=pltpu.CompilerParams(vmem_limit_bytes=48 * 1024 * 1024),
        cost_estimate=COST,
        name="delta_forward",
    )(place, z, taps, doc_col, doc_row, gain)


def bwd_kernel(heads, chunks, dotg, dot,
               place, dh_own, dh_other, z_ref, taps_ref, doc_col, doc_row, gain_ref,
               mixed_ref, conv_ref, t_ref, h_ref, a_ref, qt_ref, w_ref, u_ref,
               dz_own, dz_other, dtaps_ref, dgain_ref,
               dz_ref, dh_ref, do_s, eb_s, e_s, dc_s, db_s):
    width = heads * HS
    tokens = chunks * CH
    dh_ref[:tokens // 2] = dh_own[...]
    dh_ref[tokens // 2:] = dh_other[...]
    dc_s[tokens:] = jnp.zeros((8, 3 * width), F32)
    row_i = lax.broadcasted_iota(jnp.int32, (CH, CH), 0)
    col_i = lax.broadcasted_iota(jnp.int32, (CH, CH), 1)

    def rows_of(c):
        return pl.ds(pl.multiple_of(c * CH, CH), CH)

    def phase_one(c, total):
        for h in range(heads):
            i = c * heads + h
            cols = slice(h * HS, (h + 1) * HS)
            m = mixed_ref[rows_of(c), cols]
            dy = dh_ref[place_rows(place, c), cols].astype(F32)
            r = lax.rsqrt(jnp.mean(m * m, axis=1, keepdims=True) + HEAD_FLOOR)
            mr = m * r
            total = total + jnp.sum(dy * mr, axis=0, keepdims=True)
            gy = gain_ref[...] * dy
            dm = r * (gy - mr * jnp.mean(mr * gy, axis=1, keepdims=True))
            do_s[i] = dm
            eb_s[i] = dot(qt_ref[i], dm, TN)
        return total

    dgain_ref[...] = lax.fori_loop(0, chunks, phase_one, jnp.zeros((1, HS), F32))

    def phase_two(n, state):
        c = chunks - 1 - n
        new = []
        for h in range(heads):
            i = c * heads + h
            e_s[i] = state[h]
            new.append(dot(a_ref[i], state[h], TN) + eb_s[i])
        return tuple(new)

    lax.fori_loop(0, chunks, phase_two, tuple(jnp.zeros((HS, HS), F32) for _ in range(heads)))

    def one(c, h):
        i = c * heads + h
        col, row, prev, last = chunk_docs(doc_col, doc_row, c)
        same = col == row
        strict = same & (row_i > col_i)
        incl = same & (row_i >= col_i)
        carried = (col == prev).astype(F32)
        closing = (col == last).astype(F32)

        def conv(which):
            s, y = silu_parts(conv_ref[rows_of(c), which * width + h * HS:which * width + (h + 1) * HS])
            return y, s + y * (1.0 - s)

        q, q_slope = conv(0)
        k, k_slope = conv(1)
        v, v_slope = conv(2)
        n = lax.rsqrt(jnp.sum(k * k, axis=1, keepdims=True) + EPSILON)
        k = k * n
        beta = 1.0 / (1.0 + jnp.exp(-own_beta(z_ref[place_rows(place, c), 3 * width:], place[chunks], heads, h)))
        inv, state, w, u, dm, e = t_ref[i], h_ref[i], w_ref[i], u_ref[i], do_s[i], e_s[i]
        yield
        gram = dotg(k, k, NT)
        yield
        p = jnp.where(incl, dot(q, k, NT), 0.0)
        yield
        r = u - dot(w, state)
        yield
        y = v - carried * dot(k, state)
        yield
        dr = dot(p, dm, TN) + closing * dot(k, e)
        yield
        x = dot(inv, dr, TN)
        yield
        dp = jnp.where(incl, dot(dm, r, NT), 0.0)
        yield
        dq = dot(dp, k) + carried * dot(dm, state, NT)
        yield
        dlow = jnp.where(strict, -dot(x, r, NT), 0.0)
        dgram = beta * dlow
        yield
        dk = closing * dot(r, e, NT) + dot(dp, q, TN)
        yield
        dk = dk + dot(dgram, k) + dot(dgram, k, TN)
        yield
        dk = dk - (carried * beta) * dot(x, state, NT)
        yield
        dbeta = jnp.sum(dlow * gram, axis=1, keepdims=True) + jnp.sum(x * y, axis=1, keepdims=True)
        dk = n * (dk - k * jnp.sum(k * dk, axis=1, keepdims=True))
        for which, value in ((0, dq * q_slope), (1, dk * k_slope), (2, beta * x * v_slope)):
            dc_s[rows_of(c), which * width + h * HS:which * width + (h + 1) * HS] = value
        db_s[h, rows_of(c)] = dbeta * beta * (1.0 - beta)

    per = 4

    def phase_three(g, carry):
        together(one(g * per + e, h) for e in range(per) for h in range(heads))
        return carry

    lax.fori_loop(0, chunks // per, phase_three, 0)

    def phase_four(c, sums):
        col = doc_col[pl.ds(pl.multiple_of(c * CH + 8, 8), CH), :]
        after = doc_col[pl.ds(pl.multiple_of(c * CH + 8, 8), CH + 8), :]
        later = [jnp.broadcast_to((after[j:CH + j] == col).astype(F32), (CH, HS)) for j in (1, 2, 3)]
        new = []
        for b in range(3 * heads):
            cols = slice(b * HS, (b + 1) * HS)
            z = z_ref[place_rows(place, c), cols]
            win = dc_s[pl.ds(pl.multiple_of(c * CH, CH), CH + 8), cols]
            dz = 0.0
            for j in range(4):
                d = win[:CH] if j == 0 else later[j - 1] * pltpu.roll(win, CH + 8 - j, 0)[:CH]
                dz = dz + d * taps_ref[3 - j:4 - j, cols]
                new.append(sums[4 * b + j] + jnp.sum((d * z).reshape(CH // 8, 8, HS), axis=0))
            dz_ref[place_rows(place, c), cols] = dz.astype(BF16)
        lane = lax.broadcasted_iota(jnp.int32, (CH, HS), 1) - place[chunks] * heads
        betas = sum(jnp.where(lane == h, db_s[h, rows_of(c)], 0.0) for h in range(heads))
        dz_ref[place_rows(place, c), 3 * width:] = betas.astype(BF16)
        return tuple(new)

    sums = lax.fori_loop(0, chunks, phase_four, tuple(jnp.zeros((8, HS), F32) for _ in range(12 * heads)))
    for b in range(3 * heads):
        for j in range(4):
            dtaps_ref[3 - j:4 - j, b * HS:(b + 1) * HS] = jnp.sum(sums[4 * b + j], axis=0, keepdims=True)
    dz_own[...] = dz_ref[:tokens // 2]
    dz_other[...] = dz_ref[tokens // 2:]


def delta_backward(place, own, other, z, taps, doc_col, doc_row, gain, saved, ready=(), dots=(dot3, dot3)):
    tokens, width = z.shape[0], taps.shape[1] // 3
    heads = width // HS
    chunks = tokens // CH
    n = chunks * heads
    sq = pltpu.VMEM((n, CH, HS), F32)
    return pl.pallas_call(
        after(functools.partial(bwd_kernel, heads, chunks, *dots), 16, len(ready)),
        out_shape=(jax.ShapeDtypeStruct((tokens // 2, z.shape[1]), BF16), jax.ShapeDtypeStruct((tokens // 2, z.shape[1]), BF16),
                   jax.ShapeDtypeStruct((4, 3 * width), F32),
                   jax.ShapeDtypeStruct((1, HS), F32)),
        in_specs=[SMEM] + vm(15) + [ANY] * len(ready), out_specs=tuple(vm(4)),
        scratch_shapes=[pltpu.VMEM(z.shape, BF16), pltpu.VMEM((tokens, width), BF16), sq, sq, sq, pltpu.VMEM((tokens + 8, 3 * width), F32),
                        pltpu.VMEM((heads, tokens, 1), F32)],
        compiler_params=pltpu.CompilerParams(vmem_limit_bytes=48 * 1024 * 1024),
        cost_estimate=COST,
        name="delta_backward",
    )(place, own, other, z, taps, doc_col, doc_row, gain, *saved, *ready)


def norm_kernel(chunk_of, half_of, a_ref, b_ref, gain_ref, out_ref):
    half = a_ref.shape[1]
    a, b = a_ref[...].astype(F32), b_ref[...].astype(F32)
    total = jnp.sum(a * a, axis=1, keepdims=True) + jnp.sum(b * b, axis=1, keepdims=True)
    r = lax.rsqrt(total / (2 * half) + EPSILON)
    out_ref[:, :half] = (a * r * gain_ref[:, :half]).astype(BF16)
    out_ref[:, half:] = (b * r * gain_ref[:, half:]).astype(BF16)


def copy_kernel(chunk_of, half_of, a_ref, b_ref, out_ref):
    half = a_ref.shape[1]
    out_ref[:, :half] = a_ref[...]
    out_ref[:, half:] = b_ref[...]


def ordered(kernel, chunk_of, half_of, x, *rest, ready=()):
    tokens, width = x.shape
    half = width // 2
    return pl.pallas_call(
        after(kernel, 4 + len(rest), len(ready)),
        grid_spec=pltpu.PrefetchScalarGridSpec(
            num_scalar_prefetch=2,
            grid=(tokens // CH,),
            in_specs=[
                pl.BlockSpec((CH, half), lambda p, ch, hf: (ch[p], hf[0])),
                pl.BlockSpec((CH, half), lambda p, ch, hf: (ch[p], hf[1])),
            ] + [pl.BlockSpec((1, width), lambda p, ch, hf: (0, 0)) for _ in rest] + [ANY] * len(ready),
            out_specs=pl.BlockSpec((CH, width), lambda p, ch, hf: (p, 0)),
        ),
        out_shape=jax.ShapeDtypeStruct((tokens, width), BF16),
        compiler_params=pltpu.CompilerParams(vmem_limit_bytes=32 * 1024 * 1024),
        cost_estimate=COST,
        name="ordered_rows",
    )(chunk_of, half_of, x, x, *rest, *ready)


def place_kernel(count, first, chunk_of, half_of, *refs):
    out, token = refs[-2:]
    half = out.shape[1] // 2
    token[...] = jnp.zeros_like(token)
    for p in range(count):

        @pl.when(pl.program_id(0) == p)
        def _(p=p):
            for h in range(2):
                to = half_of[h] if first == 0 else half_of[1 - h]
                out[:, pl.ds(pl.multiple_of(to * half, half), half)] = refs[p][:, h * half:(h + 1) * half]


def place(chunk_of, half_of, pieces, rest=None, ready=()):
    count = len(pieces)
    rows, width = CH, pieces[0].shape[1]
    first = 0 if rest is None else count
    extra = () if rest is None else (rest,)
    return pl.pallas_call(
        after(functools.partial(place_kernel, count, first), 2 + count, len(extra) + len(ready)),
        grid_spec=pltpu.PrefetchScalarGridSpec(
            num_scalar_prefetch=2,
            grid=(count,),
            in_specs=[pl.BlockSpec((rows, width), lambda p, ch, hf: (0, 0)) for _ in range(count)]
            + [ANY] * (len(extra) + len(ready)),
            out_specs=(
                pl.BlockSpec((rows, width), lambda p, ch, hf: (ch[p + first], 0)),
                pl.BlockSpec((8, HS), lambda p, ch, hf: (0, 0)),
            ),
        ),
        out_shape=(
            jax.ShapeDtypeStruct((2 * count * rows, width), pieces[0].dtype), jax.ShapeDtypeStruct((8, HS), F32),
        ),
        input_output_aliases={} if rest is None else {2 + count: 0},
        compiler_params=pltpu.CompilerParams(vmem_limit_bytes=32 * 1024 * 1024),
        cost_estimate=COST,
        name="place_rows",
    )(chunk_of, half_of, *pieces, *extra, *ready)


BIG = pltpu.CompilerParams(vmem_limit_bytes=32 * 1024 * 1024)


def swiglu_kernel(rows, *refs):
    acts, (wg, wgx, wu, wux, dh, d_gate, out, act_near, act_far) = refs[:rows], refs[rows:]
    half = wg.shape[0]
    near = jnp.concatenate([wg[...], wu[...]], 1)
    far = jnp.concatenate([wgx[...], wux[...]], 1)
    cut = wg.shape[1]
    size = acts[0].shape[0]

    @pl.when(pl.program_id(0) == 0)
    def _():
        for k in range(rows):
            act_near[k * size:(k + 1) * size] = acts[k][:, :half]
            act_far[k * size:(k + 1) * size] = acts[k][:, half:]

    for k in range(rows):
        both = dot1(acts[k][:, :half], near) + dot1(acts[k][:, half:], far)
        gate, up, dhk = both[:, :cut], both[:, cut:], dh[k * size:(k + 1) * size].astype(F32)
        s = 1.0 / (1.0 + jnp.exp(-gate))
        gs = gate * s
        d_gate[k * size:(k + 1) * size] = (dhk * up * (s + gs * (1.0 - s))).astype(BF16)
        for i, v in enumerate((gs * up, dhk * gs)):
            out[(i * rows + k) * size:(i * rows + k + 1) * size] = v.astype(BF16)


def swiglu(acts, w_gate, w_gate_x, w_up, w_up_x, d_hidden):
    rows = len(acts)
    size, width = acts[0].shape
    half, feed = w_gate.shape
    tile = 128
    tokens = rows * size
    weight = pl.BlockSpec((half, tile), lambda n: (0, n))
    return pl.pallas_call(
        functools.partial(swiglu_kernel, rows),
        grid=(feed // tile,),
        in_specs=[pl.BlockSpec((size, width), lambda n: (0, 0))] * rows + [weight] * 4
        + [pl.BlockSpec((tokens, tile), lambda n: (0, n))],
        out_specs=(pl.BlockSpec((tokens, tile), lambda n: (0, n)), pl.BlockSpec((2 * tokens, tile), lambda n: (0, n)))
        + (pl.BlockSpec((tokens, half), lambda n: (0, 0)),) * 2,
        out_shape=(jax.ShapeDtypeStruct((tokens, feed), BF16), jax.ShapeDtypeStruct((2 * tokens, feed), BF16))
        + (jax.ShapeDtypeStruct((tokens, half), BF16), jax.ShapeDtypeStruct((tokens, half), BF16)),
        compiler_params=BIG,
        cost_estimate=COST,
        name="swiglu",
    )(*acts, w_gate, w_gate_x, w_up, w_up_x, d_hidden)


def back_kernel(count, parts, *refs):
    lefts, near, far = refs[:count], refs[count:2 * count], refs[2 * count:3 * count]
    outs = refs[3 * count:]

    def store(weights):
        both = sum(dot1(left[...], w[...], NT) for left, w in zip(lefts, weights))
        size = both.shape[0] // parts
        for k in range(parts):
            outs[k][...] = both[k * size:(k + 1) * size].astype(outs[k].dtype)

    steps = pl.num_programs(0) // 2
    pl.when(pl.program_id(0) < steps)(lambda: store(near))
    pl.when(pl.program_id(0) >= steps)(lambda: store(far))


def back(lefts, near, far, parts, tokens, ready=(), cost=COST):
    count = len(lefts)
    half = near[0].shape[0]
    tile = 512
    steps = half // tile
    size = tokens // parts
    return pl.pallas_call(
        after(functools.partial(back_kernel, count, parts), 3 * count, len(ready)),
        grid=(2 * steps,),
        in_specs=[pl.BlockSpec((tokens, v.shape[1]), lambda n, i=i: (i, 0)) for v, i in lefts]
        + [pl.BlockSpec((tile, w.shape[1]), lambda n: (jnp.minimum(n, steps - 1), 0)) for w in near]
        + [pl.BlockSpec((tile, w.shape[1]), lambda n: (jnp.maximum(n - steps, 0), 0)) for w in far] + [ANY] * len(ready),
        out_specs=tuple(pl.BlockSpec((size, tile), lambda n: (0, n)) for _ in range(parts)),
        out_shape=tuple(jax.ShapeDtypeStruct((size, 2 * half), F32) if k == 0 else jax.ShapeDtypeStruct((size, 2 * half), BF16) for k in range(parts)),
        compiler_params=BIG,
        cost_estimate=cost,
        name="back_product",
    )(*[v for v, _ in lefts], *near, *far, *ready)


def grad_kernel(pairs, bit, *refs):
    lefts, rights = refs[:len(pairs)], refs[len(pairs):-2]
    send, keep = refs[-2:]
    out = jnp.concatenate([
        sum(lax.dot_general(lefts[i][...], rights[j][...], TN, preferred_element_type=F32) for i, j in group)
        for group in zip(*[[(i, j) for j in js] for i, js in enumerate(pairs)])
    ], 1).astype(BF16)
    steps = pl.num_programs(0) // 2

    @pl.when(pl.program_id(0) < steps)
    def _():
        send[0] = out

    @pl.when(pl.program_id(0) >= steps)
    def _():
        keep[0] = out


def weight_grad(bit, lefts, rights, pairs, tokens, columns, shards, ready=()):
    rows = columns // shards
    wide = sum(rights[j][0].shape[1] for j in pairs[0])
    half = shards // 2

    def shard(n, b):
        return (n % half) * 2 + jnp.where(n < half, 1 - b[0], b[0])

    shape = jax.ShapeDtypeStruct((half, rows, wide), BF16)
    return pl.pallas_call(
        after(functools.partial(grad_kernel, pairs), 1 + len(lefts) + len(rights), len(ready)),
        grid_spec=pltpu.PrefetchScalarGridSpec(
            num_scalar_prefetch=1,
            grid=(shards,),
            in_specs=[pl.BlockSpec((tokens, rows), lambda n, b, i=i: (i, shard(n, b))) for _, i in lefts]
            + [pl.BlockSpec((tokens, v.shape[1]), lambda n, b, i=i: (i, 0)) for v, i in rights] + [ANY] * len(ready),
            out_specs=(
                pl.BlockSpec((1, rows, wide), lambda n, b: (jnp.minimum(n, half - 1), 0, 0)),
                pl.BlockSpec((1, rows, wide), lambda n, b: (jnp.maximum(n - half, 0), 0, 0)),
            ),
        ),
        out_shape=(jax.ShapeDtypeStruct(shape.shape, BF16), shape),
        compiler_params=BIG,
        cost_estimate=COST,
        name="weight_grad",
    )(bit, *[v for v, _ in lefts], *[v for v, _ in rights], *ready)


def out_kernel(col, own, other, near, far, *outs):
    first, width = col[0], own.shape[1]
    left = jnp.concatenate([own[...], other[...]], 1)
    half = near.shape[1]
    for h, w in enumerate((near, far)):
        right = jnp.concatenate([w[pl.ds(pl.multiple_of(i * width, width), width)] for i in (first, 1 - first)], 0)
        both = dot1(left, right)
        size = outs[0].shape[0]
        for k, out in enumerate(outs):
            out[:, h * half:(h + 1) * half] = both[k * size:(k + 1) * size].astype(out.dtype)


def out_product(col, heads, other, w_out, w_out_x, parts, ready=()):
    tokens, width = other.shape[0] // 2, other.shape[1]
    half = w_out.shape[1]
    size = tokens // parts
    full = lambda v: pl.BlockSpec(v.shape, lambda n, c: (0, 0))
    return pl.pallas_call(
        after(out_kernel, 5, len(ready)),
        grid_spec=pltpu.PrefetchScalarGridSpec(
            num_scalar_prefetch=1,
            grid=(1,),
            in_specs=[
                pl.BlockSpec((tokens, width), lambda n, c: (0, 0)), pl.BlockSpec((tokens, width), lambda n, c: (1, 0)),
                full(w_out), full(w_out_x),
            ] + [ANY] * len(ready),
            out_specs=tuple(pl.BlockSpec((size, 2 * half), lambda n, c: (0, 0)) for _ in range(parts)),
        ),
        out_shape=tuple(jax.ShapeDtypeStruct((size, 2 * half), F32) if k == 0 else jax.ShapeDtypeStruct((size, 2 * half), BF16) for k in range(parts)),
        compiler_params=BIG,
        cost_estimate=COST,
        name="out_product",
    )(col, heads, other, w_out, w_out_x, *ready)


def head_grad_kernel(parts, col, *refs):
    grads, (near, far, own, other, near_out, far_out) = refs[:parts], refs[parts:]
    width, half = own.shape[1], near.shape[1]
    size = grads[0].shape[0]
    for k in range(parts):
        near_out[k * size:(k + 1) * size] = grads[k][:, :half]
        far_out[k * size:(k + 1) * size] = grads[k][:, half:]
    for i, out in ((col[0], own), (1 - col[0], other)):
        rows = pl.ds(pl.multiple_of(i * width, width), width)
        right = jnp.concatenate([near[rows], far[rows]], 1)
        for k in range(parts):
            out[k * size:(k + 1) * size] = dot1(grads[k][...], right, NT).astype(BF16)


def head_grad(col, grads, w_out, w_out_x, width, ready=()):
    parts, size = len(grads), grads[0].shape[0]
    shape = jax.ShapeDtypeStruct((parts * size, width), BF16)
    shape_two = jax.ShapeDtypeStruct((parts * size, w_out.shape[1]), BF16)
    return pl.pallas_call(
        after(functools.partial(head_grad_kernel, parts), parts + 3, len(ready)),
        in_specs=[SMEM] + vm(parts + 2) + [ANY] * len(ready),
        out_specs=tuple(vm(4)),
        out_shape=(shape, jax.ShapeDtypeStruct(shape.shape, BF16), shape_two, jax.ShapeDtypeStruct(shape_two.shape, BF16)),
        compiler_params=BIG,
        cost_estimate=COST,
        name="head_grad",
    )(col, *grads, w_out, w_out_x, *ready)


def middle_kernel(count, chunk_of, half_of, *refs):
    terms, (a, b, gain, middle, act, own) = refs[:count], refs[count:]
    own[...] = jnp.concatenate([a[...], b[...]], 1)
    total = own[...].astype(F32)
    for term in terms:
        total = total + term[...].astype(F32)
    middle[...] = total
    act[...] = (total * lax.rsqrt(jnp.mean(total * total, axis=1, keepdims=True) + EPSILON) * gain[...]).astype(BF16)


def middle_rows(chunk_of, half_of, terms, x, gain, ready=()):
    count = len(terms)
    rows, width = terms[0].shape
    steps, rows = 4, rows // 4
    whole = pl.BlockSpec((rows, width), lambda n, ch, hf: (n, 0))
    return pl.pallas_call(
        after(functools.partial(middle_kernel, count), count + 5, len(ready)),
        grid_spec=pltpu.PrefetchScalarGridSpec(
            num_scalar_prefetch=2,
            grid=(steps,),
            in_specs=[whole] * count + [
                pl.BlockSpec((rows, width // 2), lambda n, ch, hf: (ch[0] * steps + n, hf[0])),
                pl.BlockSpec((rows, width // 2), lambda n, ch, hf: (ch[0] * steps + n, hf[1])),
                pl.BlockSpec((1, width), lambda n, ch, hf: (0, 0)),
            ] + [ANY] * len(ready),
            out_specs=(whole, whole, whole),
        ),
        out_shape=(
            jax.ShapeDtypeStruct((steps * rows, width), F32), jax.ShapeDtypeStruct((steps * rows, width), BF16),
            jax.ShapeDtypeStruct((steps * rows, width), BF16),
        ),
        compiler_params=BIG,
        cost_estimate=COST,
        name="middle_rows",
    )(chunk_of, half_of, *terms, x, x, gain, *ready)


def norm_back_kernel(count, *refs):
    terms, (values, gain, upstream, total, low, part) = refs[:count], refs[count:]
    grads = terms[0][...]
    for term in terms[1:]:
        grads = grads + term[...].astype(F32)
    v = values[...].astype(F32)
    r = lax.rsqrt(jnp.mean(v * v, axis=1, keepdims=True) + EPSILON)
    normal = v * r
    scaled = gain[...] * grads
    out = upstream[...].astype(F32) + r * (scaled - normal * jnp.mean(normal * scaled, axis=1, keepdims=True))
    total[...] = out
    low[...] = out.astype(BF16)

    @pl.when(pl.program_id(0) == 0)
    def _():
        part[...] = jnp.zeros_like(part)

    part[...] += jnp.sum(grads * normal, axis=0, keepdims=True)


def norm_back(terms, values, gain, upstream, ready=(), cost=COST):
    count = len(terms)
    rows, width = values.shape
    steps = 4
    whole = pl.BlockSpec((rows // steps, width), lambda n: (n, 0))
    row = pl.BlockSpec((1, width), lambda n: (0, 0))
    return pl.pallas_call(
        after(functools.partial(norm_back_kernel, count), count + 3, len(ready)),
        grid=(steps,),
        in_specs=[whole] * (count + 1) + [row, whole] + [ANY] * len(ready),
        out_specs=(whole, whole, row),
        out_shape=(
            jax.ShapeDtypeStruct((rows, width), F32), jax.ShapeDtypeStruct((rows, width), BF16),
            jax.ShapeDtypeStruct((1, width), F32),
        ),
        compiler_params=BIG,
        cost_estimate=cost,
        name="norm_back",
    )(*terms, values, gain, upstream, *ready)


def split_rows(bit, value, send, keep):
    rows = send.shape[1]
    for j in range(2 * send.shape[0]):
        part = value[j * rows:(j + 1) * rows].astype(BF16)
        for to, same in ((send, False), (keep, True)):

            @pl.when((bit == j % 2) == same)
            def _(to=to, j=j, part=part):
                to[j // 2] = part


def down_kernel(bit, hidden, hidden_x, cot, cot_x, send, keep):
    split_rows(bit[0], dot1(hidden[...], cot[...], TN) + dot1(hidden_x[...], cot_x[...], TN), send, keep)


def down_weight_grad(bit, hidden, hidden_x, cot, half, shards, ready=()):
    tokens, feed = hidden.shape[0] // 2, hidden.shape[1]
    tile = 512
    shape = jax.ShapeDtypeStruct((shards // 2, feed // shards, half), BF16)
    out = pl.BlockSpec((shards // 2, feed // shards, tile), lambda n, b: (0, 0, n))
    return pl.pallas_call(
        after(down_kernel, 5, len(ready)),
        grid_spec=pltpu.PrefetchScalarGridSpec(
            num_scalar_prefetch=1,
            grid=(half // tile,),
            in_specs=[
                pl.BlockSpec((tokens, feed), lambda n, b: (0, 0)),
                pl.BlockSpec((tokens, feed), lambda n, b: (0, 0)),
                pl.BlockSpec((tokens, tile), lambda n, b: (0, n)),
                pl.BlockSpec((tokens, tile), lambda n, b: (1, n)),
            ] + [ANY] * len(ready),
            out_specs=(out, out),
        ),
        out_shape=(jax.ShapeDtypeStruct(shape.shape, BF16), shape),
        compiler_params=BIG,
        cost_estimate=COST,
        name="down_weight_grad",
    )(bit, hidden, hidden_x, cot, cot, *ready)


def blocks_of(v):
    return jnp.concatenate([v[:, j:j + HS] for j in range(0, v.shape[1], HS)], 0)


def other_grad_kernel(flip, bit, act, act_far, dz, dz_far, heads, other, grads, grads_x, send, keep, rows_out):
    steps = pl.num_programs(0)
    tokens = grads.shape[0]

    @pl.when(pl.program_id(0) == 0)
    def _():
        g, gx = grads[...], grads_x[...]
        own = dot1(heads[:tokens], g, TN) + dot1(heads[tokens:], gx, TN)
        away = dot1(other[tokens:], g, TN) + dot1(other[:tokens], gx, TN)
        rows_out[...] = jnp.concatenate([own, away], 0).astype(BF16)

    n = pl.program_id(0)
    half = steps // 2
    shard = (n % half) * 2 + jnp.where(n < half, 1 - bit[0], bit[0])
    size = rows_out.shape[0] // steps
    place = (shard + flip[0] * half) % steps
    part = rows_out[pl.ds(pl.multiple_of(place * size, size), size)]
    value = (dot1(act[...], dz[...], TN) + dot1(act_far[...], dz_far[...], TN)).astype(BF16)
    value = jnp.concatenate([blocks_of(value), blocks_of(part)], 0)
    pl.when(n < half)(lambda: send.__setitem__(0, value))
    pl.when(n >= half)(lambda: keep.__setitem__(0, value))


def other_grads(flip, bit, act, dz, dz_far, heads, other, grads, grads_x, columns, shards, ready=()):
    tokens, wide = dz.shape
    rows, half = columns // shards, shards // 2
    out_rows, out_wide = 2 * heads.shape[1], grads.shape[1]
    deep = rows * (wide // HS) + out_rows // shards * (out_wide // HS)

    def shard(n, b):
        return (n % half) * 2 + jnp.where(n < half, 1 - b[0], b[0])

    whole = lambda v: pl.BlockSpec(v.shape, lambda n, f, b: (0, 0))
    shape = jax.ShapeDtypeStruct((half, deep, HS), BF16)
    return pl.pallas_call(
        after(other_grad_kernel, 10, len(ready)),
        grid_spec=pltpu.PrefetchScalarGridSpec(
            num_scalar_prefetch=2,
            grid=(shards,),
            in_specs=[pl.BlockSpec((tokens, rows), lambda n, f, b, i=i: (i, shard(n, b))) for i in range(2)]
            + [whole(v) for v in (dz, dz_far, heads, other, grads, grads_x)] + [ANY] * len(ready),
            out_specs=(
                pl.BlockSpec((1, deep, HS), lambda n, f, b: (jnp.minimum(n, half - 1), 0, 0)),
                pl.BlockSpec((1, deep, HS), lambda n, f, b: (jnp.maximum(n - half, 0), 0, 0)),
            ),
            scratch_shapes=[pltpu.VMEM((out_rows, out_wide), BF16)],
        ),
        out_shape=(jax.ShapeDtypeStruct(shape.shape, BF16), shape),
        compiler_params=BIG,
        cost_estimate=COST,
        name="other_grads",
    )(flip, bit, act, act, dz, dz_far, heads, other, grads, grads_x, *ready)


def feed_kernel(parts, hidden, near, far, keep, send):
    size = hidden.shape[0] // parts

    def store(w):
        both = dot1(hidden[...], w[...])
        for k in range(0, parts, 2):
            keep[k // 2 * size:(k // 2 + 1) * size] = both[k * size:(k + 1) * size]
            send[k // 2 * size:(k // 2 + 1) * size] = both[(k + 1) * size:(k + 2) * size].astype(BF16)

    pl.when(pl.program_id(0) == 0)(lambda: store(near))
    pl.when(pl.program_id(0) == 1)(lambda: store(far))


def feed_product(hidden, near, far, parts, ready=()):
    tokens, half = hidden.shape[0] // 2, near.shape[1]
    whole = lambda v: pl.BlockSpec(v.shape, lambda n: (0, 0))
    return pl.pallas_call(
        after(functools.partial(feed_kernel, parts), 3, len(ready)),
        grid=(2,),
        in_specs=[pl.BlockSpec((tokens, hidden.shape[1]), lambda n: (0, 0)), whole(near), whole(far)] + [ANY] * len(ready),
        out_specs=(pl.BlockSpec((tokens // 2, half), lambda n: (0, n)),) * 2,
        out_shape=(jax.ShapeDtypeStruct((tokens // 2, 2 * half), F32), jax.ShapeDtypeStruct((tokens // 2, 2 * half), BF16)),
        compiler_params=BIG,
        cost_estimate=COST,
        name="feed_product",
    )(hidden, near, far, *ready)


def pair_kernel(kept, got, keep, send):
    size = keep.shape[0]
    keep[...] = kept[:size] + got[:size].astype(F32)
    send[...] = (kept[size:] + got[size:].astype(F32)).astype(BF16)


def pair_rows(kept, got, ready=()):
    rows, width = kept.shape
    return pl.pallas_call(
        after(pair_kernel, 2, len(ready)),
        in_specs=vm(2) + [ANY] * len(ready),
        out_specs=tuple(vm(2)),
        out_shape=(jax.ShapeDtypeStruct((rows // 2, width), F32), jax.ShapeDtypeStruct((rows // 2, width), BF16)),
        compiler_params=BIG,
        cost_estimate=COST,
        name="pair_rows",
    )(kept, got, *ready)


def split_row(v):
    hi = v.astype(BF16).astype(F32)
    return jnp.concatenate([hi, v - hi], 0)


def last_norm_kernel(count, *refs):
    terms, (values, gain, upstream, feed_part, head_part, out) = refs[:count], refs[count:]
    grads = terms[0][...]
    for term in terms[1:]:
        grads = grads + term[...].astype(F32)
    v = values[...].astype(F32)
    r = lax.rsqrt(jnp.mean(v * v, axis=1, keepdims=True) + EPSILON)
    normal = v * r
    scaled = gain[...] * grads
    rows, width = v.shape
    out[:rows] = (upstream[...] + r * (scaled - normal * jnp.mean(normal * scaled, axis=1, keepdims=True))).astype(BF16)
    part = jnp.sum(grads * normal, axis=0, keepdims=True)
    head = jnp.concatenate([head_part[...], jnp.zeros((1, width - HS), F32)], 1)
    extra = [split_row(part), split_row(feed_part[...]), split_row(head), jnp.zeros((10, width), F32)]
    out[rows:] = jnp.concatenate(extra, 0).astype(BF16)


def last_norm_back(terms, values, gain, upstream, feed_part, head_part, ready=()):
    count = len(terms)
    rows, width = values.shape
    return pl.pallas_call(
        after(functools.partial(last_norm_kernel, count), count + 5, len(ready)),
        in_specs=vm(count + 5) + [ANY] * len(ready),
        out_specs=vm(1)[0],
        out_shape=jax.ShapeDtypeStruct((rows + 16, width), BF16),
        compiler_params=BIG,
        cost_estimate=spent(4),
        name="last_norm_back",
    )(*terms, values, gain, upstream, feed_part, head_part, *ready)


def total_kernel(half_of, *refs):
    pieces, out = refs[:-1], refs[-1]
    half = out.shape[1] // 2
    count = len(pieces) // 2
    for h in range(2):
        own = sum(ref[...].astype(F32)[:, h * half:(h + 1) * half] for ref in pieces[:count])
        oth = sum(ref[...].astype(F32)[:, (1 - h) * half:(2 - h) * half] for ref in pieces[count:])
        total = own + oth
        out[:, pl.ds(pl.multiple_of(half_of[h] * half, half), half)] = jnp.concatenate(
            [total[n:n + 1] + total[n + 1:n + 2] for n in (0, 2)] + [jnp.zeros((6, half), F32)], 0)
    heads = sum(ref[...].astype(F32)[4:6, :HS] for ref in pieces)
    out[2:3, :HS] = heads[0:1] + heads[1:2]


def totals(half_of, own, partner, ready=()):
    rows, width = own[0].shape
    at = (rows - 16) // 16
    return pl.pallas_call(
        after(total_kernel, 1 + 2 * len(own), len(ready)),
        grid_spec=pltpu.PrefetchScalarGridSpec(
            num_scalar_prefetch=1,
            grid=(1,),
            in_specs=[pl.BlockSpec((16, width), lambda n, hf: (at, 0))] * (2 * len(own)) + [ANY] * len(ready),
            out_specs=pl.BlockSpec((8, width), lambda n, hf: (0, 0)),
        ),
        out_shape=jax.ShapeDtypeStruct((8, width), F32),
        compiler_params=BIG,
        cost_estimate=COST,
        name="totals",
    )(half_of, *own, *partner, *ready)


def sum_kernel(*refs):
    total = refs[0][...]
    for ref in refs[1:-1]:
        total = total + ref[...].astype(F32)
    refs[-1][...] = total.astype(BF16)


def sum_rows(terms, ready=()):
    return pl.pallas_call(
        after(sum_kernel, len(terms), len(ready)),
        in_specs=vm(len(terms)) + [ANY] * len(ready),
        out_specs=vm(1)[0],
        out_shape=jax.ShapeDtypeStruct(terms[0].shape, BF16),
        compiler_params=BIG,
        cost_estimate=COST,
        name="sum_rows",
    )(*terms, *ready)


def halve_kernel(bit, kept, got, send, keep):
    for out, i in ((send, 1 - bit[0]), (keep, bit[0])):
        out[...] = (kept[pl.ds(i, 1)].astype(F32) + got[pl.ds(i, 1)].astype(F32)).astype(BF16)


def halve(bit, kept, got, ready=()):
    shards, rows, columns = kept.shape
    pair = pl.BlockSpec((2, rows, columns), lambda n, b: (n, 0, 0))
    one = pl.BlockSpec((1, rows, columns), lambda n, b: (n, 0, 0))
    shape = jax.ShapeDtypeStruct((shards // 2, rows, columns), BF16)
    return pl.pallas_call(
        after(halve_kernel, 3, len(ready)),
        grid_spec=pltpu.PrefetchScalarGridSpec(
            num_scalar_prefetch=1, grid=(shards // 2,), in_specs=[pair, pair] + [ANY] * len(ready), out_specs=(one, one),
        ),
        out_shape=(jax.ShapeDtypeStruct(shape.shape, BF16), shape),
        compiler_params=BIG,
        cost_estimate=COST,
        name="halve",
    )(bit, kept, got, *ready)


def add_kernel(a, b, out):
    out[...] = a[...] + b[...]


def add(a, b, ready):
    return pl.pallas_call(
        after(add_kernel, 2, len(ready)),
        in_specs=vm(2) + [ANY] * len(ready),
        out_specs=vm(1)[0],
        out_shape=jax.ShapeDtypeStruct(a.shape, a.dtype),
        cost_estimate=COST,
        name="add",
    )(a, b, *ready)


def hold(v, ready):
    def kernel(v_ref, *refs):
        pass

    return pl.pallas_call(
        kernel,
        in_specs=[ANY] + [ANY] * len(ready),
        out_specs=ANY,
        out_shape=jax.ShapeDtypeStruct(v.shape, v.dtype),
        input_output_aliases={0: 0},
        cost_estimate=COST,
        name="hold",
    )(v, *ready)


def finish_kernel(kept, got, out, token):
    out[...] = kept[0].astype(F32) + got[0].astype(F32)
    token[...] = jnp.zeros_like(token)


def finish(kept, got, ready=()):
    _, rows, columns = kept.shape
    steps = 2 if rows % 32 == 0 else 1
    part = pl.BlockSpec((1, rows // steps, columns), lambda n: (0, n, 0))
    return pl.pallas_call(
        after(finish_kernel, 2, len(ready)),
        grid=(steps,),
        in_specs=[part, part] + [ANY] * len(ready),
        out_specs=(pl.BlockSpec((rows // steps, columns), lambda n: (n, 0)), pl.BlockSpec((8, HS), lambda n: (0, 0))),
        out_shape=(jax.ShapeDtypeStruct((rows, columns), F32), jax.ShapeDtypeStruct((8, HS), F32)),
        compiler_params=BIG,
        cost_estimate=COST,
        name="finish",
    )(kept, got, *ready)


def finish_small_kernel(gains, share, group, small, got, mixer, feed, head, *taps):
    i = group[0]
    total = small[...] + got[...]
    per, steps = gains // HS, mixer.shape[0]
    mixer[...] = sum(jnp.where(i == n, total[n * steps:(n + 1) * steps], 0.0) for n in range(per // steps))
    feed[...] = sum(jnp.where(i == n, total[per + n * steps:per + (n + 1) * steps], 0.0) for n in range(per // steps))
    head[...] = total[2 * per:2 * per + 1]
    tiles = share * (per // steps) // HS
    for which, out in enumerate(taps):
        rows = []
        for t in range(out.shape[0]):
            at = 3 * per + (t * len(taps) + which) * tiles
            rows.append(sum(
                jnp.where(i == n, total[at + n * share // HS:at + n * share // HS + 1, n * share % HS:n * share % HS + share], 0.0)
                for n in range(per // steps)
            ))
        out[...] = jnp.concatenate(rows, 0)


def finish_small(group, small, got, gains, tap_shape, shares, ready=()):
    taps, wide = tap_shape
    share = wide // 3 // shares
    shapes = [(gains // HS // shares, HS)] * 2 + [(1, HS)] + [(taps, share)] * 3
    return pl.pallas_call(
        after(functools.partial(finish_small_kernel, gains, share), 3, len(ready)),
        in_specs=[SMEM] + vm(2) + [ANY] * len(ready),
        out_specs=tuple(vm(6)),
        out_shape=tuple(jax.ShapeDtypeStruct(shape, F32) for shape in shapes),
        compiler_params=BIG,
        cost_estimate=COST,
        name="finish_small",
    )(group, small, got, *ready)


def finish_pair_kernel(col, own_kept, own_got, oth_kept, oth_got, *outs):
    own = own_kept[0].astype(F32) + own_got[0].astype(F32)
    oth = oth_kept[0].astype(F32) + oth_got[0].astype(F32)
    rows, wide = own.shape
    width = outs[0].shape[1] // 2
    blocks = wide // HS
    rest = oth[blocks * rows:]
    oth = jnp.concatenate([oth[j * rows:(j + 1) * rows] for j in range(blocks)], 1)
    for n, out in enumerate(outs[:3]):
        for i, v in ((col[0], own), (1 - col[0], oth)):
            out[:, pl.ds(pl.multiple_of(i * width, width), width)] = v[:, n * width:(n + 1) * width]
    outs[3][...] = own[:, 3 * width:] + oth[:, 3 * width:]
    size = outs[4].shape[0]
    outs[4][...] = jnp.concatenate([rest[j * size:(j + 1) * size] for j in range(rest.shape[0] // size)], 1)


def finish_pair(col, own_kept, own_got, oth_kept, oth_got, width, out_rows, ready=()):
    _, rows, columns = own_kept.shape
    blocks = (oth_kept.shape[1] - rows * (columns // HS)) // out_rows
    shapes = [(rows, 2 * width)] * 3 + [(rows, columns - 3 * width), (out_rows, blocks * HS)]
    return pl.pallas_call(
        after(finish_pair_kernel, 5, len(ready)),
        in_specs=[SMEM] + vm(4) + [ANY] * len(ready),
        out_specs=tuple(vm(5)),
        out_shape=tuple(jax.ShapeDtypeStruct(shape, F32) for shape in shapes),
        compiler_params=BIG,
        cost_estimate=COST,
        name="finish_pair",
    )(col, own_kept, own_got, oth_kept, oth_got, *ready)


def mm(left, right, dims=NN):
    return lax.dot_general(left, right, dims, preferred_element_type=F32)


def body(
    inputs, segments, mixer_gain, w_query, w_key, w_value, w_beta, conv_query, conv_key, conv_value,
    head_gain, w_out, feed_gain, w_gate, w_up, w_down, cotangent,
):
    cols, rows, groups = lax.axis_size("col"), lax.axis_size("row"), lax.axis_size("dp")
    c, r, g = lax.axis_index("col"), lax.axis_index("row"), lax.axis_index("dp")
    tokens, width = inputs.shape
    half, mine = width // cols, tokens // cols
    own_width = conv_query.shape[0]
    feed = w_gate.shape[1]

    def swap(v):
        return lax.ppermute(v, "col", [(i, i ^ 1) for i in range(cols)])

    def to_row(v, k):
        return lax.ppermute(v, "row", [(i, i ^ k) for i in range(rows)])

    def row_terms(blocks):
        return [blocks[0]] + [to_row(blocks[k], k) for k in range(rows - 1, 0, -1)]

    def row_gather(own):
        return [own] + [to_row(own, k) for k in range(1, rows)]

    def own_first(v, axis=-1):
        size = v.shape[axis] // 2
        return jnp.concatenate([lax.dynamic_slice_in_dim(v, i * size, size, axis) for i in (c, 1 - c)], axis)

    def halves(v, bit):
        parts = v.reshape(v.shape[0] // 2, 2, *v.shape[1:])
        return [lax.dynamic_index_in_dim(parts, i, 1, keepdims=False) for i in (1 - bit, bit)]

    def traded(v, step):
        return lax.ppermute(v, "dp", [(i, i ^ step) for i in range(groups)])

    def group_steps(pair, got, ready):
        step = 1
        while step * 2 < groups:
            got = got if step == 1 else traded(pair[0], step)
            step *= 2
            pair = halve(((g // step) % 2).astype(jnp.int32)[None], pair[1], got, ready)
        return pair

    def shards_of(v):
        return halves(v.astype(BF16).reshape(groups, -1, v.shape[-1]), g % 2)

    def grads_of(lefts, rights, pairs, columns, ready):
        if columns // groups % 128 == 0:
            return weight_grad(low_bit, lefts, rights, pairs, mine, columns, groups, ready)

        def rows_of(v, i):
            return v[i * mine:(i + 1) * mine]

        return shards_of(jnp.concatenate([
            sum(mm(rows_of(*lefts[i])[:, :columns], rows_of(*rights[j]), TN) for i, j in enumerate(js)) for js in zip(*pairs)
        ], 1))

    def all_sum(v):
        v = v + swap(v)
        k = 1
        while k < rows:
            v = v + to_row(v, k)
            k *= 2
        k = 1
        while k < groups:
            v = v + lax.ppermute(v, "dp", [(i, i ^ k) for i in range(groups)])
            k *= 2
        return v

    order = jnp.arange(cols * rows, dtype=jnp.int32)
    chunk_of = ((order % rows) ^ r) * cols + ((order // rows) ^ c)
    place_of = ((order % cols) ^ c) * rows + ((order // cols) ^ r)
    half_of = jnp.stack([c, 1 - c]).astype(jnp.int32)
    place_of = jnp.concatenate([place_of, half_of[:1]])
    low_bit = (g % 2).astype(jnp.int32)[None]
    documents = (segments + (jnp.arange(segments.shape[0], dtype=jnp.int32) * segments.shape[1])[:, None]).reshape(-1)
    doc_col = jnp.pad(documents, (8, 8), constant_values=-1)[:, None]
    doc_row = documents.reshape(-1, CH)
    taps = jnp.concatenate([conv_query.T, conv_key.T, conv_value.T], 1)
    gain_row = head_gain[None]
    gain_one, gain_two = own_first(mixer_gain)[None], own_first(feed_gain)[None]

    w_beta_wide = jnp.pad(w_beta, ((0, 0), (0, HS - w_beta.shape[1])))

    def columns(i):
        parts = [lax.dynamic_slice_in_dim(w, i * own_width, own_width, 1) for w in (w_query, w_key, w_value)]
        return jnp.concatenate(parts + [w_beta_wide], 1)

    w_own, w_oth = columns(c), columns(1 - c)
    w_own_x = swap(w_oth)
    act = ordered(norm_kernel, chunk_of, half_of, inputs, gain_one)
    z = mm(act[:, :half], w_own) + mm(act[:, half:], w_own_x)
    heads, *saved = delta_forward(place_of, z, taps, doc_col, doc_row, gain_row)
    w_out_x, w_gate_x, w_up_x, w_down_x, w_oth_x = swap(w_out), swap(w_gate), swap(w_up), swap(w_down), swap(w_own)
    col = half_of[:1]

    last = groups // 2
    heads_x = swap(heads)
    attended = row_terms(out_product(col, heads, heads_x, w_out, w_out_x, rows, (w_gate_x, w_up_x, w_down_x, w_oth_x)))
    cot = ordered(copy_kernel, chunk_of, half_of, cotangent, ready=attended[:1])
    d_hidden = mm(cot[:mine, :half], w_down, NT) + mm(cot[:mine, half:], w_down_x, NT)
    middle, act_two, x_own = middle_rows(chunk_of, half_of, attended, inputs, gain_two, (d_hidden, cot))

    act_two = row_gather(act_two)
    d_gate, feeds, act_near, act_far = swiglu(act_two, w_gate, w_gate_x, w_up, w_up_x, d_hidden)
    act_x, d_gate_x = swap(act_far), swap(d_gate)
    feeds_x = swap(hold(feeds, (act_x, d_gate_x)))
    act_pair = [(act_near, 0), (act_x, 0)]
    gate_grad = grads_of(act_pair, [(d_gate, 0), (d_gate_x, 0)], [(0,), (1,)], half, ())
    gate_got = traded(gate_grad[0], 1)
    d_act_two = row_terms(back([(d_gate, 0), (feeds, 1)], [w_gate, w_up], [w_gate_x, w_up_x], rows, mine, gate_grad[:1]))
    up_grad = grads_of(act_pair, [(feeds, 1), (feeds_x, 1)], [(0,), (1,)], half, d_act_two[:1])
    up_got = traded(up_grad[0], 1)
    feed_keep, feed_send = feed_product(feeds, w_down, w_down_x, rows, up_grad[:1])
    gate_grad = group_steps(gate_grad, gate_got, (feed_send,))
    gate_got = traded(gate_grad[0], last)
    d_middle, d_att, feed_part = norm_back(d_act_two, middle, gain_two, cot, gate_grad[:1], cost=spent(4))

    down_grad = down_weight_grad(low_bit, feeds, feeds_x, cot, half, groups, (d_att,))
    down_got = traded(down_grad[0], 1)
    up_grad = group_steps(up_grad, up_got, down_grad[:1])
    up_got = traded(up_grad[0], last)
    d_heads, d_heads_x, d_att_near, d_att_x = head_grad(
        col, row_gather(d_att), w_out, w_out_x, own_width, (up_grad[0], gate_got)
    )
    d_heads_x, d_att_x = swap(d_heads_x), swap(d_att_x)
    feed_got = to_row(feed_send, 1)
    dz, dz_far, d_taps, head_part = delta_backward(
        place_of, d_heads, d_heads_x, z, taps, doc_col, doc_row, gain_row, saved, (d_att_x,)
    )

    feed_keep, feed_send = pair_rows(feed_keep, feed_got, (dz_far, up_got))
    feed_got = to_row(feed_send, 2)
    dz_x, dz_far_x = swap(dz_far), swap(dz)
    act_pair = [(act, 0), (act, 1)]
    grad_own = grads_of(act_pair, [(dz, 0), (dz_far, 0)], [(0,), (1,)], half, (feed_send,))
    own_got = traded(grad_own[0], 1)
    d_act = row_terms(back(
        [(dz, 0), (dz_x, 0)], [w_own, w_oth], [w_own_x, w_oth_x], rows, mine, (grad_own[0], feed_got, dz_far_x), spent(2)
    ))
    down_grad = group_steps(down_grad, down_got, d_act[:1])
    down_got = traded(down_grad[0], last)
    if half // groups % 128 == 0:
        grad_oth = other_grads(
            col, low_bit, act, dz_x, dz_far_x, heads, heads_x, d_att_near, d_att_x, half, groups, down_grad[:1]
        )
    else:
        def shard_blocks(v):
            v = v.reshape(groups, v.shape[0] // groups, v.shape[1] // HS, HS)
            return jnp.swapaxes(v, 1, 2).reshape(groups, -1, HS)

        projected = mm(act[:mine, :half], dz_x, TN) + mm(act[mine:, :half], dz_far_x, TN)
        first = mm(heads[:mine], d_att_near, TN) + mm(heads[mine:], d_att_x, TN)
        second = mm(heads_x[mine:], d_att_near, TN) + mm(heads_x[:mine], d_att_x, TN)
        outs = jnp.where(c == 0, jnp.concatenate([first, second], 0), jnp.concatenate([second, first], 0))
        grad_oth = halves(jnp.concatenate([shard_blocks(projected), shard_blocks(outs)], 1).astype(BF16), g % 2)
    oth_got = traded(grad_oth[0], 1)
    gate_grad, token = finish(gate_grad[1], gate_got, grad_oth[:1])
    up_grad, token = finish(up_grad[1], up_got, (token,))
    grad_own = group_steps(grad_own, own_got, (token,))
    own_got = traded(grad_own[0], last)
    output = sum_rows([middle, feed_keep, feed_got], grad_own[:1])
    input_grad = last_norm_back(d_act, x_own, gain_one, d_middle, feed_part, head_part, (output, down_got))

    input_grad = row_gather(input_grad)
    grad_oth = group_steps(grad_oth, oth_got, (own_got,))
    oth_got = traded(grad_oth[0], last)
    input_grad_x = [swap(v) for v in input_grad]
    placed, token = place(chunk_of, half_of, input_grad, None, (grad_oth[0],))
    small = totals(half_of, input_grad, input_grad_x, (token,))
    output = row_gather(hold(output, (input_grad[1],)))
    input_grad, token = place(chunk_of, half_of, input_grad_x, placed, (small,))
    small = hold(jnp.concatenate([small[:3].reshape(-1), d_taps.reshape(-1)]).reshape(-1, HS), (token,))
    k = 1
    while 2 * k < groups:
        small = add(small, traded(small, k), ())
        k *= 2
    small_got = traded(small, last)
    down_grad, token = finish(down_grad[1], down_got, (token,))
    output[0] = hold(output[0], (token,))
    output_x = [swap(v) for v in output]
    placed, token = place(chunk_of, half_of, output, None, (token,))
    output, token = place(chunk_of, half_of, output_x, placed, (token,))
    *projections, beta_grad, out_grad = finish_pair(
        col, grad_own[1], own_got, grad_oth[1], oth_got, own_width, w_out.shape[0] // groups, (token,)
    )
    mixer_gain_grad, feed_gain_grad, head_gain_grad, *conv_grads = finish_small(
        g.astype(jnp.int32)[None], small, small_got, width, d_taps.shape, groups, (beta_grad,)
    )
    beta_grad = beta_grad[:, :w_beta.shape[1]]
    mixer_gain_grad, feed_gain_grad, head_gain_grad = (
        v.reshape(-1) for v in (mixer_gain_grad, feed_gain_grad, head_gain_grad)
    )
    conv_grads = [v.T for v in conv_grads]
    return (
        output, input_grad, mixer_gain_grad, *projections, beta_grad, *conv_grads,
        head_gain_grad, out_grad, feed_gain_grad, gate_grad, up_grad, down_grad,
    )


def solution(mesh):
    weight, swapped = P("col", "row"), P("row", "col")
    taps = P(("row", "col"), None)
    grad, grad_taps = P(("col", "dp"), "row"), P(("row", "col", "dp"), None)
    grad_swapped = P(("row", "dp"), "col")
    tokens = P("dp", None)
    return jax.shard_map(
        body,
        mesh=mesh,
        in_specs=(
            tokens, tokens, P(), weight, weight, weight, weight, taps, taps, taps, P(), swapped, P(), weight, weight,
            swapped, tokens,
        ),
        out_specs=(
            tokens, tokens, P("dp"), grad, grad, grad, grad, grad_taps, grad_taps, grad_taps, P(), grad_swapped, P("dp"),
            grad, grad, grad_swapped,
        ),
        check_vma=False,
    )
```

```python
import functools
import jax
import jax.numpy as jnp
from jax import lax
from jax.experimental import pallas as pl
from jax.experimental.pallas import tpu as pltpu
from jax.sharding import PartitionSpec as P

EPSILON = 1e-06
HEAD_FLOOR = 0.02
CH = 128
HS = 128
F32 = jnp.float32
BF16 = jnp.bfloat16

NN = (((1,), (0,)), ((), ()))
NT = (((1,), (1,)), ((), ()))
TN = (((0,), (0,)), ((), ()))


def dot1(a, b, dims=NN):
    return lax.dot_general(a.astype(BF16), b.astype(BF16), dims, preferred_element_type=F32)


def split(a):
    hi = a.astype(BF16)
    return hi, (a - hi.astype(F32)).astype(BF16)


def dot3s(a, b, dims=NN):
    (ah, al), (bh, bl) = a, b
    ka, kb = dims[0][0][0], dims[0][1][0]
    left = jnp.concatenate([ah, al], ka)
    right = jnp.concatenate([jnp.concatenate([bh, bl], 1 - kb), jnp.concatenate([bh, jnp.zeros_like(bh)], 1 - kb)], kb)
    both = lax.dot_general(left, right, dims, preferred_element_type=F32)
    width = both.shape[1] // 2
    return both[:, :width] + both[:, width:]


def dot3(a, b, dims=NN):
    return dot3s(split(a), split(b), dims)


def silu_parts(z):
    s = 1.0 / (1.0 + jnp.exp(-z))
    return s, z * s


def together(steps):
    steps = list(steps)
    while steps:
        steps = [step for step in steps if next(step, steps) is not steps]


def unit_inverse(low, xor, eye, dot):
    inv = eye - jnp.where(xor < 2, low, 0.0)
    low16 = low.astype(BF16)
    size = 2
    while size < CH:
        part = jnp.where((xor >= size) & (xor < 2 * size), low, 0.0).astype(BF16)
        inv16 = inv.astype(BF16)
        half = dot1(inv16, part)
        yield
        inv = inv - dot1(half, inv16)
        yield
        size *= 2
    parts = split(inv)
    rest = (eye - inv) - dot3s(split(low), parts)
    yield
    return inv + dot3s(parts, split(rest))


def window(ref, c, cols):
    return ref[pl.ds(pl.multiple_of(c * CH, CH), CH + 8), cols]


def conv_chunk(win, taps, masks):
    out = win[8:] * taps[3]
    for j in (1, 2, 3):
        out = out + masks[j - 1] * pltpu.roll(win, j, 0)[8:] * taps[3 - j]
    return out


def chunk_docs(doc_col, doc_row, c):
    col = doc_col[pl.ds(pl.multiple_of(c * CH + 8, 8), CH), :]
    row = doc_row[pl.ds(c, 1), :]
    prev = doc_col[pl.ds(pl.multiple_of(c * CH, 8), 8), :][7:8]
    last = col[CH - 1:CH]
    return col, row, prev, last


def place_rows(place, c):
    return pl.ds(pl.multiple_of(place[c] * CH, CH), CH)


def own_beta(lanes, column, heads, h):
    return jnp.where(column == 0, lanes[:, h:h + 1], lanes[:, heads + h:heads + h + 1])


def fill_pad(pad, place, z_ref, chunks, width):
    pad[0:8] = jnp.zeros((8, 3 * width), F32)
    for c in range(chunks):
        pad[c * CH + 8:(c + 1) * CH + 8] = z_ref[place_rows(place, c), :3 * width]


def fwd_kernel(heads, chunks, dotg, doti, dot,
               place, z_ref, taps_ref, doc_col, doc_row, gain_ref,
               out_ref, mixed_ref, conv_ref, t_ref, h_ref, a_ref, qt_ref, w_ref, u_ref,
               pad, pu_s, b_s):
    width = heads * HS
    fill_pad(pad, place, z_ref, chunks, width)
    row_i = lax.broadcasted_iota(jnp.int32, (CH, CH), 0)
    col_i = lax.broadcasted_iota(jnp.int32, (CH, CH), 1)
    xor = row_i ^ col_i
    eye = (xor == 0).astype(F32)

    def one(c, h):
        col, row, prev, last = chunk_docs(doc_col, doc_row, c)
        same = col == row
        strict = same & (row_i > col_i)
        incl = same & (row_i >= col_i)
        carried = (col == prev).astype(F32)
        closing = (col == last).astype(F32)
        keep = (last == prev).astype(F32)
        dwin = doc_col[pl.ds(pl.multiple_of(c * CH, CH), CH + 8), :]
        masks = [(dwin[8 - j:CH + 8 - j] == col).astype(F32) for j in (1, 2, 3)]

        def conv(which):
            cols = slice(which * width + h * HS, which * width + (h + 1) * HS)
            taps = [taps_ref[t:t + 1, cols] for t in range(4)]
            z = conv_chunk(window(pad, c, cols), taps, masks)
            conv_ref[pl.ds(pl.multiple_of(c * CH, CH), CH), cols] = z
            return silu_parts(z)[1]

        q, k, v = conv(0), conv(1), conv(2)
        k = k * lax.rsqrt(jnp.sum(k * k, axis=1, keepdims=True) + EPSILON)
        beta = 1.0 / (1.0 + jnp.exp(-own_beta(z_ref[place_rows(place, c), 3 * width:], place[chunks], heads, h)))
        yield
        gram = dotg(k, k, NT)
        yield
        low = jnp.where(strict, beta * gram, 0.0)
        yield
        inv = yield from unit_inverse(low, xor, eye, doti)
        yield
        wu = dot(inv, jnp.concatenate([(carried * beta) * k, beta * v], 1))
        w, u = wu[:, :HS], wu[:, HS:]
        yield
        p = jnp.where(incl, dot(q, k, NT), 0.0)
        yield
        wus = split(wu)
        pwu = dot3s(split(p), wus)
        qt = carried * q - pwu[:, :HS]
        pu = pwu[:, HS:]
        yield
        kcl = closing * k
        ab = dot3s(split(kcl), wus, TN)
        a = keep * eye - ab[:, :HS]
        b = ab[:, HS:]
        yield
        i = c * heads + h
        t_ref[i] = inv
        qt_ref[i] = qt
        a_ref[i] = a
        w_ref[i] = w
        u_ref[i] = u
        pu_s[i] = pu
        b_s[i] = b

    per = 4

    def phase_one(g, carry):
        together(one(g * per + e, h) for e in range(per) for h in range(heads))
        return carry

    lax.fori_loop(0, chunks // per, phase_one, 0)

    def phase_two(c, state):
        new = []
        for h in range(heads):
            i = c * heads + h
            h_ref[i] = state[h]
            new.append(dot(a_ref[i], state[h]) + b_s[i])
        return tuple(new)

    lax.fori_loop(0, chunks, phase_two, tuple(jnp.zeros((HS, HS), F32) for _ in range(heads)))

    def phase_three(c, carry):
        for h in range(heads):
            i = c * heads + h
            rows = pl.ds(pl.multiple_of(c * CH, CH), CH)
            cols = slice(h * HS, (h + 1) * HS)
            mixed = dot(qt_ref[i], h_ref[i]) + pu_s[i]
            mixed_ref[rows, cols] = mixed
            r = lax.rsqrt(jnp.mean(mixed * mixed, axis=1, keepdims=True) + HEAD_FLOOR)
            out_ref[place_rows(place, c), cols] = (mixed * r * gain_ref[...]).astype(BF16)
        return carry

    lax.fori_loop(0, chunks, phase_three, 0)


def vm(n):
    return [pl.BlockSpec(memory_space=pltpu.VMEM)] * n


def spent(us):
    return pl.CostEstimate(flops=int(us * 1_150_000_000), bytes_accessed=1000, transcendentals=0)


COST = pl.CostEstimate(flops=1000, bytes_accessed=1000, transcendentals=0)
SMEM = pl.BlockSpec(memory_space=pltpu.SMEM)
ANY = pl.BlockSpec(memory_space=pl.ANY)


def after(kernel, count, extra):
    return lambda *refs: kernel(*refs[:count], *refs[count + extra:])


def delta_forward(place, z, taps, doc_col, doc_row, gain, dots=(dot3, dot3, dot3)):
    tokens, width = z.shape[0], taps.shape[1] // 3
    heads = width // HS
    chunks = tokens // CH
    n = chunks * heads
    sq = jax.ShapeDtypeStruct((n, CH, HS), F32)
    return pl.pallas_call(
        functools.partial(fwd_kernel, heads, chunks, *dots),
        out_shape=(jax.ShapeDtypeStruct((tokens, width), BF16), jax.ShapeDtypeStruct((tokens, width), F32),
                   jax.ShapeDtypeStruct((tokens, 3 * width), F32), sq, sq, sq, sq, sq, sq),
        in_specs=[SMEM] + vm(5), out_specs=tuple(vm(9)),
        scratch_shapes=[pltpu.VMEM((tokens + 8, 3 * width), F32), pltpu.VMEM((n, CH, HS), F32), pltpu.VMEM((n, CH, HS), F32)],
        compiler_params=pltpu.CompilerParams(vmem_limit_bytes=48 * 1024 * 1024),
        cost_estimate=COST,
        name="delta_forward",
    )(place, z, taps, doc_col, doc_row, gain)


def bwd_kernel(heads, chunks, dotg, dot,
               place, dh_own, dh_other, z_ref, taps_ref, doc_col, doc_row, gain_ref,
               mixed_ref, conv_ref, t_ref, h_ref, a_ref, qt_ref, w_ref, u_ref,
               dz_own, dz_other, dtaps_ref, dgain_ref,
               dz_ref, dh_ref, do_s, eb_s, e_s, dc_s, db_s):
    width = heads * HS
    tokens = chunks * CH
    dh_ref[:tokens // 2] = dh_own[...]
    dh_ref[tokens // 2:] = dh_other[...]
    dc_s[tokens:] = jnp.zeros((8, 3 * width), F32)
    row_i = lax.broadcasted_iota(jnp.int32, (CH, CH), 0)
    col_i = lax.broadcasted_iota(jnp.int32, (CH, CH), 1)

    def rows_of(c):
        return pl.ds(pl.multiple_of(c * CH, CH), CH)

    def phase_one(c, total):
        for h in range(heads):
            i = c * heads + h
            cols = slice(h * HS, (h + 1) * HS)
            m = mixed_ref[rows_of(c), cols]
            dy = dh_ref[place_rows(place, c), cols].astype(F32)
            r = lax.rsqrt(jnp.mean(m * m, axis=1, keepdims=True) + HEAD_FLOOR)
            mr = m * r
            total = total + jnp.sum(dy * mr, axis=0, keepdims=True)
            gy = gain_ref[...] * dy
            dm = r * (gy - mr * jnp.mean(mr * gy, axis=1, keepdims=True))
            do_s[i] = dm
            eb_s[i] = dot(qt_ref[i], dm, TN)
        return total

    dgain_ref[...] = lax.fori_loop(0, chunks, phase_one, jnp.zeros((1, HS), F32))

    def phase_two(n, state):
        c = chunks - 1 - n
        new = []
        for h in range(heads):
            i = c * heads + h
            e_s[i] = state[h]
            new.append(dot(a_ref[i], state[h], TN) + eb_s[i])
        return tuple(new)

    lax.fori_loop(0, chunks, phase_two, tuple(jnp.zeros((HS, HS), F32) for _ in range(heads)))

    def one(c, h):
        i = c * heads + h
        col, row, prev, last = chunk_docs(doc_col, doc_row, c)
        same = col == row
        strict = same & (row_i > col_i)
        incl = same & (row_i >= col_i)
        carried = (col == prev).astype(F32)
        closing = (col == last).astype(F32)

        def conv(which):
            s, y = silu_parts(conv_ref[rows_of(c), which * width + h * HS:which * width + (h + 1) * HS])
            return y, s + y * (1.0 - s)

        q, q_slope = conv(0)
        k, k_slope = conv(1)
        v, v_slope = conv(2)
        n = lax.rsqrt(jnp.sum(k * k, axis=1, keepdims=True) + EPSILON)
        k = k * n
        beta = 1.0 / (1.0 + jnp.exp(-own_beta(z_ref[place_rows(place, c), 3 * width:], place[chunks], heads, h)))
        inv, state, w, u, dm, e = t_ref[i], h_ref[i], w_ref[i], u_ref[i], do_s[i], e_s[i]
        yield
        gram = dotg(k, k, NT)
        yield
        p = jnp.where(incl, dot(q, k, NT), 0.0)
        yield
        r = u - dot(w, state)
        yield
        y = v - carried * dot(k, state)
        yield
        dr = dot(p, dm, TN) + closing * dot(k, e)
        yield
        x = dot(inv, dr, TN)
        yield
        dp = jnp.where(incl, dot(dm, r, NT), 0.0)
        yield
        dq = dot(dp, k) + carried * dot(dm, state, NT)
        yield
        dlow = jnp.where(strict, -dot(x, r, NT), 0.0)
        dgram = beta * dlow
        yield
        dk = closing * dot(r, e, NT) + dot(dp, q, TN)
        yield
        dk = dk + dot(dgram, k) + dot(dgram, k, TN)
        yield
        dk = dk - (carried * beta) * dot(x, state, NT)
        yield
        dbeta = jnp.sum(dlow * gram, axis=1, keepdims=True) + jnp.sum(x * y, axis=1, keepdims=True)
        dk = n * (dk - k * jnp.sum(k * dk, axis=1, keepdims=True))
        for which, value in ((0, dq * q_slope), (1, dk * k_slope), (2, beta * x * v_slope)):
            dc_s[rows_of(c), which * width + h * HS:which * width + (h + 1) * HS] = value
        db_s[h, rows_of(c)] = dbeta * beta * (1.0 - beta)

    per = 4

    def phase_three(g, carry):
        together(one(g * per + e, h) for e in range(per) for h in range(heads))
        return carry

    lax.fori_loop(0, chunks // per, phase_three, 0)

    def phase_four(c, sums):
        col = doc_col[pl.ds(pl.multiple_of(c * CH + 8, 8), CH), :]
        after = doc_col[pl.ds(pl.multiple_of(c * CH + 8, 8), CH + 8), :]
        later = [jnp.broadcast_to((after[j:CH + j] == col).astype(F32), (CH, HS)) for j in (1, 2, 3)]
        new = []
        for b in range(3 * heads):
            cols = slice(b * HS, (b + 1) * HS)
            z = z_ref[place_rows(place, c), cols]
            win = dc_s[pl.ds(pl.multiple_of(c * CH, CH), CH + 8), cols]
            dz = 0.0
            for j in range(4):
                d = win[:CH] if j == 0 else later[j - 1] * pltpu.roll(win, CH + 8 - j, 0)[:CH]
                dz = dz + d * taps_ref[3 - j:4 - j, cols]
                new.append(sums[4 * b + j] + jnp.sum((d * z).reshape(CH // 8, 8, HS), axis=0))
            dz_ref[place_rows(place, c), cols] = dz.astype(BF16)
        lane = lax.broadcasted_iota(jnp.int32, (CH, HS), 1) - place[chunks] * heads
        betas = sum(jnp.where(lane == h, db_s[h, rows_of(c)], 0.0) for h in range(heads))
        dz_ref[place_rows(place, c), 3 * width:] = betas.astype(BF16)
        return tuple(new)

    sums = lax.fori_loop(0, chunks, phase_four, tuple(jnp.zeros((8, HS), F32) for _ in range(12 * heads)))
    for b in range(3 * heads):
        for j in range(4):
            dtaps_ref[3 - j:4 - j, b * HS:(b + 1) * HS] = jnp.sum(sums[4 * b + j], axis=0, keepdims=True)
    dz_own[...] = dz_ref[:tokens // 2]
    dz_other[...] = dz_ref[tokens // 2:]


def delta_backward(place, own, other, z, taps, doc_col, doc_row, gain, saved, ready=(), dots=(dot3, dot3)):
    tokens, width = z.shape[0], taps.shape[1] // 3
    heads = width // HS
    chunks = tokens // CH
    n = chunks * heads
    sq = pltpu.VMEM((n, CH, HS), F32)
    return pl.pallas_call(
        after(functools.partial(bwd_kernel, heads, chunks, *dots), 16, len(ready)),
        out_shape=(jax.ShapeDtypeStruct((tokens // 2, z.shape[1]), BF16), jax.ShapeDtypeStruct((tokens // 2, z.shape[1]), BF16),
                   jax.ShapeDtypeStruct((4, 3 * width), F32),
                   jax.ShapeDtypeStruct((1, HS), F32)),
        in_specs=[SMEM] + vm(15) + [ANY] * len(ready), out_specs=tuple(vm(4)),
        scratch_shapes=[pltpu.VMEM(z.shape, BF16), pltpu.VMEM((tokens, width), BF16), sq, sq, sq, pltpu.VMEM((tokens + 8, 3 * width), F32),
                        pltpu.VMEM((heads, tokens, 1), F32)],
        compiler_params=pltpu.CompilerParams(vmem_limit_bytes=48 * 1024 * 1024),
        cost_estimate=COST,
        name="delta_backward",
    )(place, own, other, z, taps, doc_col, doc_row, gain, *saved, *ready)


def norm_kernel(chunk_of, half_of, a_ref, b_ref, gain_ref, out_ref):
    half = a_ref.shape[1]
    a, b = a_ref[...].astype(F32), b_ref[...].astype(F32)
    total = jnp.sum(a * a, axis=1, keepdims=True) + jnp.sum(b * b, axis=1, keepdims=True)
    r = lax.rsqrt(total / (2 * half) + EPSILON)
    out_ref[:, :half] = (a * r * gain_ref[:, :half]).astype(BF16)
    out_ref[:, half:] = (b * r * gain_ref[:, half:]).astype(BF16)


def copy_kernel(chunk_of, half_of, a_ref, b_ref, out_ref):
    half = a_ref.shape[1]
    out_ref[:, :half] = a_ref[...]
    out_ref[:, half:] = b_ref[...]


def ordered(kernel, chunk_of, half_of, x, *rest, ready=()):
    tokens, width = x.shape
    half = width // 2
    return pl.pallas_call(
        after(kernel, 4 + len(rest), len(ready)),
        grid_spec=pltpu.PrefetchScalarGridSpec(
            num_scalar_prefetch=2,
            grid=(tokens // CH,),
            in_specs=[
                pl.BlockSpec((CH, half), lambda p, ch, hf: (ch[p], hf[0])),
                pl.BlockSpec((CH, half), lambda p, ch, hf: (ch[p], hf[1])),
            ] + [pl.BlockSpec((1, width), lambda p, ch, hf: (0, 0)) for _ in rest] + [ANY] * len(ready),
            out_specs=pl.BlockSpec((CH, width), lambda p, ch, hf: (p, 0)),
        ),
        out_shape=jax.ShapeDtypeStruct((tokens, width), BF16),
        compiler_params=pltpu.CompilerParams(vmem_limit_bytes=32 * 1024 * 1024),
        cost_estimate=COST,
        name="ordered_rows",
    )(chunk_of, half_of, x, x, *rest, *ready)


def place_kernel(count, first, chunk_of, half_of, *refs):
    out, token = refs[-2:]
    half = out.shape[1] // 2
    token[...] = jnp.zeros_like(token)
    for p in range(count):

        @pl.when(pl.program_id(0) == p)
        def _(p=p):
            for h in range(2):
                to = half_of[h] if first == 0 else half_of[1 - h]
                out[:, pl.ds(pl.multiple_of(to * half, half), half)] = refs[p][:, h * half:(h + 1) * half]


def place(chunk_of, half_of, pieces, rest=None, ready=()):
    count = len(pieces)
    rows, width = CH, pieces[0].shape[1]
    first = 0 if rest is None else count
    extra = () if rest is None else (rest,)
    return pl.pallas_call(
        after(functools.partial(place_kernel, count, first), 2 + count, len(extra) + len(ready)),
        grid_spec=pltpu.PrefetchScalarGridSpec(
            num_scalar_prefetch=2,
            grid=(count,),
            in_specs=[pl.BlockSpec((rows, width), lambda p, ch, hf: (0, 0)) for _ in range(count)]
            + [ANY] * (len(extra) + len(ready)),
            out_specs=(
                pl.BlockSpec((rows, width), lambda p, ch, hf: (ch[p + first], 0)),
                pl.BlockSpec((8, HS), lambda p, ch, hf: (0, 0)),
            ),
        ),
        out_shape=(
            jax.ShapeDtypeStruct((2 * count * rows, width), pieces[0].dtype), jax.ShapeDtypeStruct((8, HS), F32),
        ),
        input_output_aliases={} if rest is None else {2 + count: 0},
        compiler_params=pltpu.CompilerParams(vmem_limit_bytes=32 * 1024 * 1024),
        cost_estimate=COST,
        name="place_rows",
    )(chunk_of, half_of, *pieces, *extra, *ready)


BIG = pltpu.CompilerParams(vmem_limit_bytes=32 * 1024 * 1024)
FULL = pltpu.CompilerParams(vmem_limit_bytes=60 * 1024 * 1024)


def swiglu_kernel(rows, *refs):
    acts, (wg, wgx, wu, wux, dh, d_gate, out, act_near, act_far) = refs[:rows], refs[rows:]
    half = wg.shape[0]
    near = jnp.concatenate([wg[...], wu[...]], 1)
    far = jnp.concatenate([wgx[...], wux[...]], 1)
    cut = wg.shape[1]
    size = acts[0].shape[0]

    @pl.when(pl.program_id(0) == 0)
    def _():
        for k in range(rows):
            act_near[k * size:(k + 1) * size] = acts[k][:, :half]
            act_far[k * size:(k + 1) * size] = acts[k][:, half:]

    for k in range(rows):
        both = dot1(acts[k][:, :half], near) + dot1(acts[k][:, half:], far)
        gate, up, dhk = both[:, :cut], both[:, cut:], dh[k * size:(k + 1) * size].astype(F32)
        s = 1.0 / (1.0 + jnp.exp(-gate))
        gs = gate * s
        d_gate[k * size:(k + 1) * size] = (dhk * up * (s + gs * (1.0 - s))).astype(BF16)
        for i, v in enumerate((gs * up, dhk * gs)):
            out[(i * rows + k) * size:(i * rows + k + 1) * size] = v.astype(BF16)


def swiglu(acts, w_gate, w_gate_x, w_up, w_up_x, d_hidden):
    rows = len(acts)
    size, width = acts[0].shape
    half, feed = w_gate.shape
    tile = 128
    tokens = rows * size
    weight = pl.BlockSpec((half, tile), lambda n: (0, n))
    return pl.pallas_call(
        functools.partial(swiglu_kernel, rows),
        grid=(feed // tile,),
        in_specs=[pl.BlockSpec((size, width), lambda n: (0, 0))] * rows + [weight] * 4
        + [pl.BlockSpec((tokens, tile), lambda n: (0, n))],
        out_specs=(pl.BlockSpec((tokens, tile), lambda n: (0, n)), pl.BlockSpec((2 * tokens, tile), lambda n: (0, n)))
        + (pl.BlockSpec((tokens, half), lambda n: (0, 0)),) * 2,
        out_shape=(jax.ShapeDtypeStruct((tokens, feed), BF16), jax.ShapeDtypeStruct((2 * tokens, feed), BF16))
        + (jax.ShapeDtypeStruct((tokens, half), BF16), jax.ShapeDtypeStruct((tokens, half), BF16)),
        compiler_params=BIG,
        cost_estimate=COST,
        name="swiglu",
    )(*acts, w_gate, w_gate_x, w_up, w_up_x, d_hidden)


def back_kernel(count, parts, *refs):
    lefts, near, far = refs[:count], refs[count:2 * count], refs[2 * count:3 * count]
    outs = refs[3 * count:]

    def store(weights):
        both = sum(dot1(left[...], w[...], NT) for left, w in zip(lefts, weights))
        size = both.shape[0] // parts
        for k in range(parts):
            outs[k][...] = both[k * size:(k + 1) * size].astype(outs[k].dtype)

    steps = pl.num_programs(0) // 2
    pl.when(pl.program_id(0) < steps)(lambda: store(near))
    pl.when(pl.program_id(0) >= steps)(lambda: store(far))


def back(lefts, near, far, parts, tokens, ready=(), cost=COST):
    count = len(lefts)
    half = near[0].shape[0]
    tile = 512
    steps = half // tile
    size = tokens // parts
    return pl.pallas_call(
        after(functools.partial(back_kernel, count, parts), 3 * count, len(ready)),
        grid=(2 * steps,),
        in_specs=[pl.BlockSpec((tokens, v.shape[1]), lambda n, i=i: (i, 0)) for v, i in lefts]
        + [pl.BlockSpec((tile, w.shape[1]), lambda n: (jnp.minimum(n, steps - 1), 0)) for w in near]
        + [pl.BlockSpec((tile, w.shape[1]), lambda n: (jnp.maximum(n - steps, 0), 0)) for w in far] + [ANY] * len(ready),
        out_specs=tuple(pl.BlockSpec((size, tile), lambda n: (0, n)) for _ in range(parts)),
        out_shape=tuple(jax.ShapeDtypeStruct((size, 2 * half), F32) if k == 0 else jax.ShapeDtypeStruct((size, 2 * half), BF16) for k in range(parts)),
        compiler_params=BIG,
        cost_estimate=cost,
        name="back_product",
    )(*[v for v, _ in lefts], *near, *far, *ready)


def grad_kernel(pairs, bit, *refs):
    lefts, rights = refs[:len(pairs)], refs[len(pairs):-2]
    send, keep = refs[-2:]
    out = jnp.concatenate([
        sum(lax.dot_general(lefts[i][...], rights[j][...], TN, preferred_element_type=F32) for i, j in group)
        for group in zip(*[[(i, j) for j in js] for i, js in enumerate(pairs)])
    ], 1).astype(BF16)
    steps = pl.num_programs(0) // 2

    @pl.when(pl.program_id(0) < steps)
    def _():
        send[0] = out

    @pl.when(pl.program_id(0) >= steps)
    def _():
        keep[0] = out


def weight_grad(bit, lefts, rights, pairs, tokens, columns, shards, ready=(), params=BIG):
    rows = columns // shards
    wide = sum(rights[j][0].shape[1] for j in pairs[0])
    half = shards // 2

    def shard(n, b):
        return (n % half) * 2 + jnp.where(n < half, 1 - b[0], b[0])

    shape = jax.ShapeDtypeStruct((half, rows, wide), BF16)
    return pl.pallas_call(
        after(functools.partial(grad_kernel, pairs), 1 + len(lefts) + len(rights), len(ready)),
        grid_spec=pltpu.PrefetchScalarGridSpec(
            num_scalar_prefetch=1,
            grid=(shards,),
            in_specs=[pl.BlockSpec((tokens, rows), lambda n, b, i=i: (i, shard(n, b))) for _, i in lefts]
            + [pl.BlockSpec((tokens, v.shape[1]), lambda n, b, i=i: (i, 0)) for v, i in rights] + [ANY] * len(ready),
            out_specs=(
                pl.BlockSpec((1, rows, wide), lambda n, b: (jnp.minimum(n, half - 1), 0, 0)),
                pl.BlockSpec((1, rows, wide), lambda n, b: (jnp.maximum(n - half, 0), 0, 0)),
            ),
        ),
        out_shape=(jax.ShapeDtypeStruct(shape.shape, BF16), shape),
        compiler_params=params,
        cost_estimate=COST,
        name="weight_grad",
    )(bit, *[v for v, _ in lefts], *[v for v, _ in rights], *ready)


def out_kernel(col, own, other, near, far, *outs):
    first, width = col[0], own.shape[1]
    left = jnp.concatenate([own[...], other[...]], 1)
    half = near.shape[1]
    for h, w in enumerate((near, far)):
        right = jnp.concatenate([w[pl.ds(pl.multiple_of(i * width, width), width)] for i in (first, 1 - first)], 0)
        both = dot1(left, right)
        size = outs[0].shape[0]
        for k, out in enumerate(outs):
            out[:, h * half:(h + 1) * half] = both[k * size:(k + 1) * size].astype(out.dtype)


def out_product(col, heads, other, w_out, w_out_x, parts, ready=()):
    tokens, width = other.shape[0] // 2, other.shape[1]
    half = w_out.shape[1]
    size = tokens // parts
    full = lambda v: pl.BlockSpec(v.shape, lambda n, c: (0, 0))
    return pl.pallas_call(
        after(out_kernel, 5, len(ready)),
        grid_spec=pltpu.PrefetchScalarGridSpec(
            num_scalar_prefetch=1,
            grid=(1,),
            in_specs=[
                pl.BlockSpec((tokens, width), lambda n, c: (0, 0)), pl.BlockSpec((tokens, width), lambda n, c: (1, 0)),
                full(w_out), full(w_out_x),
            ] + [ANY] * len(ready),
            out_specs=tuple(pl.BlockSpec((size, 2 * half), lambda n, c: (0, 0)) for _ in range(parts)),
        ),
        out_shape=tuple(jax.ShapeDtypeStruct((size, 2 * half), F32) if k == 0 else jax.ShapeDtypeStruct((size, 2 * half), BF16) for k in range(parts)),
        compiler_params=BIG,
        cost_estimate=COST,
        name="out_product",
    )(col, heads, other, w_out, w_out_x, *ready)


def head_grad_kernel(parts, col, *refs):
    grads, (near, far, own, other, near_out, far_out) = refs[:parts], refs[parts:]
    width, half = own.shape[1], near.shape[1]
    size = grads[0].shape[0]
    for k in range(parts):
        near_out[k * size:(k + 1) * size] = grads[k][:, :half]
        far_out[k * size:(k + 1) * size] = grads[k][:, half:]
    for i, out in ((col[0], own), (1 - col[0], other)):
        rows = pl.ds(pl.multiple_of(i * width, width), width)
        right = jnp.concatenate([near[rows], far[rows]], 1)
        for k in range(parts):
            out[k * size:(k + 1) * size] = dot1(grads[k][...], right, NT).astype(BF16)


def head_grad(col, grads, w_out, w_out_x, width, ready=()):
    parts, size = len(grads), grads[0].shape[0]
    shape = jax.ShapeDtypeStruct((parts * size, width), BF16)
    shape_two = jax.ShapeDtypeStruct((parts * size, w_out.shape[1]), BF16)
    return pl.pallas_call(
        after(functools.partial(head_grad_kernel, parts), parts + 3, len(ready)),
        in_specs=[SMEM] + vm(parts + 2) + [ANY] * len(ready),
        out_specs=tuple(vm(4)),
        out_shape=(shape, jax.ShapeDtypeStruct(shape.shape, BF16), shape_two, jax.ShapeDtypeStruct(shape_two.shape, BF16)),
        compiler_params=BIG,
        cost_estimate=COST,
        name="head_grad",
    )(col, *grads, w_out, w_out_x, *ready)


def middle_kernel(count, chunk_of, half_of, *refs):
    terms, (a, b, gain, middle, act, own) = refs[:count], refs[count:]
    own[...] = jnp.concatenate([a[...], b[...]], 1)
    total = own[...].astype(F32)
    for term in terms:
        total = total + term[...].astype(F32)
    middle[...] = total
    act[...] = (total * lax.rsqrt(jnp.mean(total * total, axis=1, keepdims=True) + EPSILON) * gain[...]).astype(BF16)


def middle_rows(chunk_of, half_of, terms, x, gain, ready=()):
    count = len(terms)
    rows, width = terms[0].shape
    steps, rows = 4, rows // 4
    whole = pl.BlockSpec((rows, width), lambda n, ch, hf: (n, 0))
    return pl.pallas_call(
        after(functools.partial(middle_kernel, count), count + 5, len(ready)),
        grid_spec=pltpu.PrefetchScalarGridSpec(
            num_scalar_prefetch=2,
            grid=(steps,),
            in_specs=[whole] * count + [
                pl.BlockSpec((rows, width // 2), lambda n, ch, hf: (ch[0] * steps + n, hf[0])),
                pl.BlockSpec((rows, width // 2), lambda n, ch, hf: (ch[0] * steps + n, hf[1])),
                pl.BlockSpec((1, width), lambda n, ch, hf: (0, 0)),
            ] + [ANY] * len(ready),
            out_specs=(whole, whole, whole),
        ),
        out_shape=(
            jax.ShapeDtypeStruct((steps * rows, width), F32), jax.ShapeDtypeStruct((steps * rows, width), BF16),
            jax.ShapeDtypeStruct((steps * rows, width), BF16),
        ),
        compiler_params=BIG,
        cost_estimate=COST,
        name="middle_rows",
    )(chunk_of, half_of, *terms, x, x, gain, *ready)


def norm_back_kernel(count, *refs):
    terms, (values, gain, upstream, total, low, part) = refs[:count], refs[count:]
    grads = terms[0][...]
    for term in terms[1:]:
        grads = grads + term[...].astype(F32)
    v = values[...].astype(F32)
    r = lax.rsqrt(jnp.mean(v * v, axis=1, keepdims=True) + EPSILON)
    normal = v * r
    scaled = gain[...] * grads
    out = upstream[...].astype(F32) + r * (scaled - normal * jnp.mean(normal * scaled, axis=1, keepdims=True))
    total[...] = out
    low[...] = out.astype(BF16)

    @pl.when(pl.program_id(0) == 0)
    def _():
        part[...] = jnp.zeros_like(part)

    part[...] += jnp.sum(grads * normal, axis=0, keepdims=True)


def norm_back(terms, values, gain, upstream, ready=(), cost=COST):
    count = len(terms)
    rows, width = values.shape
    steps = 4
    whole = pl.BlockSpec((rows // steps, width), lambda n: (n, 0))
    row = pl.BlockSpec((1, width), lambda n: (0, 0))
    return pl.pallas_call(
        after(functools.partial(norm_back_kernel, count), count + 3, len(ready)),
        grid=(steps,),
        in_specs=[whole] * (count + 1) + [row, whole] + [ANY] * len(ready),
        out_specs=(whole, whole, row),
        out_shape=(
            jax.ShapeDtypeStruct((rows, width), F32), jax.ShapeDtypeStruct((rows, width), BF16),
            jax.ShapeDtypeStruct((1, width), F32),
        ),
        compiler_params=BIG,
        cost_estimate=cost,
        name="norm_back",
    )(*terms, values, gain, upstream, *ready)


def split_rows(bit, value, send, keep):
    rows = send.shape[1]
    for j in range(2 * send.shape[0]):
        part = value[j * rows:(j + 1) * rows].astype(BF16)
        for to, same in ((send, False), (keep, True)):

            @pl.when((bit == j % 2) == same)
            def _(to=to, j=j, part=part):
                to[j // 2] = part


def down_kernel(bit, hidden, hidden_x, cot, cot_x, send, keep):
    split_rows(bit[0], dot1(hidden[...], cot[...], TN) + dot1(hidden_x[...], cot_x[...], TN), send, keep)


def down_weight_grad(bit, hidden, hidden_x, cot, half, shards, ready=()):
    tokens, feed = hidden.shape[0] // 2, hidden.shape[1]
    tile = 512
    shape = jax.ShapeDtypeStruct((shards // 2, feed // shards, half), BF16)
    out = pl.BlockSpec((shards // 2, feed // shards, tile), lambda n, b: (0, 0, n))
    return pl.pallas_call(
        after(down_kernel, 5, len(ready)),
        grid_spec=pltpu.PrefetchScalarGridSpec(
            num_scalar_prefetch=1,
            grid=(half // tile,),
            in_specs=[
                pl.BlockSpec((tokens, feed), lambda n, b: (0, 0)),
                pl.BlockSpec((tokens, feed), lambda n, b: (0, 0)),
                pl.BlockSpec((tokens, tile), lambda n, b: (0, n)),
                pl.BlockSpec((tokens, tile), lambda n, b: (1, n)),
            ] + [ANY] * len(ready),
            out_specs=(out, out),
        ),
        out_shape=(jax.ShapeDtypeStruct(shape.shape, BF16), shape),
        compiler_params=BIG,
        cost_estimate=COST,
        name="down_weight_grad",
    )(bit, hidden, hidden_x, cot, cot, *ready)


def blocks_of(v):
    return jnp.concatenate([v[:, j:j + HS] for j in range(0, v.shape[1], HS)], 0)


def other_grad_kernel(flip, bit, act, act_far, dz, dz_far, heads, other, grads, grads_x, send, keep, rows_out):
    steps = pl.num_programs(0)
    tokens = grads.shape[0]

    @pl.when(pl.program_id(0) == 0)
    def _():
        g, gx = grads[...], grads_x[...]
        own = dot1(heads[:tokens], g, TN) + dot1(heads[tokens:], gx, TN)
        away = dot1(other[tokens:], g, TN) + dot1(other[:tokens], gx, TN)
        rows_out[...] = jnp.concatenate([own, away], 0).astype(BF16)

    n = pl.program_id(0)
    half = steps // 2
    shard = (n % half) * 2 + jnp.where(n < half, 1 - bit[0], bit[0])
    size = rows_out.shape[0] // steps
    place = (shard + flip[0] * half) % steps
    part = rows_out[pl.ds(pl.multiple_of(place * size, size), size)]
    value = (dot1(act[...], dz[...], TN) + dot1(act_far[...], dz_far[...], TN)).astype(BF16)
    value = jnp.concatenate([blocks_of(value), blocks_of(part)], 0)
    pl.when(n < half)(lambda: send.__setitem__(0, value))
    pl.when(n >= half)(lambda: keep.__setitem__(0, value))


def other_grads(flip, bit, act, dz, dz_far, heads, other, grads, grads_x, columns, shards, ready=()):
    tokens, wide = dz.shape
    rows, half = columns // shards, shards // 2
    out_rows, out_wide = 2 * heads.shape[1], grads.shape[1]
    deep = rows * (wide // HS) + out_rows // shards * (out_wide // HS)

    def shard(n, b):
        return (n % half) * 2 + jnp.where(n < half, 1 - b[0], b[0])

    whole = lambda v: pl.BlockSpec(v.shape, lambda n, f, b: (0, 0))
    shape = jax.ShapeDtypeStruct((half, deep, HS), BF16)
    return pl.pallas_call(
        after(other_grad_kernel, 10, len(ready)),
        grid_spec=pltpu.PrefetchScalarGridSpec(
            num_scalar_prefetch=2,
            grid=(shards,),
            in_specs=[pl.BlockSpec((tokens, rows), lambda n, f, b, i=i: (i, shard(n, b))) for i in range(2)]
            + [whole(v) for v in (dz, dz_far, heads, other, grads, grads_x)] + [ANY] * len(ready),
            out_specs=(
                pl.BlockSpec((1, deep, HS), lambda n, f, b: (jnp.minimum(n, half - 1), 0, 0)),
                pl.BlockSpec((1, deep, HS), lambda n, f, b: (jnp.maximum(n - half, 0), 0, 0)),
            ),
            scratch_shapes=[pltpu.VMEM((out_rows, out_wide), BF16)],
        ),
        out_shape=(jax.ShapeDtypeStruct(shape.shape, BF16), shape),
        compiler_params=BIG,
        cost_estimate=COST,
        name="other_grads",
    )(flip, bit, act, act, dz, dz_far, heads, other, grads, grads_x, *ready)


def feed_kernel(parts, hidden, near, far, keep, send):
    size = hidden.shape[0] // parts

    def store(w):
        both = dot1(hidden[...], w[...])
        for k in range(0, parts, 2):
            keep[k // 2 * size:(k // 2 + 1) * size] = both[k * size:(k + 1) * size]
            send[k // 2 * size:(k // 2 + 1) * size] = both[(k + 1) * size:(k + 2) * size].astype(BF16)

    pl.when(pl.program_id(0) == 0)(lambda: store(near))
    pl.when(pl.program_id(0) == 1)(lambda: store(far))


def feed_product(hidden, near, far, parts, ready=()):
    tokens, half = hidden.shape[0] // 2, near.shape[1]
    whole = lambda v: pl.BlockSpec(v.shape, lambda n: (0, 0))
    return pl.pallas_call(
        after(functools.partial(feed_kernel, parts), 3, len(ready)),
        grid=(2,),
        in_specs=[pl.BlockSpec((tokens, hidden.shape[1]), lambda n: (0, 0)), whole(near), whole(far)] + [ANY] * len(ready),
        out_specs=(pl.BlockSpec((tokens // 2, half), lambda n: (0, n)),) * 2,
        out_shape=(jax.ShapeDtypeStruct((tokens // 2, 2 * half), F32), jax.ShapeDtypeStruct((tokens // 2, 2 * half), BF16)),
        compiler_params=BIG,
        cost_estimate=COST,
        name="feed_product",
    )(hidden, near, far, *ready)


def pair_kernel(kept, got, keep, send):
    size = keep.shape[0]
    keep[...] = kept[:size] + got[:size].astype(F32)
    send[...] = (kept[size:] + got[size:].astype(F32)).astype(BF16)


def pair_rows(kept, got, ready=()):
    rows, width = kept.shape
    return pl.pallas_call(
        after(pair_kernel, 2, len(ready)),
        in_specs=vm(2) + [ANY] * len(ready),
        out_specs=tuple(vm(2)),
        out_shape=(jax.ShapeDtypeStruct((rows // 2, width), F32), jax.ShapeDtypeStruct((rows // 2, width), BF16)),
        compiler_params=BIG,
        cost_estimate=COST,
        name="pair_rows",
    )(kept, got, *ready)


def split_row(v):
    hi = v.astype(BF16).astype(F32)
    return jnp.concatenate([hi, v - hi], 0)


def last_norm_kernel(count, *refs):
    terms, (values, gain, upstream, feed_part, head_part, out) = refs[:count], refs[count:]
    grads = terms[0][...]
    for term in terms[1:]:
        grads = grads + term[...].astype(F32)
    v = values[...].astype(F32)
    r = lax.rsqrt(jnp.mean(v * v, axis=1, keepdims=True) + EPSILON)
    normal = v * r
    scaled = gain[...] * grads
    rows, width = v.shape
    out[:rows] = (upstream[...] + r * (scaled - normal * jnp.mean(normal * scaled, axis=1, keepdims=True))).astype(BF16)
    part = jnp.sum(grads * normal, axis=0, keepdims=True)
    head = jnp.concatenate([head_part[...], jnp.zeros((1, width - HS), F32)], 1)
    extra = [split_row(part), split_row(feed_part[...]), split_row(head), jnp.zeros((10, width), F32)]
    out[rows:] = jnp.concatenate(extra, 0).astype(BF16)


def last_norm_back(terms, values, gain, upstream, feed_part, head_part, ready=()):
    count = len(terms)
    rows, width = values.shape
    return pl.pallas_call(
        after(functools.partial(last_norm_kernel, count), count + 5, len(ready)),
        in_specs=vm(count + 5) + [ANY] * len(ready),
        out_specs=vm(1)[0],
        out_shape=jax.ShapeDtypeStruct((rows + 16, width), BF16),
        compiler_params=BIG,
        cost_estimate=spent(4),
        name="last_norm_back",
    )(*terms, values, gain, upstream, feed_part, head_part, *ready)


def total_kernel(half_of, *refs):
    pieces, out = refs[:-1], refs[-1]
    half = out.shape[1] // 2
    count = len(pieces) // 2
    for h in range(2):
        own = sum(ref[...].astype(F32)[:, h * half:(h + 1) * half] for ref in pieces[:count])
        oth = sum(ref[...].astype(F32)[:, (1 - h) * half:(2 - h) * half] for ref in pieces[count:])
        total = own + oth
        out[:, pl.ds(pl.multiple_of(half_of[h] * half, half), half)] = jnp.concatenate(
            [total[n:n + 1] + total[n + 1:n + 2] for n in (0, 2)] + [jnp.zeros((6, half), F32)], 0)
    heads = sum(ref[...].astype(F32)[4:6, :HS] for ref in pieces)
    out[2:3, :HS] = heads[0:1] + heads[1:2]


def totals(half_of, own, partner, ready=()):
    rows, width = own[0].shape
    at = (rows - 16) // 16
    return pl.pallas_call(
        after(total_kernel, 1 + 2 * len(own), len(ready)),
        grid_spec=pltpu.PrefetchScalarGridSpec(
            num_scalar_prefetch=1,
            grid=(1,),
            in_specs=[pl.BlockSpec((16, width), lambda n, hf: (at, 0))] * (2 * len(own)) + [ANY] * len(ready),
            out_specs=pl.BlockSpec((8, width), lambda n, hf: (0, 0)),
        ),
        out_shape=jax.ShapeDtypeStruct((8, width), F32),
        compiler_params=BIG,
        cost_estimate=COST,
        name="totals",
    )(half_of, *own, *partner, *ready)


def sum_kernel(*refs):
    total = refs[0][...]
    for ref in refs[1:-1]:
        total = total + ref[...].astype(F32)
    refs[-1][...] = total.astype(BF16)


def sum_rows(terms, ready=()):
    return pl.pallas_call(
        after(sum_kernel, len(terms), len(ready)),
        in_specs=vm(len(terms)) + [ANY] * len(ready),
        out_specs=vm(1)[0],
        out_shape=jax.ShapeDtypeStruct(terms[0].shape, BF16),
        compiler_params=BIG,
        cost_estimate=COST,
        name="sum_rows",
    )(*terms, *ready)


def halve_kernel(bit, kept, got, send, keep):
    for out, i in ((send, 1 - bit[0]), (keep, bit[0])):
        out[...] = (kept[pl.ds(i, 1)].astype(F32) + got[pl.ds(i, 1)].astype(F32)).astype(BF16)


def halve(bit, kept, got, ready=()):
    shards, rows, columns = kept.shape
    pair = pl.BlockSpec((2, rows, columns), lambda n, b: (n, 0, 0))
    one = pl.BlockSpec((1, rows, columns), lambda n, b: (n, 0, 0))
    shape = jax.ShapeDtypeStruct((shards // 2, rows, columns), BF16)
    return pl.pallas_call(
        after(halve_kernel, 3, len(ready)),
        grid_spec=pltpu.PrefetchScalarGridSpec(
            num_scalar_prefetch=1, grid=(shards // 2,), in_specs=[pair, pair] + [ANY] * len(ready), out_specs=(one, one),
        ),
        out_shape=(jax.ShapeDtypeStruct(shape.shape, BF16), shape),
        compiler_params=BIG,
        cost_estimate=COST,
        name="halve",
    )(bit, kept, got, *ready)


def add_kernel(a, b, out):
    out[...] = a[...] + b[...]


def add(a, b, ready):
    return pl.pallas_call(
        after(add_kernel, 2, len(ready)),
        in_specs=vm(2) + [ANY] * len(ready),
        out_specs=vm(1)[0],
        out_shape=jax.ShapeDtypeStruct(a.shape, a.dtype),
        cost_estimate=COST,
        name="add",
    )(a, b, *ready)


def hold(v, ready):
    def kernel(v_ref, *refs):
        pass

    return pl.pallas_call(
        kernel,
        in_specs=[ANY] + [ANY] * len(ready),
        out_specs=ANY,
        out_shape=jax.ShapeDtypeStruct(v.shape, v.dtype),
        input_output_aliases={0: 0},
        cost_estimate=COST,
        name="hold",
    )(v, *ready)


def finish_kernel(kept, got, out, token):
    out[...] = kept[0].astype(F32) + got[0].astype(F32)
    token[...] = jnp.zeros_like(token)


def finish(kept, got, ready=()):
    _, rows, columns = kept.shape
    steps = 2 if rows % 32 == 0 else 1
    part = pl.BlockSpec((1, rows // steps, columns), lambda n: (0, n, 0))
    return pl.pallas_call(
        after(finish_kernel, 2, len(ready)),
        grid=(steps,),
        in_specs=[part, part] + [ANY] * len(ready),
        out_specs=(pl.BlockSpec((rows // steps, columns), lambda n: (n, 0)), pl.BlockSpec((8, HS), lambda n: (0, 0))),
        out_shape=(jax.ShapeDtypeStruct((rows, columns), F32), jax.ShapeDtypeStruct((8, HS), F32)),
        compiler_params=BIG,
        cost_estimate=COST,
        name="finish",
    )(kept, got, *ready)


def finish_small_kernel(gains, share, group, small, got, mixer, feed, head, *taps):
    i = group[0]
    total = small[...] + got[...]
    per, steps = gains // HS, mixer.shape[0]
    mixer[...] = sum(jnp.where(i == n, total[n * steps:(n + 1) * steps], 0.0) for n in range(per // steps))
    feed[...] = sum(jnp.where(i == n, total[per + n * steps:per + (n + 1) * steps], 0.0) for n in range(per // steps))
    head[...] = total[2 * per:2 * per + 1]
    tiles = share * (per // steps) // HS
    for which, out in enumerate(taps):
        rows = []
        for t in range(out.shape[0]):
            at = 3 * per + (t * len(taps) + which) * tiles
            rows.append(sum(
                jnp.where(i == n, total[at + n * share // HS:at + n * share // HS + 1, n * share % HS:n * share % HS + share], 0.0)
                for n in range(per // steps)
            ))
        out[...] = jnp.concatenate(rows, 0)


def finish_small(group, small, got, gains, tap_shape, shares, ready=()):
    taps, wide = tap_shape
    share = wide // 3 // shares
    shapes = [(gains // HS // shares, HS)] * 2 + [(1, HS)] + [(taps, share)] * 3
    return pl.pallas_call(
        after(functools.partial(finish_small_kernel, gains, share), 3, len(ready)),
        in_specs=[SMEM] + vm(2) + [ANY] * len(ready),
        out_specs=tuple(vm(6)),
        out_shape=tuple(jax.ShapeDtypeStruct(shape, F32) for shape in shapes),
        compiler_params=BIG,
        cost_estimate=COST,
        name="finish_small",
    )(group, small, got, *ready)


def finish_pair_kernel(col, own_kept, own_got, oth_kept, oth_got, *outs):
    own = own_kept[0].astype(F32) + own_got[0].astype(F32)
    oth = oth_kept[0].astype(F32) + oth_got[0].astype(F32)
    rows, wide = own.shape
    width = outs[0].shape[1] // 2
    blocks = wide // HS
    rest = oth[blocks * rows:]
    oth = jnp.concatenate([oth[j * rows:(j + 1) * rows] for j in range(blocks)], 1)
    for n, out in enumerate(outs[:3]):
        for i, v in ((col[0], own), (1 - col[0], oth)):
            out[:, pl.ds(pl.multiple_of(i * width, width), width)] = v[:, n * width:(n + 1) * width]
    outs[3][...] = own[:, 3 * width:] + oth[:, 3 * width:]
    size = outs[4].shape[0]
    outs[4][...] = jnp.concatenate([rest[j * size:(j + 1) * size] for j in range(rest.shape[0] // size)], 1)


def finish_pair(col, own_kept, own_got, oth_kept, oth_got, width, out_rows, ready=()):
    _, rows, columns = own_kept.shape
    blocks = (oth_kept.shape[1] - rows * (columns // HS)) // out_rows
    shapes = [(rows, 2 * width)] * 3 + [(rows, columns - 3 * width), (out_rows, blocks * HS)]
    return pl.pallas_call(
        after(finish_pair_kernel, 5, len(ready)),
        in_specs=[SMEM] + vm(4) + [ANY] * len(ready),
        out_specs=tuple(vm(5)),
        out_shape=tuple(jax.ShapeDtypeStruct(shape, F32) for shape in shapes),
        compiler_params=BIG,
        cost_estimate=COST,
        name="finish_pair",
    )(col, own_kept, own_got, oth_kept, oth_got, *ready)


def mm(left, right, dims=NN):
    return lax.dot_general(left, right, dims, preferred_element_type=F32)


def body(
    inputs, segments, mixer_gain, w_query, w_key, w_value, w_beta, conv_query, conv_key, conv_value,
    head_gain, w_out, feed_gain, w_gate, w_up, w_down, cotangent,
):
    cols, rows, groups = lax.axis_size("col"), lax.axis_size("row"), lax.axis_size("dp")
    c, r, g = lax.axis_index("col"), lax.axis_index("row"), lax.axis_index("dp")
    tokens, width = inputs.shape
    half, mine = width // cols, tokens // cols
    own_width = conv_query.shape[0]
    feed = w_gate.shape[1]

    def swap(v):
        return lax.ppermute(v, "col", [(i, i ^ 1) for i in range(cols)])

    def to_row(v, k):
        return lax.ppermute(v, "row", [(i, i ^ k) for i in range(rows)])

    def row_terms(blocks):
        return [blocks[0]] + [to_row(blocks[k], k) for k in range(rows - 1, 0, -1)]

    def row_gather(own):
        return [own] + [to_row(own, k) for k in range(1, rows)]

    def own_first(v, axis=-1):
        size = v.shape[axis] // 2
        return jnp.concatenate([lax.dynamic_slice_in_dim(v, i * size, size, axis) for i in (c, 1 - c)], axis)

    def halves(v, bit):
        parts = v.reshape(v.shape[0] // 2, 2, *v.shape[1:])
        return [lax.dynamic_index_in_dim(parts, i, 1, keepdims=False) for i in (1 - bit, bit)]

    def traded(v, step):
        return lax.ppermute(v, "dp", [(i, i ^ step) for i in range(groups)])

    def group_steps(pair, got, ready):
        step = 1
        while step * 2 < groups:
            got = got if step == 1 else traded(pair[0], step)
            step *= 2
            pair = halve(((g // step) % 2).astype(jnp.int32)[None], pair[1], got, ready)
        return pair

    def shards_of(v):
        return halves(v.astype(BF16).reshape(groups, -1, v.shape[-1]), g % 2)

    def grads_of(lefts, rights, pairs, columns, ready, params=BIG):
        if columns // groups % 128 == 0:
            return weight_grad(low_bit, lefts, rights, pairs, mine, columns, groups, ready, params)

        def rows_of(v, i):
            return v[i * mine:(i + 1) * mine]

        return shards_of(jnp.concatenate([
            sum(mm(rows_of(*lefts[i])[:, :columns], rows_of(*rights[j]), TN) for i, j in enumerate(js)) for js in zip(*pairs)
        ], 1))

    def all_sum(v):
        v = v + swap(v)
        k = 1
        while k < rows:
            v = v + to_row(v, k)
            k *= 2
        k = 1
        while k < groups:
            v = v + lax.ppermute(v, "dp", [(i, i ^ k) for i in range(groups)])
            k *= 2
        return v

    order = jnp.arange(cols * rows, dtype=jnp.int32)
    chunk_of = ((order % rows) ^ r) * cols + ((order // rows) ^ c)
    place_of = ((order % cols) ^ c) * rows + ((order // cols) ^ r)
    half_of = jnp.stack([c, 1 - c]).astype(jnp.int32)
    place_of = jnp.concatenate([place_of, half_of[:1]])
    low_bit = (g % 2).astype(jnp.int32)[None]
    documents = (segments + (jnp.arange(segments.shape[0], dtype=jnp.int32) * segments.shape[1])[:, None]).reshape(-1)
    doc_col = jnp.pad(documents, (8, 8), constant_values=-1)[:, None]
    doc_row = documents.reshape(-1, CH)
    taps = jnp.concatenate([conv_query.T, conv_key.T, conv_value.T], 1)
    gain_row = head_gain[None]
    gain_one, gain_two = own_first(mixer_gain)[None], own_first(feed_gain)[None]

    w_beta_wide = jnp.pad(w_beta, ((0, 0), (0, HS - w_beta.shape[1])))

    def columns(i):
        parts = [lax.dynamic_slice_in_dim(w, i * own_width, own_width, 1) for w in (w_query, w_key, w_value)]
        return jnp.concatenate(parts + [w_beta_wide], 1)

    w_own, w_oth = columns(c), columns(1 - c)
    w_own_x = swap(w_oth)
    act = ordered(norm_kernel, chunk_of, half_of, inputs, gain_one)
    z = mm(act[:, :half], w_own) + mm(act[:, half:], w_own_x)
    heads, *saved = delta_forward(place_of, z, taps, doc_col, doc_row, gain_row)
    w_out_x, w_gate_x, w_up_x, w_down_x, w_oth_x = swap(w_out), swap(w_gate), swap(w_up), swap(w_down), swap(w_own)
    col = half_of[:1]

    last = groups // 2
    heads_x = swap(heads)
    attended = row_terms(out_product(col, heads, heads_x, w_out, w_out_x, rows, (w_gate_x, w_up_x, w_down_x, w_oth_x)))
    cot = ordered(copy_kernel, chunk_of, half_of, cotangent, ready=attended[:1])
    d_hidden = mm(cot[:mine, :half], w_down, NT) + mm(cot[:mine, half:], w_down_x, NT)
    middle, act_two, x_own = middle_rows(chunk_of, half_of, attended, inputs, gain_two, (d_hidden, cot))

    act_two = row_gather(act_two)
    d_gate, feeds, act_near, act_far = swiglu(act_two, w_gate, w_gate_x, w_up, w_up_x, d_hidden)
    act_x, d_gate_x = swap(act_far), swap(d_gate)
    feeds_x = swap(hold(feeds, (act_x, d_gate_x)))
    act_pair = [(act_near, 0), (act_x, 0)]
    gate_grad = grads_of(act_pair, [(d_gate, 0), (d_gate_x, 0)], [(0,), (1,)], half, (), FULL)
    gate_got = traded(gate_grad[0], 1)
    d_act_two = row_terms(back([(d_gate, 0), (feeds, 1)], [w_gate, w_up], [w_gate_x, w_up_x], rows, mine, gate_grad[:1]))
    up_grad = grads_of(act_pair, [(feeds, 1), (feeds_x, 1)], [(0,), (1,)], half, d_act_two[:1])
    up_got = traded(up_grad[0], 1)
    feed_keep, feed_send = feed_product(feeds, w_down, w_down_x, rows, up_grad[:1])
    gate_grad = group_steps(gate_grad, gate_got, (feed_send,))
    gate_got = traded(gate_grad[0], last)
    d_middle, d_att, feed_part = norm_back(d_act_two, middle, gain_two, cot, gate_grad[:1], cost=spent(4))

    down_grad = down_weight_grad(low_bit, feeds, feeds_x, cot, half, groups, (d_att,))
    down_got = traded(down_grad[0], 1)
    up_grad = group_steps(up_grad, up_got, down_grad[:1])
    up_got = traded(up_grad[0], last)
    d_heads, d_heads_x, d_att_near, d_att_x = head_grad(
        col, row_gather(d_att), w_out, w_out_x, own_width, (up_grad[0], gate_got)
    )
    d_heads_x, d_att_x = swap(d_heads_x), swap(d_att_x)
    feed_got = to_row(feed_send, 1)
    dz, dz_far, d_taps, head_part = delta_backward(
        place_of, d_heads, d_heads_x, z, taps, doc_col, doc_row, gain_row, saved, (d_att_x,)
    )

    feed_keep, feed_send = pair_rows(feed_keep, feed_got, (dz_far, up_got))
    feed_got = to_row(feed_send, 2)
    dz_x, dz_far_x = swap(dz_far), swap(dz)
    act_pair = [(act, 0), (act, 1)]
    grad_own = grads_of(act_pair, [(dz, 0), (dz_far, 0)], [(0,), (1,)], half, (feed_send,))
    own_got = traded(grad_own[0], 1)
    d_act = row_terms(back(
        [(dz, 0), (dz_x, 0)], [w_own, w_oth], [w_own_x, w_oth_x], rows, mine, (grad_own[0], feed_got, dz_far_x), spent(2)
    ))
    down_grad = group_steps(down_grad, down_got, d_act[:1])
    down_got = traded(down_grad[0], last)
    if half // groups % 128 == 0:
        grad_oth = other_grads(
            col, low_bit, act, dz_x, dz_far_x, heads, heads_x, d_att_near, d_att_x, half, groups, down_grad[:1]
        )
    else:
        def shard_blocks(v):
            v = v.reshape(groups, v.shape[0] // groups, v.shape[1] // HS, HS)
            return jnp.swapaxes(v, 1, 2).reshape(groups, -1, HS)

        projected = mm(act[:mine, :half], dz_x, TN) + mm(act[mine:, :half], dz_far_x, TN)
        first = mm(heads[:mine], d_att_near, TN) + mm(heads[mine:], d_att_x, TN)
        second = mm(heads_x[mine:], d_att_near, TN) + mm(heads_x[:mine], d_att_x, TN)
        outs = jnp.where(c == 0, jnp.concatenate([first, second], 0), jnp.concatenate([second, first], 0))
        grad_oth = halves(jnp.concatenate([shard_blocks(projected), shard_blocks(outs)], 1).astype(BF16), g % 2)
    oth_got = traded(grad_oth[0], 1)
    gate_grad, token = finish(gate_grad[1], gate_got, grad_oth[:1])
    up_grad, token = finish(up_grad[1], up_got, (token,))
    grad_own = group_steps(grad_own, own_got, (token,))
    own_got = traded(grad_own[0], last)
    output = sum_rows([middle, feed_keep, feed_got], grad_own[:1])
    input_grad = last_norm_back(d_act, x_own, gain_one, d_middle, feed_part, head_part, (output, down_got))

    input_grad = row_gather(input_grad)
    grad_oth = group_steps(grad_oth, oth_got, (own_got,))
    oth_got = traded(grad_oth[0], last)
    input_grad_x = [swap(v) for v in input_grad]
    placed, token = place(chunk_of, half_of, input_grad, None, (grad_oth[0],))
    small = totals(half_of, input_grad, input_grad_x, (token,))
    output = row_gather(hold(output, (input_grad[1],)))
    input_grad, token = place(chunk_of, half_of, input_grad_x, placed, (small,))
    down_grad, token = finish(down_grad[1], down_got, (token,))
    small = hold(jnp.concatenate([small[:3].reshape(-1), d_taps.reshape(-1)]).reshape(-1, HS), (token,))
    k = 1
    while 2 * k < groups:
        small = add(small, traded(small, k), ())
        k *= 2
    small_got = traded(small, last)
    output[0] = hold(output[0], (token,))
    output_x = [swap(v) for v in output]
    placed, token = place(chunk_of, half_of, output, None, (token,))
    output, token = place(chunk_of, half_of, output_x, placed, (token,))
    *projections, beta_grad, out_grad = finish_pair(
        col, grad_own[1], own_got, grad_oth[1], oth_got, own_width, w_out.shape[0] // groups, (token,)
    )
    mixer_gain_grad, feed_gain_grad, head_gain_grad, *conv_grads = finish_small(
        g.astype(jnp.int32)[None], small, small_got, width, d_taps.shape, groups, (beta_grad,)
    )
    beta_grad = beta_grad[:, :w_beta.shape[1]]
    mixer_gain_grad, feed_gain_grad, head_gain_grad = (
        v.reshape(-1) for v in (mixer_gain_grad, feed_gain_grad, head_gain_grad)
    )
    conv_grads = [v.T for v in conv_grads]
    return (
        output, input_grad, mixer_gain_grad, *projections, beta_grad, *conv_grads,
        head_gain_grad, out_grad, feed_gain_grad, gate_grad, up_grad, down_grad,
    )


def solution(mesh):
    weight, swapped = P("col", "row"), P("row", "col")
    taps = P(("row", "col"), None)
    grad, grad_taps = P(("col", "dp"), "row"), P(("row", "col", "dp"), None)
    grad_swapped = P(("row", "dp"), "col")
    tokens = P("dp", None)
    return jax.shard_map(
        body,
        mesh=mesh,
        in_specs=(
            tokens, tokens, P(), weight, weight, weight, weight, taps, taps, taps, P(), swapped, P(), weight, weight,
            swapped, tokens,
        ),
        out_specs=(
            tokens, tokens, P("dp"), grad, grad, grad, grad, grad_taps, grad_taps, grad_taps, P(), grad_swapped, P("dp"),
            grad, grad, grad_swapped,
        ),
        check_vma=False,
    )
```
